128 devices in a mesh: dp: 4 (over z), segment: 4 (over x), space: 8 (over y, core).
Axes of the slice: x: 4, y: 4, z: 4, core: 2. Of those that a mesh axis runs over, the one named last changes fastest.
Arguments:
- terrain_in: bfloat16 [8, 2, 64, 256], P('dp', None, 'space'), may hold values from -6 to 6
- meso_in: bfloat16 [8, 4, 32, 32, 128], P('dp', None, None, 'space'), may hold values from -6 to 6
- wind_cot: bfloat16 [8, 3, 32, 128], P('dp', None, 'space'), may hold values from -6 to 6
- patch_weight: bfloat16 [256, 8], replicated, may hold values from -2 to 2
- terrain_weight: bfloat16 [256, 2304], replicated, may hold values from -0.125 to 0.125
- lift_weight: bfloat16 [384, 128], replicated, may hold values from -0.5 to 0.5
- meso_weight: bfloat16 [384, 3456], replicated, may hold values from -0.109375 to 0.109375
- merging_weight: bfloat16 [256, 5760], replicated, may hold values from -0.078125 to 0.078125
- decoder_weight: bfloat16 [256, 2304], replicated, may hold values from -0.125 to 0.125
- head_weight: bfloat16 [3, 256], replicated, may hold values from -0.375 to 0.375
Outputs:
- patch_grad: float32 [256, 8], replicated
- terrain_grad: float32 [256, 2304], replicated
- lift_grad: float32 [384, 128], replicated
- meso_grad: float32 [384, 3456], replicated
- merging_grad: float32 [256, 5760], replicated
- decoder_grad: float32 [256, 2304], replicated
- head_grad: float32 [3, 256], replicated
The draws below stay inside these ranges and needn't reach their ends.
All inputs are finite; a program needn't handle non-finite values.
Results may differ from the reference program's by a relative error of at most 0.017.
Values may be sent and summed in bfloat16 or wider, within the bound.
No kernel may reach another device: no remote copies, remote signals or barrier semaphores. Data moves between devices by JAX's collectives and lax.ppermute only.
A program may use at most 192 MiB of HBM per device.

```python
import math
import jax
import jax.numpy as jnp
from jax import lax

C_TERR = 256
C_MESO = 384
C_MIX = 256
FIELDS = 2
VARS = 4
LEVELS = 32
WINDS = 3
COLS = 128
NROWS = 32
BATCH = 8


def levels(own_key, dims, cuts, least, top_value):
    gain, own = 1.0, jax.random.fold_in(own_key, 6)
    for axis_at, shards_of in cuts:
        draws = jnp.exp(jax.random.uniform(jax.random.fold_in(own, axis_at), (shards_of,), jnp.float32, least / len(cuts), top_value / len(cuts)))
        gain = gain * jnp.repeat(draws, dims[axis_at] // shards_of).reshape([-1 if axis == axis_at else 1 for axis in range(len(dims))])
    return gain


def scatter_about(key, dims, scale, reach, cuts=(), held_as=jnp.bfloat16):
    values = scale * jax.random.normal(key, dims, jnp.float32)
    if cuts:
        values = values * levels(key, dims, cuts, -0.22, 0.18)
    return jnp.clip(values, -reach, reach).astype(held_as)


def setup_inputs(seed: int = 0) -> dict:
    key_of = jax.random.split(jax.random.key(seed), 11)
    return {
        "terrain_in": scatter_about(key_of[0], (BATCH, FIELDS, 2 * NROWS, 2 * COLS), 1.0, 6.0, ((0, 4), (2, 8))),
        "meso_in": scatter_about(key_of[1], (BATCH, VARS, LEVELS, NROWS, COLS), 1.0, 6.0, ((0, 4), (3, 8))),
        "wind_cot": scatter_about(key_of[2], (BATCH, WINDS, NROWS, COLS), 1.0, 6.0, ((0, 4), (2, 8))),
        "patch_weight": scatter_about(key_of[3], (C_TERR, 4 * FIELDS), (4 * FIELDS) ** -0.5, 2.0),
        "terrain_weight": scatter_about(key_of[4], (C_TERR, 9 * C_TERR), (9 * C_TERR) ** -0.5, 0.125),
        "lift_weight": scatter_about(key_of[5], (C_MESO, VARS * LEVELS), (VARS * LEVELS) ** -0.5, 0.5),
        "meso_weight": scatter_about(key_of[6], (C_MESO, 9 * C_MESO), (9 * C_MESO) ** -0.5, 0.109375),
        "merging_weight": scatter_about(key_of[7], (C_MIX, 9 * (C_TERR + C_MESO)), (9 * (C_TERR + C_MESO)) ** -0.5, 0.078125),
        "decoder_weight": scatter_about(key_of[8], (C_MIX, 9 * C_MIX), (9 * C_MIX) ** -0.5, 0.125),
        "head_weight": scatter_about(key_of[9], (WINDS, C_MIX), C_MIX ** -0.5, 0.375),
    }


def depth_stack(terrain):
    fields, padded_rows, columns = terrain.shape
    split = terrain.reshape(fields, padded_rows // 2, 2, columns // 2, 2)
    return split.transpose(0, 2, 4, 1, 3).reshape(fields * 4, padded_rows // 2 * (columns // 2))

def silu_slope(pre_act):
    sigma = jax.nn.sigmoid(pre_act)
    return sigma * (1.0 + pre_act * (1.0 - sigma))

def conv_forward(weight, source):
    channels, height, breadth = source.shape
    padded = jnp.pad(source, ((0, 0), (1, 1), (1, 1)))
    result = jnp.zeros((weight.shape[0], height * breadth), jnp.float32)
    for tap_index in range(9):
        row_shift = tap_index // 3
        column_shift = tap_index % 3
        window = padded[:, row_shift:row_shift + height, column_shift:column_shift + breadth].reshape(channels, height * breadth)
        result = result + jnp.dot(weight[:, tap_index * channels:(tap_index + 1) * channels], window, preferred_element_type=jnp.float32)
    return result.reshape(weight.shape[0], height, breadth)

def conv_input_grad(weight, back_delta):
    outputs, height, breadth = back_delta.shape
    channels = weight.shape[1] // 9
    padded = jnp.pad(back_delta, ((0, 0), (1, 1), (1, 1)))
    result = jnp.zeros((channels, height * breadth), jnp.float32)
    for tap_index in range(9):
        row_shift = 2 - tap_index // 3
        column_shift = 2 - tap_index % 3
        window = padded[:, row_shift:row_shift + height, column_shift:column_shift + breadth].reshape(outputs, height * breadth)
        result = result + lax.dot_general(weight[:, tap_index * channels:(tap_index + 1) * channels], window, (((0,), (0,)), ((), ())), preferred_element_type=jnp.float32)
    return result.reshape(channels, height, breadth)

def conv_weight_grad(back_delta, source):
    outputs, height, breadth = back_delta.shape
    channels = source.shape[0]
    padded = jnp.pad(source, ((0, 0), (1, 1), (1, 1)))
    delta_flat = back_delta.reshape(outputs, height * breadth)
    pieces = []
    for tap_index in range(9):
        row_shift = tap_index // 3
        column_shift = tap_index % 3
        window = padded[:, row_shift:row_shift + height, column_shift:column_shift + breadth].reshape(channels, height * breadth)
        pieces.append(lax.dot_general(delta_flat, window, (((1,), (1,)), ((), ())), preferred_element_type=jnp.float32))
    return jnp.concatenate(pieces, axis=1)

def reference(terrain_in, meso_in, wind_cot, patch_weight, terrain_weight, lift_weight, meso_weight, merging_weight, decoder_weight, head_weight):
    grad_scale = 1.0 / math.sqrt(BATCH * NROWS * COLS)
    cell_count = NROWS * COLS
    patch_sum = jnp.zeros(patch_weight.shape, jnp.float32)
    terrain_sum = jnp.zeros(terrain_weight.shape, jnp.float32)
    lift_sum = jnp.zeros(lift_weight.shape, jnp.float32)
    meso_sum = jnp.zeros(meso_weight.shape, jnp.float32)
    merging_sum = jnp.zeros(merging_weight.shape, jnp.float32)
    decoder_sum = jnp.zeros(decoder_weight.shape, jnp.float32)
    head_sum = jnp.zeros(head_weight.shape, jnp.float32)
    for sample in range(BATCH):
        terrain_flat = depth_stack(terrain_in[sample])
        terrain_act = jnp.dot(patch_weight, terrain_flat, preferred_element_type=jnp.float32).astype(jnp.bfloat16).reshape(C_TERR, NROWS, COLS)
        terrain_pre = conv_forward(terrain_weight, terrain_act)
        terrain_out = jax.nn.silu(terrain_pre).astype(jnp.bfloat16)
        meso_flat = meso_in[sample].reshape(VARS * LEVELS, cell_count)
        meso_act = jnp.dot(lift_weight, meso_flat, preferred_element_type=jnp.float32).astype(jnp.bfloat16).reshape(C_MESO, NROWS, COLS)
        meso_pre = conv_forward(meso_weight, meso_act)
        meso_out = jax.nn.silu(meso_pre).astype(jnp.bfloat16)
        joined = jnp.concatenate([terrain_out, meso_out], axis=0)
        merging_pre = conv_forward(merging_weight, joined)
        merging_out = jax.nn.silu(merging_pre).astype(jnp.bfloat16)
        decoder_pre = conv_forward(decoder_weight, merging_out)
        decoder_out = jax.nn.silu(decoder_pre).astype(jnp.bfloat16)
        cot_flat = wind_cot[sample].reshape(WINDS, cell_count)
        head_sum = head_sum + grad_scale * lax.dot_general(cot_flat, decoder_out.reshape(C_MIX, cell_count), (((1,), (1,)), ((), ())), preferred_element_type=jnp.float32)
        decoder_back = grad_scale * lax.dot_general(head_weight, cot_flat, (((0,), (0,)), ((), ())), preferred_element_type=jnp.float32)
        decoder_delta = (silu_slope(decoder_pre) * decoder_back.reshape(C_MIX, NROWS, COLS)).astype(jnp.bfloat16)
        decoder_sum = decoder_sum + conv_weight_grad(decoder_delta, merging_out)
        merging_back = conv_input_grad(decoder_weight, decoder_delta).astype(jnp.bfloat16)
        merging_delta = (silu_slope(merging_pre) * merging_back).astype(jnp.bfloat16)
        merging_sum = merging_sum + conv_weight_grad(merging_delta, joined)
        joined_back = conv_input_grad(merging_weight, merging_delta).astype(jnp.bfloat16)
        terrain_delta = (silu_slope(terrain_pre) * joined_back[:C_TERR]).astype(jnp.bfloat16)
        meso_delta = (silu_slope(meso_pre) * joined_back[C_TERR:]).astype(jnp.bfloat16)
        terrain_sum = terrain_sum + conv_weight_grad(terrain_delta, terrain_act)
        terrain_back = conv_input_grad(terrain_weight, terrain_delta).astype(jnp.bfloat16)
        patch_sum = patch_sum + lax.dot_general(terrain_back.reshape(C_TERR, cell_count), terrain_flat, (((1,), (1,)), ((), ())), preferred_element_type=jnp.float32)
        meso_sum = meso_sum + conv_weight_grad(meso_delta, meso_act)
        meso_back = conv_input_grad(meso_weight, meso_delta).astype(jnp.bfloat16)
        lift_sum = lift_sum + lax.dot_general(meso_back.reshape(C_MESO, cell_count), meso_flat, (((1,), (1,)), ((), ())), preferred_element_type=jnp.float32)
    return (patch_sum, terrain_sum, lift_sum, meso_sum, merging_sum, decoder_sum, head_sum)
```

```python
import math

import jax
import jax.numpy as jnp
from jax import lax
from jax.experimental import pallas as pl
from jax.experimental.pallas import tpu as pltpu
from jax.sharding import PartitionSpec as P

BF = jnp.bfloat16
F32 = jnp.float32
TERR, MESO, MIX = 256, 384, 256
JOINT = TERR + MESO
LEV = 128
SLAB = 16
PACK = LEV + SLAB
ROWS, COLS = 4, 128
HALO = 5
CHUNK = 2 * COLS
OQ, MQ = MIX // 4, MESO // 4
WIDE = 1280
PIECES = 32
NT = (((1,), (1,)), ((), ()))


def dot(a, b):
    return jnp.dot(a, b, preferred_element_type=F32)


def dot_nt(a, b):
    return lax.dot_general(a, b, NT, preferred_element_type=F32)


def params(mib):
    return pltpu.CompilerParams(vmem_limit_bytes=mib * 1024 * 1024)


def prep_kernel(mw, lw, tw, pw, gw, dw, wm, wt, gt, dt):
    for tap in range(9):
        wm[:, tap * LEV : (tap + 1) * LEV] = dot(
            mw[:, tap * MESO : (tap + 1) * MESO], lw[...]
        ).astype(BF)
    wt[...] = jnp.concatenate(
        [dot(tw[:, tap * TERR : (tap + 1) * TERR], pw[...]).astype(BF) for tap in range(9)], axis=1
    )
    for tap in range(9):
        gt[:, tap * MIX : (tap + 1) * MIX] = gw[:, tap * JOINT : (tap + 1) * JOINT].T
        dt[:, tap * MIX : (tap + 1) * MIX] = dw[:, tap * MIX : (tap + 1) * MIX].T


def prep(meso_weight, lift_weight, terrain_weight, patch16, merging_weight, decoder_weight):
    return pl.pallas_call(
        prep_kernel,
        out_shape=(
            jax.ShapeDtypeStruct((MESO, 9 * LEV), BF),
            jax.ShapeDtypeStruct((TERR, 9 * SLAB), BF),
            jax.ShapeDtypeStruct((JOINT, 9 * MIX), BF),
            jax.ShapeDtypeStruct((MIX, 9 * MIX), BF),
        ),
        compiler_params=params(40),
        cost_estimate=pl.CostEstimate(
            flops=2 * 9 * 384 * 384 * 128, bytes_accessed=17_000_000, transcendentals=0
        ),
        name="prep",
    )(meso_weight, lift_weight, terrain_weight, patch16, merging_weight, decoder_weight)


def neighbours(v):
    width = v.shape[1]
    lane = lax.broadcasted_iota(jnp.int32, (1, width), 1) % COLS
    left, right = [], []
    for r in range(width // COLS):
        piece = v[:, r * COLS : (r + 1) * COLS]
        left.append(pltpu.roll(piece, 1, 1))
        right.append(pltpu.roll(piece, COLS - 1, 1))
    left = jnp.where(lane == 0, 0.0, jnp.concatenate(left, axis=1))
    right = jnp.where(lane == COLS - 1, 0.0, jnp.concatenate(right, axis=1))
    return left, right


def logistic(v):
    return 0.5 * (1.0 + jnp.tanh(0.5 * v))


def main_kernel(
    place, x, wm, wt, gw, dw, gt, dt, hw, out, x3, p9, j3, jslope, m3, mslope, dout, d3, e3
):
    segment, first_row = place[0], place[1] * ROWS

    def lanes(row):
        return pl.ds(pl.multiple_of(row * COLS, COLS), CHUNK)

    def inside(row):
        at = lax.broadcasted_iota(jnp.int32, (1, CHUNK), 1) // COLS + row + first_row
        return jnp.logical_and(at >= 0, at < 8 * ROWS)

    n_in, n_join, n_mix, n_dec, n_back = (
        ROWS + 2 * HALO,
        ROWS + 8,
        ROWS + 6,
        ROWS + 4,
        ROWS + 2,
    )

    def load(i, carry):
        s, r = i // n_in, i % n_in
        v = x[s, r].astype(F32)
        left, right = neighbours(v)
        at = pl.ds(pl.multiple_of(r * COLS, COLS), COLS)
        for b, u in enumerate((left, v, right)):
            u = u.astype(BF)
            x3[s, b * LEV : (b + 1) * LEV, at] = u[:LEV]
            for a in range(3):

                @pl.when(jnp.logical_and(r >= a, r < n_join + a))
                def _(a=a, b=b, u=u):
                    to = pl.ds(pl.multiple_of((r - a) * COLS, COLS), COLS)
                    tap = 3 * a + b
                    p9[s, tap * SLAB : (tap + 1) * SLAB, to] = u[LEV:]

        return carry

    lax.fori_loop(0, 2 * n_in, load, 0)

    def first(i, carry):
        s, k = i // (n_join // 2), i % (n_join // 2)
        row = 2 * k
        pre_t = dot(wt[...], p9[s, :, lanes(row)])
        pre_m = sum(
            dot(wm[:, a * 3 * LEV : (a + 1) * 3 * LEV], x3[s, :, lanes(row + a)]) for a in range(3)
        )
        valid = inside(row - 4)
        for at, pre in ((0, pre_t), (TERR, pre_m)):
            size = pre.shape[0]
            sigma = logistic(pre)
            v = jnp.where(valid, pre * sigma, 0.0)
            left, right = neighbours(v)
            for b, u in enumerate((left, v, right)):
                j3[s, b * JOINT + at : b * JOINT + at + size, lanes(row)] = u.astype(BF)

            @pl.when(jnp.logical_and(row >= 4, row < 8))
            def _(at=at, size=size, sigma=sigma, pre=pre):
                jslope[s, at : at + size, lanes(row - 4)] = sigma * (1.0 + pre * (1.0 - sigma))

        return carry

    lax.fori_loop(0, n_join, first, 0)

    def merge(i, carry):
        s, k = i // (n_mix // 2), i % (n_mix // 2)
        row = 2 * k
        pre = sum(
            dot(gw[:, a * 3 * JOINT : (a + 1) * 3 * JOINT], j3[s, :, lanes(row + a)])
            for a in range(3)
        )
        sigma = logistic(pre)
        v = jnp.where(inside(row - 3), pre * sigma, 0.0)
        left, right = neighbours(v)
        for b, u in enumerate((left, v, right)):
            m3[s, b * MIX : (b + 1) * MIX, lanes(row)] = u.astype(BF)
        mslope[s, :, lanes(row)] = sigma * (1.0 + pre * (1.0 - sigma))
        return carry

    lax.fori_loop(0, n_mix, merge, 0)

    scale = 1.0 / math.sqrt(8 * 32 * 128)

    def decode(i, carry):
        s, k = i // (n_dec // 2), i % (n_dec // 2)
        row = 2 * k
        pre = sum(
            dot(dw[:, a * 3 * MIX : (a + 1) * 3 * MIX], m3[s, :, lanes(row + a)]) for a in range(3)
        )
        sigma = logistic(pre)
        cot = jnp.concatenate([x[s, row + 3, LEV:], x[s, row + 4, LEV:]], axis=1)
        back = scale * dot(hw[...], cot)
        v = sigma * (1.0 + pre * (1.0 - sigma)) * back
        left, right = neighbours(v)
        for b, u in enumerate((right, v, left)):
            d3[s, b * MIX : (b + 1) * MIX, lanes(row)] = u.astype(BF)

        @pl.when(jnp.logical_and(row >= 2, row < 6))
        def _():
            dout[s, :, lanes(row - 2)] = (pre * sigma).astype(BF)

        return carry

    lax.fori_loop(0, n_dec, decode, 0)

    def back_decoder(i, carry):
        s, k = i // (n_back // 2), i % (n_back // 2)
        row = 2 * k
        back = sum(
            dot(dt[:, a * 3 * MIX : (a + 1) * 3 * MIX], d3[s, :, lanes(row + 2 - a)])
            for a in range(3)
        )
        v = jnp.where(inside(row - 1), mslope[s, :, lanes(row + 2)] * back, 0.0)
        left, right = neighbours(v)
        for b, u in enumerate((right, v, left)):
            e3[s, b * MIX : (b + 1) * MIX, lanes(row)] = u.astype(BF)
        return carry

    lax.fori_loop(0, n_back, back_decoder, 0)

    def back_merging(i, carry):
        s, k = i // (ROWS // 2), i % (ROWS // 2)
        row = 2 * k
        back = sum(
            dot(gt[:, a * 3 * MIX : (a + 1) * 3 * MIX], e3[s, :, lanes(row + 2 - a)])
            for a in range(3)
        )
        jslope[s, :, lanes(row)] = jslope[s, :, lanes(row)] * back
        return carry

    lax.fori_loop(0, ROWS, back_merging, 0)

    def put(rows, column, value):
        value = value.astype(BF)
        width = value.shape[1]
        done = 0
        while done < width:
            group, offset = divmod(column + done, WIDE)
            take = min(width - done, WIDE - offset)
            for t in range(value.shape[0] // 16):
                out[(rows // 16 + t) * 8 + group, :, offset : offset + take] = value[
                    t * 16 : (t + 1) * 16, done : done + take
                ]
            done += take

    own = ROWS * COLS
    q = pl.ds(pl.multiple_of(segment * OQ, OQ), OQ)
    qd = pl.ds(pl.multiple_of(MIX + segment * OQ, OQ), OQ)
    qm = pl.ds(pl.multiple_of(TERR + segment * MQ, 32), MQ)
    e_own = [e3[s, qd, COLS : COLS + own] for s in range(2)]
    for tap in range(9):
        a, b = divmod(tap, 3)
        put(
            0,
            tap * JOINT,
            sum(
                dot_nt(e_own[s], j3[s, b * JOINT : (b + 1) * JOINT, (3 + a) * COLS : (3 + a) * COLS + own])
                for s in range(2)
            ),
        )
    column = 9 * JOINT
    d_own = [d3[s, qd, 2 * COLS : 2 * COLS + own] for s in range(2)]
    for a in range(3):
        put(
            0,
            column + a * 3 * MIX,
            sum(
                dot_nt(d_own[s], m3[s, :, (2 + a) * COLS : (2 + a) * COLS + own]) for s in range(2)
            ),
        )
    column += 9 * MIX
    h_own = [jslope[s, qm, :].astype(BF) for s in range(2)]
    for a in range(3):
        h = sum(
            dot_nt(h_own[s], x3[s, :, (4 + a) * COLS : (4 + a) * COLS + own]) for s in range(2)
        )
        put(0, column + a * 3 * LEV, h[:64])
        spare = column + 9 * LEV
        for c in range(3):
            at = a * 3 * LEV + c * LEV
            piece = h[64:, c * LEV : (c + 1) * LEV]
            if at < 640:
                put(0, spare + at, piece)
            else:
                put(32, spare + at - 640, piece)
    put(32, column + 9 * LEV + 512, jnp.zeros((32, 128), F32))
    column += 9 * LEV + 640
    t_own = [jslope[s, q, :].astype(BF) for s in range(2)]
    g = sum(dot_nt(t_own[s], p9[s, :, 4 * COLS : 4 * COLS + own]) for s in range(2))
    head = scale * sum(
        dot_nt(
            dout[s, q, :],
            jnp.concatenate([x[s, HALO + r, LEV:] for r in range(ROWS)], axis=1),
        )
        for s in range(2)
    )
    tail = 8 * WIDE - column
    put(0, column, jnp.concatenate([g, head, jnp.zeros((OQ, tail - 10 * SLAB), F32)], axis=1))


def main(place, x, wm, wt, gw, dw, gt, dt, hw):
    vmem = pl.BlockSpec(memory_space=pltpu.VMEM)
    return pl.pallas_call(
        main_kernel,
        out_shape=jax.ShapeDtypeStruct((PIECES, 16, WIDE), BF),
        in_specs=[pl.BlockSpec(memory_space=pltpu.SMEM)] + [vmem] * 8,
        out_specs=vmem,
        scratch_shapes=[
            pltpu.VMEM((2, 3 * LEV, (ROWS + 2 * HALO) * COLS), BF),
            pltpu.VMEM((2, 9 * SLAB, (ROWS + 8) * COLS), BF),
            pltpu.VMEM((2, 3 * JOINT, (ROWS + 8) * COLS), BF),
            pltpu.VMEM((2, JOINT, ROWS * COLS), F32),
            pltpu.VMEM((2, 3 * MIX, (ROWS + 6) * COLS), BF),
            pltpu.VMEM((2, MIX, (ROWS + 6) * COLS), F32),
            pltpu.VMEM((2, MIX, ROWS * COLS), BF),
            pltpu.VMEM((2, 3 * MIX, (ROWS + 4) * COLS), BF),
            pltpu.VMEM((2, 3 * MIX, (ROWS + 2) * COLS), BF),
        ],
        compiler_params=params(56),
        cost_estimate=pl.CostEstimate(
            flops=19_000_000_000, bytes_accessed=14_000_000, transcendentals=3_000_000
        ),
        name="sections",
    )(place, x, wm, wt, gw, dw, gt, dt, hw)


def finish_kernel(got, mw, lw, tw, pw, patch, terrain, lift, meso, merging, decoder, head, ht, gt):
    for seg in range(4):
        for t in range(4):
            lo = seg * OQ + t * 16

            def take(column, width):
                pieces = []
                done = 0
                while done < width:
                    group, offset = divmod(column + done, WIDE)
                    n = min(width - done, WIDE - offset)
                    pieces.append(got[seg * PIECES + t * 8 + group, :, offset : offset + n])
                    done += n
                return pieces[0] if len(pieces) == 1 else jnp.concatenate(pieces, axis=1)

            merging[lo : lo + 16, :] = take(0, 9 * JOINT).astype(F32)
            decoder[lo : lo + 16, :] = take(9 * JOINT, 9 * MIX).astype(F32)
            column = 9 * JOINT + 9 * MIX
            mlo = seg * MQ + t * 16
            ht[mlo : mlo + 16, :] = take(column, 9 * LEV)
            mlo = seg * MQ + 64 + (t % 2) * 16
            if t < 2:
                ht[mlo : mlo + 16, :640] = take(column + 9 * LEV, 640)
            else:
                ht[mlo : mlo + 16, 640:] = take(column + 9 * LEV, 512)
            gt[lo : lo + 16, :] = take(column + 9 * LEV + 640, 256)
    h = ht[...]
    for tap in range(9):
        meso[:, tap * MESO : (tap + 1) * MESO] = dot_nt(h[:, tap * LEV : (tap + 1) * LEV], lw[...])
    turned = h.astype(F32).T.astype(BF)
    lift[...] = sum(
        dot(turned[tap * LEV : (tap + 1) * LEV, :], mw[:, tap * MESO : (tap + 1) * MESO])
        for tap in range(9)
    ).T
    g = gt[...]
    for tap in range(9):
        terrain[:, tap * TERR : (tap + 1) * TERR] = dot_nt(
            g[:, tap * SLAB : (tap + 1) * SLAB], pw[...]
        )
    turned = g.astype(F32).T
    patch[...] = sum(
        dot(
            turned[tap * SLAB : (tap + 1) * SLAB, :].astype(BF),
            tw[:, tap * TERR : (tap + 1) * TERR],
        )
        for tap in range(9)
    ).T[:, :8]
    head[...] = turned[9 * SLAB + 8 : 9 * SLAB + 11, :]


def finish(got, meso_weight, lift_weight, terrain_weight, patch16):
    return pl.pallas_call(
        finish_kernel,
        out_shape=(
            jax.ShapeDtypeStruct((TERR, 8), F32),
            jax.ShapeDtypeStruct((TERR, 9 * TERR), F32),
            jax.ShapeDtypeStruct((MESO, LEV), F32),
            jax.ShapeDtypeStruct((MESO, 9 * MESO), F32),
            jax.ShapeDtypeStruct((MIX, 9 * JOINT), F32),
            jax.ShapeDtypeStruct((MIX, 9 * MIX), F32),
            jax.ShapeDtypeStruct((3, MIX), F32),
        ),
        scratch_shapes=[pltpu.VMEM((MESO, 9 * LEV), BF), pltpu.VMEM((MIX, 256), BF)],
        compiler_params=params(52),
        name="finish",
    )(got, meso_weight, lift_weight, terrain_weight, patch16)


def packed(terrain_in, meso_in, wind_cot):
    samples = terrain_in.shape[0]
    source = lax.broadcasted_iota(jnp.int32, (2 * COLS, 2 * COLS), 0)
    target = lax.broadcasted_iota(jnp.int32, (2 * COLS, 2 * COLS), 1)
    pick = (source == 2 * (target % COLS) + target // COLS).astype(BF)
    split = dot(terrain_in.reshape(samples * 4 * ROWS, 2 * COLS), pick).astype(BF)
    patches = (
        split.reshape(samples, 2, ROWS, 2, 2, COLS)
        .transpose(0, 2, 1, 3, 4, 5)
        .reshape(samples, ROWS, 8, COLS)
    )
    levels = meso_in.reshape(samples, LEV, ROWS, COLS).transpose(0, 2, 1, 3)
    cot = wind_cot.transpose(0, 2, 1, 3)
    rest = jnp.zeros((samples, ROWS, PACK - LEV - 11, COLS), BF)
    return jnp.concatenate([levels, patches, cot, rest], axis=2)


def shifted(v, by):
    count = lax.axis_size("space")
    return lax.ppermute(
        v, "space", [(i, i + by) for i in range(count) if 0 <= i + by < count]
    )


def local(
    terrain_in,
    meso_in,
    wind_cot,
    patch_weight,
    terrain_weight,
    lift_weight,
    meso_weight,
    merging_weight,
    decoder_weight,
    head_weight,
):
    own = packed(terrain_in, meso_in, wind_cot)
    haloed = jnp.concatenate(
        [shifted(own[:, 3:], 2), shifted(own, 1), own, shifted(own, -1), shifted(own[:, :1], -2)],
        axis=1,
    )
    patch16 = jnp.pad(patch_weight, ((0, 0), (0, SLAB - 8)))
    head16 = jnp.pad(head_weight.T, ((0, 0), (8, SLAB - 11)))
    wm, wt, gt, dt = prep(
        meso_weight, lift_weight, terrain_weight, patch16, merging_weight, decoder_weight
    )
    place = jnp.stack([lax.axis_index("segment"), lax.axis_index("space")]).astype(jnp.int32)
    parts = main(place, haloed, wm, wt, merging_weight, decoder_weight, gt, dt, head16)
    parts = lax.all_to_all(parts, ("dp", "space"), 0, 0, tiled=True)
    mine = jnp.sum(parts.astype(F32), axis=0).astype(BF)
    got = lax.all_gather(mine, ("segment", "dp", "space"))
    return finish(got, meso_weight, lift_weight, terrain_weight, patch16)


def solution(mesh):
    placed = (
        P("dp", None, "space", None),
        P("dp", None, None, "space", None),
        P("dp", None, "space", None),
        P(),
        P(),
        P(),
        P(),
        P(),
        P(),
        P(),
    )
    return jax.shard_map(
        local,
        mesh=mesh,
        in_specs=placed,
        out_specs=(P(), P(), P(), P(), P(), P(), P()),
        check_vma=False,
    )
```

```python
import math

import jax
import jax.numpy as jnp
from jax import lax
from jax.experimental import pallas as pl
from jax.experimental.pallas import tpu as pltpu
from jax.sharding import PartitionSpec as P

BF = jnp.bfloat16
F32 = jnp.float32
TERR, MESO, MIX = 256, 384, 256
JOINT = TERR + MESO
LEV = 128
SLAB = 16
PACK = LEV + SLAB
ROWS, COLS = 4, 128
HALO = 5
OQ, MQ = MIX // 4, MESO // 4
WIDE = 1280
NT = (((1,), (1,)), ((), ()))


def dot(a, b):
    return jnp.dot(a, b, preferred_element_type=F32)


def dot_nt(a, b):
    return lax.dot_general(a, b, NT, preferred_element_type=F32)


def params(mib):
    return pltpu.CompilerParams(vmem_limit_bytes=mib * 1024 * 1024)


def sixteen(v, above):
    rows, width = v.shape
    parts = [v.astype(F32)]
    if above:
        parts.insert(0, jnp.zeros((above, width), F32))
    if above + rows < SLAB:
        parts.append(jnp.zeros((SLAB - above - rows, width), F32))
    return jnp.concatenate(parts, axis=0)


def neighbours(v):
    width = v.shape[1]
    lane = lax.broadcasted_iota(jnp.int32, (1, width), 1) % COLS
    left, right = [], []
    for r in range(width // COLS):
        piece = v[:, r * COLS : (r + 1) * COLS]
        left.append(pltpu.roll(piece, 1, 1))
        right.append(pltpu.roll(piece, COLS - 1, 1))
    left = jnp.where(lane == 0, 0.0, jnp.concatenate(left, axis=1))
    right = jnp.where(lane == COLS - 1, 0.0, jnp.concatenate(right, axis=1))
    return left, right


def logistic(v):
    return 0.5 * (1.0 + jnp.tanh(0.5 * v))


def main_kernel(place, far_up, up, mid, down, far_down, lw, pw, hw, *refs):
    mw_hbm, tw_hbm, gw_hbm, dw_hbm, keep, send, out = refs[:7]
    mw, tw, gw, dw, wm, wt, gt, dt, sems = refs[7:16]
    x3, p9, j3, jslope, jdelta, m3, mslope, dout, d3, e3 = refs[16:]
    pairs = ((mw_hbm, mw), (tw_hbm, tw), (gw_hbm, gw), (dw_hbm, dw))
    copies = [pltpu.make_async_copy(u, v, sems.at[i]) for i, (u, v) in enumerate(pairs)]
    for copy in copies:
        copy.start()
    segment, first_row = place[0], place[1] * ROWS
    chip, core = place[1] // 2, place[1] % 2

    def cut(row, rows):
        return slice(row * COLS, (row + rows) * COLS)

    def inside(row, rows):
        at = lax.broadcasted_iota(jnp.int32, (1, rows * COLS), 1) // COLS + row + first_row
        return jnp.logical_and(at >= 0, at < 8 * ROWS)

    n_in, n_join, n_mix, n_dec, n_back = (
        ROWS + 2 * HALO,
        ROWS + 8,
        ROWS + 6,
        ROWS + 4,
        ROWS + 2,
    )

    def slab(s, r):
        for ref, rows in ((far_up, 1), (up, ROWS), (mid, ROWS), (down, ROWS), (far_down, 1)):
            if r < rows:
                return ref[s, r]
            r -= rows

    for r in range(n_in):
        for s in range(2):
            v = slab(s, r).astype(F32)
            left, right = neighbours(v)
            for b, u in enumerate((left, v, right)):
                u = u.astype(BF)
                x3[s, b * LEV : (b + 1) * LEV, cut(r, 1)] = u[:LEV]
                for a in range(3):
                    if a <= r < n_join + a:
                        tap = 3 * a + b
                        p9[s, tap * SLAB : (tap + 1) * SLAB, cut(r - a, 1)] = u[LEV:]

    pw16 = sixteen(pw[...], 0).astype(BF)
    head_turned = sixteen(hw[...], 8).T.astype(BF)
    copies[0].wait()
    for tap in range(9):
        wm[:, tap * LEV : (tap + 1) * LEV] = dot(
            mw[:, tap * MESO : (tap + 1) * MESO], lw[...]
        ).astype(BF)
    copies[1].wait()
    wt[...] = jnp.concatenate(
        [dot_nt(tw[:, tap * TERR : (tap + 1) * TERR], pw16).astype(BF) for tap in range(9)], axis=1
    )

    def first(row, rows):
        for s in range(2):
            pre_t = dot(wt[...], p9[s, :, cut(row, rows)])
            pre_m = sum(
                dot(wm[:, a * 3 * LEV : (a + 1) * 3 * LEV], x3[s, :, cut(row + a, rows)])
                for a in range(3)
            )
            for at, pre in ((0, pre_t), (TERR, pre_m)):
                size = pre.shape[0]
                sigma = logistic(pre)
                v = jnp.where(inside(row - 4, rows), pre * sigma, 0.0)
                left, right = neighbours(v)
                for b, u in enumerate((left, v, right)):
                    j3[s, b * JOINT + at : b * JOINT + at + size, cut(row, rows)] = u.astype(BF)
                if row == 4:
                    jslope[s, at : at + size, :] = sigma * (1.0 + pre * (1.0 - sigma))

    for row in (0, 4, 8):
        first(row, 4)

    copies[2].wait()
    copies[3].wait()
    for tap in range(9):
        gt[:, tap * MIX : (tap + 1) * MIX] = gw[:, tap * JOINT : (tap + 1) * JOINT].T
        dt[:, tap * MIX : (tap + 1) * MIX] = dw[:, tap * MIX : (tap + 1) * MIX].T

    for row in (0, 5):
        for s in range(2):
            pre = sum(
                dot(gw[:, a * 3 * JOINT : (a + 1) * 3 * JOINT], j3[s, :, cut(row + a, 5)])
                for a in range(3)
            )
            sigma = logistic(pre)
            v = jnp.where(inside(row - 3, 5), pre * sigma, 0.0)
            left, right = neighbours(v)
            for b, u in enumerate((left, v, right)):
                m3[s, b * MIX : (b + 1) * MIX, cut(row, 5)] = u.astype(BF)
            mslope[s, :, cut(row, 5)] = sigma * (1.0 + pre * (1.0 - sigma))

    scale = 1.0 / math.sqrt(8 * 32 * 128)

    for row in (0, 4):
        for s in range(2):
            pre = sum(
                dot(dw[:, a * 3 * MIX : (a + 1) * 3 * MIX], m3[s, :, cut(row + a, 4)])
                for a in range(3)
            )
            sigma = logistic(pre)
            cot = jnp.concatenate([slab(s, row + 3 + r)[LEV:] for r in range(4)], axis=1)
            back = scale * dot(head_turned, cot)
            v = sigma * (1.0 + pre * (1.0 - sigma)) * back
            left, right = neighbours(v)
            for b, u in enumerate((right, v, left)):
                d3[s, b * MIX : (b + 1) * MIX, cut(row, 4)] = u.astype(BF)
            half = slice(2 * COLS, 4 * COLS) if row == 0 else slice(0, 2 * COLS)
            dout[s, :, cut(row // 2, 2)] = (pre * sigma)[:, half].astype(BF)

    for row in (0, 3):
        for s in range(2):
            back = sum(
                dot(dt[:, a * 3 * MIX : (a + 1) * 3 * MIX], d3[s, :, cut(row + 2 - a, 3)])
                for a in range(3)
            )
            v = jnp.where(inside(row - 1, 3), mslope[s, :, cut(row + 2, 3)] * back, 0.0)
            left, right = neighbours(v)
            for b, u in enumerate((right, v, left)):
                e3[s, b * MIX : (b + 1) * MIX, cut(row, 3)] = u.astype(BF)

    for s in range(2):
        back = sum(
            dot(gt[:, a * 3 * MIX : (a + 1) * 3 * MIX], e3[s, :, cut(2 - a, 4)]) for a in range(3)
        )
        jdelta[s] = (jslope[s] * back).astype(BF)

    def put(rows, column, value):
        value = value.astype(BF)
        width = value.shape[1]
        done = 0
        while done < width:
            group, offset = divmod(column + done, WIDE)
            take = min(width - done, WIDE - offset)
            slot = 4 * lax.rem(core + group // 4, 2) + lax.rem(group % 4 + 4 - chip, 4)
            out[slot, rows : rows + value.shape[0], offset : offset + take] = value[
                :, done : done + take
            ]
            done += take

    def stacked(delta):
        def zero(rows):
            return jnp.zeros((delta.shape[0], rows * COLS), BF)

        return jnp.concatenate(
            [
                jnp.concatenate([delta, zero(2)], axis=1),
                jnp.concatenate([zero(1), delta, zero(1)], axis=1),
                jnp.concatenate([zero(2), delta], axis=1),
            ],
            axis=0,
        )

    q = pl.ds(pl.multiple_of(segment * OQ, OQ), OQ)
    qd = pl.ds(pl.multiple_of(MIX + segment * OQ, OQ), OQ)
    qm = pl.ds(pl.multiple_of(TERR + segment * MQ, 32), MQ)
    d_own = [stacked(d3[s, qd, cut(2, ROWS)]) for s in range(2)]
    e_own = [stacked(e3[s, qd, cut(1, ROWS)]) for s in range(2)]
    h_own = [stacked(jdelta[s, qm, :]) for s in range(2)]
    for b in range(3):
        part = sum(
            dot_nt(e_own[s], j3[s, b * JOINT : (b + 1) * JOINT, cut(3, ROWS + 2)])
            for s in range(2)
        )
        for a in range(3):
            put(0, (3 * a + b) * JOINT, part[a * OQ : (a + 1) * OQ])
    column = 9 * JOINT
    part = sum(dot_nt(d_own[s], m3[s, :, cut(2, ROWS + 2)]) for s in range(2))
    for a in range(3):
        put(0, column + a * 3 * MIX, part[a * OQ : (a + 1) * OQ])
    column += 9 * MIX
    part = sum(dot_nt(h_own[s], x3[s, :, cut(4, ROWS + 2)]) for s in range(2))
    for a in range(3):
        h = part[a * MQ : (a + 1) * MQ]
        put(0, column + a * 3 * LEV, h[:64])
        spare = column + 9 * LEV
        for c in range(3):
            at = a * 3 * LEV + c * LEV
            piece = h[64:, c * LEV : (c + 1) * LEV]
            if at < 640:
                put(0, spare + at, piece)
            else:
                put(32, spare + at - 640, piece)
    put(32, column + 9 * LEV + 512, jnp.zeros((32, 128), F32))
    column += 9 * LEV + 640
    g = sum(dot_nt(jdelta[s, q, :], p9[s, :, cut(4, ROWS)]) for s in range(2))
    head = scale * sum(
        dot_nt(
            dout[s, q, :],
            jnp.concatenate([mid[s, r, LEV:] for r in range(ROWS)], axis=1),
        )
        for s in range(2)
    )
    tail = 8 * WIDE - column
    put(0, column, jnp.concatenate([g, head, jnp.zeros((OQ, tail - 10 * SLAB), F32)], axis=1))
    keep[...] = out[:4]
    send[...] = out[4:]


def main(place, pieces, lift_weight, patch_turned, head_weight, *weights):
    smem = pl.BlockSpec(memory_space=pltpu.SMEM)
    vmem = pl.BlockSpec(memory_space=pltpu.VMEM)
    hbm = pl.BlockSpec(memory_space=pl.ANY)
    return pl.pallas_call(
        main_kernel,
        out_shape=(jax.ShapeDtypeStruct((4, OQ, WIDE), BF),) * 2,
        in_specs=[smem] + [vmem] * 8 + [hbm] * 4,
        out_specs=(vmem, vmem),
        scratch_shapes=[
            pltpu.VMEM((8, OQ, WIDE), BF),
            pltpu.VMEM((MESO, 9 * MESO), BF),
            pltpu.VMEM((TERR, 9 * TERR), BF),
            pltpu.VMEM((MIX, 9 * JOINT), BF),
            pltpu.VMEM((MIX, 9 * MIX), BF),
            pltpu.VMEM((MESO, 9 * LEV), BF),
            pltpu.VMEM((TERR, 9 * SLAB), BF),
            pltpu.VMEM((JOINT, 9 * MIX), BF),
            pltpu.VMEM((MIX, 9 * MIX), BF),
            pltpu.SemaphoreType.DMA((4,)),
            pltpu.VMEM((2, 3 * LEV, (ROWS + 2 * HALO) * COLS), BF),
            pltpu.VMEM((2, 9 * SLAB, (ROWS + 8) * COLS), BF),
            pltpu.VMEM((2, 3 * JOINT, (ROWS + 8) * COLS), BF),
            pltpu.VMEM((2, JOINT, ROWS * COLS), F32),
            pltpu.VMEM((2, JOINT, ROWS * COLS), BF),
            pltpu.VMEM((2, 3 * MIX, (ROWS + 6) * COLS), BF),
            pltpu.VMEM((2, MIX, (ROWS + 6) * COLS), F32),
            pltpu.VMEM((2, MIX, ROWS * COLS), BF),
            pltpu.VMEM((2, 3 * MIX, (ROWS + 4) * COLS), BF),
            pltpu.VMEM((2, 3 * MIX, (ROWS + 2) * COLS), BF),
        ],
        compiler_params=params(56),
        cost_estimate=pl.CostEstimate(
            flops=19_000_000_000, bytes_accessed=14_000_000, transcendentals=3_000_000
        ),
        name="sections",
    )(place, *pieces, lift_weight, patch_turned, head_weight, *weights)


def split_kernel(keep, came, own, next1, next2, next3):
    own[...] = keep[0].astype(F32) + came[0].astype(F32)
    for j, to in enumerate((next1, next2, next3), 1):
        to[...] = (keep[j].astype(F32) + came[j].astype(F32)).astype(BF)


def total_kernel(own, one, two, three, out):
    out[...] = (
        (own[...].astype(F32) + two[...].astype(F32))
        + (one[...].astype(F32) + three[...].astype(F32))
    ).astype(BF)


def stack_kernel(own, one, two, three, out):
    for j, v in enumerate((own, one, two, three)):
        out[j] = v[...]


def small(kernel, out_shape, *operands):
    return pl.pallas_call(
        kernel, out_shape=out_shape, compiler_params=params(16), name=kernel.__name__[:-7]
    )(*operands)


def by_space(v, by):
    return lax.ppermute(v, "space", [(i, (i + 2 * by) % 8) for i in range(8)])


def to_partner(v):
    return lax.ppermute(v, "space", [(i, i ^ 1) for i in range(8)])


def by_depth(v, by):
    return lax.ppermute(v, "dp", [(i, (i + by) % 4) for i in range(4)])


def across(v, by, chip_core):
    pairs = []
    for seg in range(4):
        for place in range(8):
            if place % 2 == chip_core:
                to = (seg, (place + 2 * by) % 8)
            else:
                to = ((seg + by) % 4, place)
            pairs.append((seg * 8 + place, to[0] * 8 + to[1]))
    return lax.ppermute(v, ("segment", "space"), pairs)


STEPS = (0, -1, 1, -2)


def summed_everywhere(keep, send):
    piece = jax.ShapeDtypeStruct((OQ, WIDE), BF)
    wide = jax.ShapeDtypeStruct((OQ, WIDE), F32)
    own, *parts = small(split_kernel, (wide, piece, piece, piece), keep, to_partner(send))
    own = small(total_kernel, piece, own, *[by_space(p, j) for j, p in enumerate(parts, 1)])
    own = small(total_kernel, piece, own, *[by_depth(own, j) for j in (1, 2, 3)])
    four = jax.ShapeDtypeStruct((4, OQ, WIDE), BF)
    block = small(stack_kernel, four, own, *[across(own, j, 0) for j in (1, 2, 3)])
    behind, ahead = across(block, 1, 1), across(block, -1, 1)
    mine = (block, behind, ahead, across(behind, 1, 1))
    return mine + tuple(to_partner(v) for v in mine)


def finish_kernel(place, *refs):
    blocks, (lw, pw, mw_hbm, tw_hbm) = refs[:8], refs[8:12]
    patch, lift, head, terrain, meso, merging, decoder = refs[12:19]
    mw, tw, stage, wide_m, wide_t, ht, gt, sems = refs[19:]
    reads = [
        pltpu.make_async_copy(mw_hbm, mw, sems.at[0]),
        pltpu.make_async_copy(tw_hbm, tw, sems.at[1]),
    ]
    for copy in reads:
        copy.start()
    segment, chip, core = place[0], place[1] // 2, place[1] % 2
    for i, block in enumerate(blocks):
        kind = core if i < 4 else 1 - core
        for j in range(4):
            along_space = jnp.where(kind == 0, -j, STEPS[i % 4])
            along_segment = jnp.where(kind == 0, STEPS[i % 4], -j)
            group = 4 * kind + lax.rem(chip + along_space + 4, 4)
            row = lax.rem(segment + along_segment + 4, 4) * OQ
            stage[
                pl.ds(pl.multiple_of(row, OQ), OQ), pl.ds(pl.multiple_of(group * WIDE, WIDE), WIDE)
            ] = block[j].astype(F32)
    column = 9 * JOINT + 9 * MIX
    writes = [
        pltpu.make_async_copy(stage.at[:, : 9 * JOINT], merging, sems.at[2]),
        pltpu.make_async_copy(stage.at[:, 9 * JOINT : column], decoder, sems.at[3]),
    ]
    for copy in writes:
        copy.start()
    for seg in range(4):
        lo = seg * OQ
        at = seg * MQ
        ht[at : at + 64, :] = stage[lo : lo + OQ, column : column + 9 * LEV].astype(BF)
        spare = column + 9 * LEV
        ht[at + 64 : at + MQ, :640] = stage[lo : lo + 32, spare : spare + 640].astype(BF)
        ht[at + 64 : at + MQ, 640:] = stage[lo + 32 : lo + OQ, spare : spare + 512].astype(BF)
        gt[lo : lo + OQ, :] = stage[lo : lo + OQ, spare + 640 : spare + 896]
    for a in range(3):
        for tap in range(3 * a, 3 * a + 3):
            wide_m[:, tap * MESO : (tap + 1) * MESO] = dot_nt(
                ht[:, tap * LEV : (tap + 1) * LEV], lw[...]
            )
        part = slice(3 * a * MESO, 3 * (a + 1) * MESO)
        writes.append(pltpu.make_async_copy(wide_m.at[:, part], meso.at[:, part], sems.at[4 + a]))
        writes[-1].start()
    pw16 = sixteen(pw[...], 0).astype(BF)
    g = gt[...]
    for tap in range(9):
        wide_t[:, tap * TERR : (tap + 1) * TERR] = dot(
            g[:, tap * SLAB : (tap + 1) * SLAB].astype(BF), pw16
        )
    writes.append(pltpu.make_async_copy(wide_t, terrain, sems.at[7]))
    writes[-1].start()
    turned = g.T
    head[...] = turned[9 * SLAB + 8 : 9 * SLAB + 11, :]
    reads[1].wait()
    patch[...] = sum(
        dot(
            turned[tap * SLAB : (tap + 1) * SLAB, :].astype(BF),
            tw[:, tap * TERR : (tap + 1) * TERR],
        )
        for tap in range(9)
    )[:8]
    turned = ht[...].astype(F32).T.astype(BF)
    reads[0].wait()
    lift[...] = sum(
        dot(turned[tap * LEV : (tap + 1) * LEV, :], mw[:, tap * MESO : (tap + 1) * MESO])
        for tap in range(9)
    ).T
    for copy in writes:
        copy.wait()


def finish(place, blocks, lift_weight, patch_turned, meso_weight, terrain_weight):
    smem = pl.BlockSpec(memory_space=pltpu.SMEM)
    vmem = pl.BlockSpec(memory_space=pltpu.VMEM)
    hbm = pl.BlockSpec(memory_space=pl.ANY)
    patch, lift, head, terrain, meso, merging, decoder = pl.pallas_call(
        finish_kernel,
        out_shape=(
            jax.ShapeDtypeStruct((8, TERR), F32),
            jax.ShapeDtypeStruct((MESO, LEV), F32),
            jax.ShapeDtypeStruct((3, MIX), F32),
            jax.ShapeDtypeStruct((TERR, 9 * TERR), F32),
            jax.ShapeDtypeStruct((MESO, 9 * MESO), F32),
            jax.ShapeDtypeStruct((MIX, 9 * JOINT), F32),
            jax.ShapeDtypeStruct((MIX, 9 * MIX), F32),
        ),
        in_specs=[smem] + [vmem] * 10 + [hbm] * 2,
        out_specs=(vmem,) * 3 + (hbm,) * 4,
        scratch_shapes=[
            pltpu.VMEM((MESO, 9 * MESO), BF),
            pltpu.VMEM((TERR, 9 * TERR), BF),
            pltpu.VMEM((MIX, 8 * WIDE), F32),
            pltpu.VMEM((MESO, 9 * MESO), F32),
            pltpu.VMEM((TERR, 9 * TERR), F32),
            pltpu.VMEM((MESO, 9 * LEV), BF),
            pltpu.VMEM((MIX, 256), F32),
            pltpu.SemaphoreType.DMA((8,)),
        ],
        compiler_params=params(40),
        name="finish",
    )(place, *blocks, lift_weight, patch_turned, meso_weight, terrain_weight)
    return patch.T, terrain, lift, meso, merging, decoder, head


def packed(terrain_in, meso_in, wind_cot):
    samples = terrain_in.shape[0]
    source = lax.broadcasted_iota(jnp.int32, (2 * COLS, 2 * COLS), 0)
    target = lax.broadcasted_iota(jnp.int32, (2 * COLS, 2 * COLS), 1)
    pick = (source == 2 * (target % COLS) + target // COLS).astype(BF)
    split = dot(terrain_in.reshape(samples * 4 * ROWS, 2 * COLS), pick).astype(BF)
    patches = (
        split.reshape(samples, 2, ROWS, 2, 2, COLS)
        .transpose(0, 2, 1, 3, 4, 5)
        .reshape(samples, ROWS, 8, COLS)
    )
    levels = meso_in.reshape(samples, LEV, ROWS, COLS).transpose(0, 2, 1, 3)
    cot = wind_cot.transpose(0, 2, 1, 3)
    rest = jnp.zeros((samples, ROWS, PACK - LEV - 11, COLS), BF)
    return jnp.concatenate([levels, patches, cot, rest], axis=2)


def shifted(v, by):
    count = lax.axis_size("space")
    return lax.ppermute(
        v, "space", [(i, i + by) for i in range(count) if 0 <= i + by < count]
    )


def local(
    terrain_in,
    meso_in,
    wind_cot,
    patch_weight,
    terrain_weight,
    lift_weight,
    meso_weight,
    merging_weight,
    decoder_weight,
    head_weight,
):
    own = packed(terrain_in, meso_in, wind_cot)
    up, down = shifted(own, 1), shifted(own, -1)
    far_up, far_down = shifted(own[:, 3:], 2), shifted(own[:, :1], -2)
    place = jnp.stack([lax.axis_index("segment"), lax.axis_index("space")]).astype(jnp.int32)
    keep, send = main(
        place,
        (far_up, up, own, down, far_down),
        lift_weight,
        patch_weight.T,
        head_weight,
        meso_weight,
        terrain_weight,
        merging_weight,
        decoder_weight,
    )
    blocks = summed_everywhere(keep, send)
    return finish(place, blocks, lift_weight, patch_weight.T, meso_weight, terrain_weight)


def solution(mesh):
    placed = (
        P("dp", None, "space", None),
        P("dp", None, None, "space", None),
        P("dp", None, "space", None),
        P(),
        P(),
        P(),
        P(),
        P(),
        P(),
        P(),
    )
    return jax.shard_map(
        local,
        mesh=mesh,
        in_specs=placed,
        out_specs=(P(), P(), P(), P(), P(), P(), P()),
        check_vma=False,
    )
```

```python
import math

import jax
import jax.numpy as jnp
from jax import lax
from jax.experimental import pallas as pl
from jax.experimental.pallas import tpu as pltpu
from jax.sharding import PartitionSpec as P

BF = jnp.bfloat16
F32 = jnp.float32
TERR, MESO, MIX = 256, 384, 256
JOINT = TERR + MESO
LEV = 128
SLAB = 16
PACK = LEV + SLAB
ROWS, COLS = 8, 128
HALO = 5
OQ, MQ = MIX // 4, MESO // 4
WIDE = 1280
NT = (((1,), (1,)), ((), ()))


def dot(a, b):
    return jnp.dot(a, b, preferred_element_type=F32)


def dot_nt(a, b):
    return lax.dot_general(a, b, NT, preferred_element_type=F32)


def params(mib):
    return pltpu.CompilerParams(vmem_limit_bytes=mib * 1024 * 1024)


def sixteen(v, above):
    rows, width = v.shape
    parts = [v.astype(F32)]
    if above:
        parts.insert(0, jnp.zeros((above, width), F32))
    if above + rows < SLAB:
        parts.append(jnp.zeros((SLAB - above - rows, width), F32))
    return jnp.concatenate(parts, axis=0)


def prep_kernel(mw, lw, tw, pw, gw, dw, wm, wt, gt, dt):
    for tap in range(9):
        wm[:, tap * LEV : (tap + 1) * LEV] = dot(
            mw[:, tap * MESO : (tap + 1) * MESO], lw[...]
        ).astype(BF)
    pw16 = sixteen(pw[...], 0).astype(BF)
    wt[...] = jnp.concatenate(
        [dot_nt(tw[:, tap * TERR : (tap + 1) * TERR], pw16).astype(BF) for tap in range(9)], axis=1
    )
    for tap in range(9):
        gt[:, tap * MIX : (tap + 1) * MIX] = gw[:, tap * JOINT : (tap + 1) * JOINT].T
        dt[:, tap * MIX : (tap + 1) * MIX] = dw[:, tap * MIX : (tap + 1) * MIX].T


def prep(meso_weight, lift_weight, terrain_weight, patch_turned, merging_weight, decoder_weight):
    return pl.pallas_call(
        prep_kernel,
        out_shape=(
            jax.ShapeDtypeStruct((MESO, 9 * LEV), BF),
            jax.ShapeDtypeStruct((TERR, 9 * SLAB), BF),
            jax.ShapeDtypeStruct((JOINT, 9 * MIX), BF),
            jax.ShapeDtypeStruct((MIX, 9 * MIX), BF),
        ),
        compiler_params=params(24),
        cost_estimate=pl.CostEstimate(
            flops=2 * 9 * 384 * 384 * 128, bytes_accessed=17_000_000, transcendentals=0
        ),
        name="prep",
    )(meso_weight, lift_weight, terrain_weight, patch_turned, merging_weight, decoder_weight)


def rows_kernel(place, own, partner, eight, first, last):
    core = place[1] % 2
    for c in range(2):

        @pl.when(core == c)
        def _(c=c):
            halves = (own, partner) if c == 0 else (partner, own)
            for r in range(ROWS):
                v = halves[r // 4][c, r % 4]
                eight[r] = v
                if r < HALO:
                    first[r] = v
                if r >= ROWS - HALO:
                    last[r - (ROWS - HALO)] = v


def chip_rows(place, own, partner):
    smem = pl.BlockSpec(memory_space=pltpu.SMEM)
    vmem = pl.BlockSpec(memory_space=pltpu.VMEM)
    return pl.pallas_call(
        rows_kernel,
        out_shape=tuple(
            jax.ShapeDtypeStruct((n, PACK, COLS), BF) for n in (ROWS, HALO, HALO)
        ),
        in_specs=[smem, vmem, vmem],
        out_specs=(vmem,) * 3,
        compiler_params=params(16),
        name="rows",
    )(place, own, partner)


def neighbours(v):
    width = v.shape[1]
    lane = lax.broadcasted_iota(jnp.int32, (1, width), 1) % COLS
    left, right = [], []
    for r in range(width // COLS):
        piece = v[:, r * COLS : (r + 1) * COLS]
        left.append(pltpu.roll(piece, 1, 1))
        right.append(pltpu.roll(piece, COLS - 1, 1))
    left = jnp.where(lane == 0, 0.0, jnp.concatenate(left, axis=1))
    right = jnp.where(lane == COLS - 1, 0.0, jnp.concatenate(right, axis=1))
    return left, right


def logistic(v):
    return 0.5 * (1.0 + jnp.tanh(0.5 * v))


def main_kernel(place, above, eight, below, hw, *refs):
    n_w = 6
    weights_hbm, keep, send, out = refs[:n_w], *refs[n_w : n_w + 3]
    wm, wt, gw, dw, dt, gt = weights = refs[n_w + 3 : 2 * n_w + 3]
    sems, x3, p9, j3, jslope, jdelta, m3, mslope, dout, d3, e3 = refs[2 * n_w + 3 :]
    copies = [
        pltpu.make_async_copy(u, v, sems.at[i]) for i, (u, v) in enumerate(zip(weights_hbm, weights))
    ]
    for copy in copies:
        copy.start()
    segment, depth = place[0], place[2]
    chip, core = place[1] // 2, place[1] % 2
    first_row = chip * ROWS

    def cut(row, rows):
        return slice(row * COLS, (row + rows) * COLS)

    def inside(row, rows):
        at = lax.broadcasted_iota(jnp.int32, (1, rows * COLS), 1) // COLS + row + first_row
        return jnp.logical_and(at >= 0, at < 4 * ROWS)

    def slab(r):
        for ref, rows in ((above, HALO), (eight, ROWS), (below, HALO)):
            if r < rows:
                return ref[r]
            r -= rows

    n_in, n_join = ROWS + 2 * HALO, ROWS + 8

    for r in range(n_in):
        v = slab(r).astype(F32)
        left, right = neighbours(v)
        for b, u in enumerate((left, v, right)):
            u = u.astype(BF)
            x3[b * LEV : (b + 1) * LEV, cut(r, 1)] = u[:LEV]
            for a in range(3):
                if a <= r < n_join + a:
                    tap = 3 * a + b
                    p9[tap * SLAB : (tap + 1) * SLAB, cut(r - a, 1)] = u[LEV:]

    head_turned = sixteen(hw[...], 8).T.astype(BF)
    copies[0].wait()
    copies[1].wait()

    for row in (0, 4, 8, 12):
        pre_t = dot(wt[...], p9[:, cut(row, 4)])
        pre_m = sum(
            dot(wm[:, a * 3 * LEV : (a + 1) * 3 * LEV], x3[:, cut(row + a, 4)]) for a in range(3)
        )
        for at, pre in ((0, pre_t), (TERR, pre_m)):
            size = pre.shape[0]
            sigma = logistic(pre)
            v = jnp.where(inside(row - 4, 4), pre * sigma, 0.0)
            left, right = neighbours(v)
            for b, u in enumerate((left, v, right)):
                j3[b * JOINT + at : b * JOINT + at + size, cut(row, 4)] = u.astype(BF)
            if row in (4, 8):
                jslope[at : at + size, cut(row - 4, 4)] = sigma * (1.0 + pre * (1.0 - sigma))

    copies[2].wait()
    for row, rows in ((0, 4), (4, 5), (9, 5)):
        pre = sum(
            dot(gw[:, a * 3 * JOINT : (a + 1) * 3 * JOINT], j3[:, cut(row + a, rows)])
            for a in range(3)
        )
        sigma = logistic(pre)
        v = jnp.where(inside(row - 3, rows), pre * sigma, 0.0)
        left, right = neighbours(v)
        for b, u in enumerate((left, v, right)):
            m3[b * MIX : (b + 1) * MIX, cut(row, rows)] = u.astype(BF)
        mslope[:, cut(row, rows)] = sigma * (1.0 + pre * (1.0 - sigma))

    scale = 1.0 / math.sqrt(8 * 32 * 128)

    copies[3].wait()
    for row in (0, 4, 8):
        pre = sum(
            dot(dw[:, a * 3 * MIX : (a + 1) * 3 * MIX], m3[:, cut(row + a, 4)]) for a in range(3)
        )
        sigma = logistic(pre)
        cot = jnp.concatenate([slab(row + 3 + r)[LEV:] for r in range(4)], axis=1)
        back = scale * dot(head_turned, cot)
        v = sigma * (1.0 + pre * (1.0 - sigma)) * back
        left, right = neighbours(v)
        for b, u in enumerate((right, v, left)):
            d3[b * MIX : (b + 1) * MIX, cut(row, 4)] = u.astype(BF)
        lo, hi = max(row, 2), min(row + 4, 10)
        dout[:, cut(lo - 2, hi - lo)] = (pre * sigma)[:, cut(lo - row, hi - lo)].astype(BF)

    copies[4].wait()
    for row in (0, 5):
        back = sum(
            dot(dt[:, a * 3 * MIX : (a + 1) * 3 * MIX], d3[:, cut(row + 2 - a, 5)])
            for a in range(3)
        )
        v = jnp.where(inside(row - 1, 5), mslope[:, cut(row + 2, 5)] * back, 0.0)
        left, right = neighbours(v)
        for b, u in enumerate((right, v, left)):
            e3[b * MIX : (b + 1) * MIX, cut(row, 5)] = u.astype(BF)

    copies[5].wait()
    for row in (0, 4):
        back = sum(
            dot(gt[:, a * 3 * MIX : (a + 1) * 3 * MIX], e3[:, cut(row + 2 - a, 4)])
            for a in range(3)
        )
        jdelta[:, cut(row, 4)] = (jslope[:, cut(row, 4)] * back).astype(BF)

    def put(rows, column, value):
        value = value.astype(BF)
        width = value.shape[1]
        done = 0
        while done < width:
            group, offset = divmod(column + done, WIDE)
            take = min(width - done, WIDE - offset)
            along = chip if group < 4 else depth
            slot = 4 * lax.rem(core + group // 4, 2) + lax.rem(group % 4 + 4 - along, 4)
            out[slot, rows : rows + value.shape[0], offset : offset + take] = value[
                :, done : done + take
            ]
            done += take

    def stacked(delta):
        def zero(rows):
            return jnp.zeros((delta.shape[0], rows * COLS), BF)

        return jnp.concatenate(
            [
                jnp.concatenate([delta, zero(2)], axis=1),
                jnp.concatenate([zero(1), delta, zero(1)], axis=1),
                jnp.concatenate([zero(2), delta], axis=1),
            ],
            axis=0,
        )

    q = pl.ds(pl.multiple_of(segment * OQ, OQ), OQ)
    qd = pl.ds(pl.multiple_of(MIX + segment * OQ, OQ), OQ)
    qm = pl.ds(pl.multiple_of(TERR + segment * MQ, 32), MQ)
    d_own = stacked(d3[qd, cut(2, ROWS)])
    e_own = stacked(e3[qd, cut(1, ROWS)])
    h_own = stacked(jdelta[qm, :])
    for b in range(3):
        part = dot_nt(e_own, j3[b * JOINT : (b + 1) * JOINT, cut(3, ROWS + 2)])
        for a in range(3):
            put(0, (3 * a + b) * JOINT, part[a * OQ : (a + 1) * OQ])
    column = 9 * JOINT
    part = dot_nt(d_own, m3[:, cut(2, ROWS + 2)])
    for a in range(3):
        put(0, column + a * 3 * MIX, part[a * OQ : (a + 1) * OQ])
    column += 9 * MIX
    part = dot_nt(h_own, x3[:, cut(4, ROWS + 2)])
    for a in range(3):
        h = part[a * MQ : (a + 1) * MQ]
        put(0, column + a * 3 * LEV, h[:64])
        spare = column + 9 * LEV
        for c in range(3):
            at = a * 3 * LEV + c * LEV
            piece = h[64:, c * LEV : (c + 1) * LEV]
            if at < 640:
                put(0, spare + at, piece)
            else:
                put(32, spare + at - 640, piece)
    put(32, column + 9 * LEV + 512, jnp.zeros((32, 128), F32))
    column += 9 * LEV + 640
    g = dot_nt(jdelta[q, :], p9[:, cut(4, ROWS)])
    head = scale * dot_nt(
        dout[q, :], jnp.concatenate([eight[r, LEV:] for r in range(ROWS)], axis=1)
    )
    tail = 8 * WIDE - column
    put(0, column, jnp.concatenate([g, head, jnp.zeros((OQ, tail - 10 * SLAB), F32)], axis=1))
    keep[...] = out[:4]
    send[...] = out[4:]


def main(place, above, eight, below, head_weight, *weights):
    smem = pl.BlockSpec(memory_space=pltpu.SMEM)
    vmem = pl.BlockSpec(memory_space=pltpu.VMEM)
    hbm = pl.BlockSpec(memory_space=pl.ANY)
    return pl.pallas_call(
        main_kernel,
        out_shape=(jax.ShapeDtypeStruct((4, OQ, WIDE), BF),) * 2,
        in_specs=[smem] + [vmem] * 4 + [hbm] * len(weights),
        out_specs=(vmem, vmem),
        scratch_shapes=[
            pltpu.VMEM((8, OQ, WIDE), BF),
            *[pltpu.VMEM(w.shape, BF) for w in weights],
            pltpu.SemaphoreType.DMA((len(weights),)),
            pltpu.VMEM((3 * LEV, (ROWS + 2 * HALO) * COLS), BF),
            pltpu.VMEM((9 * SLAB, (ROWS + 8) * COLS), BF),
            pltpu.VMEM((3 * JOINT, (ROWS + 8) * COLS), BF),
            pltpu.VMEM((JOINT, ROWS * COLS), F32),
            pltpu.VMEM((JOINT, ROWS * COLS), BF),
            pltpu.VMEM((3 * MIX, (ROWS + 6) * COLS), BF),
            pltpu.VMEM((MIX, (ROWS + 6) * COLS), F32),
            pltpu.VMEM((MIX, ROWS * COLS), BF),
            pltpu.VMEM((3 * MIX, (ROWS + 4) * COLS), BF),
            pltpu.VMEM((3 * MIX, (ROWS + 2) * COLS), BF),
        ],
        compiler_params=params(46),
        cost_estimate=pl.CostEstimate(
            flops=15_000_000_000, bytes_accessed=12_000_000, transcendentals=3_000_000
        ),
        name="sections",
    )(place, above, eight, below, head_weight, *weights)


def split_kernel(keep, came, own, next1, next2, next3):
    own[...] = keep[0].astype(F32) + came[0].astype(F32)
    for j, to in enumerate((next1, next2, next3), 1):
        to[...] = (keep[j].astype(F32) + came[j].astype(F32)).astype(BF)


def total_kernel(own, one, two, three, out):
    out[...] = (
        (own[...].astype(F32) + two[...].astype(F32))
        + (one[...].astype(F32) + three[...].astype(F32))
    ).astype(BF)


def stack_kernel(own, one, two, three, out):
    for j, v in enumerate((own, one, two, three)):
        out[j] = v[...]


def small(kernel, out_shape, *operands):
    return pl.pallas_call(
        kernel, out_shape=out_shape, compiler_params=params(16), name=kernel.__name__[:-7]
    )(*operands)


def moved(v, where):
    pairs = []
    for source in range(128):
        at = (source // 32, source // 8 % 4, source // 2 % 4, source % 2)
        to = where(*at)
        if to is not None:
            pairs.append((source, to[0] * 32 + to[1] * 8 + to[2] * 2 + to[3]))
    return lax.ppermute(v, ("dp", "segment", "space"), pairs)


DP, SEGMENT, CHIP = 0, 1, 2


def along(v, axes, by):
    def where(*at):
        to = list(at)
        to[axes[at[3]]] = (to[axes[at[3]]] + by) % 4
        return to

    return moved(v, where)


def to_partner(v):
    return moved(v, lambda z, x, y, c: (z, x, y, 1 - c))


STEPS = (0, -1, 1, -2)


def summed_everywhere(keep, send):
    piece = jax.ShapeDtypeStruct((OQ, WIDE), BF)
    wide = jax.ShapeDtypeStruct((OQ, WIDE), F32)
    turns = (1, 2, 3)
    own, *parts = small(split_kernel, (wide, piece, piece, piece), keep, to_partner(send))
    own = small(total_kernel, piece, own, *[along(p, (CHIP, DP), j) for p, j in zip(parts, turns)])
    own = small(total_kernel, piece, own, *[along(own, (DP, CHIP), j) for j in turns])
    four = jax.ShapeDtypeStruct((4, OQ, WIDE), BF)
    block = small(stack_kernel, four, own, *[along(own, (CHIP, SEGMENT), j) for j in turns])
    mine = (block,) + tuple(along(block, (SEGMENT, DP), -step) for step in STEPS[1:])
    return mine + tuple(to_partner(v) for v in mine)


def finish_kernel(place, *refs):
    blocks, (lw, pw, mw_hbm, tw_hbm) = refs[:8], refs[8:12]
    patch, lift, head, terrain, meso, merging, decoder = refs[12:19]
    mw, tw, stage, wide_m, wide_t, ht, gt, sems = refs[19:]
    reads = [
        pltpu.make_async_copy(mw_hbm, mw, sems.at[0]),
        pltpu.make_async_copy(tw_hbm, tw, sems.at[1]),
    ]
    for copy in reads:
        copy.start()
    segment, chip, core, depth = place[0], place[1] // 2, place[1] % 2, place[2]
    for i, block in enumerate(blocks):
        kind = core if i < 4 else 1 - core
        for j in range(4):
            along_segment = jnp.where(kind == 0, STEPS[i % 4], -j)
            group = jnp.where(
                kind == 0, lax.rem(chip - j + 4, 4), 4 + lax.rem(depth + STEPS[i % 4] + 4, 4)
            )
            row = lax.rem(segment + along_segment + 4, 4) * OQ
            stage[
                pl.ds(pl.multiple_of(row, OQ), OQ), pl.ds(pl.multiple_of(group * WIDE, WIDE), WIDE)
            ] = block[j].astype(F32)
    column = 9 * JOINT + 9 * MIX
    writes = [
        pltpu.make_async_copy(stage.at[:, : 9 * JOINT], merging, sems.at[2]),
        pltpu.make_async_copy(stage.at[:, 9 * JOINT : column], decoder, sems.at[3]),
    ]
    for copy in writes:
        copy.start()
    for seg in range(4):
        lo = seg * OQ
        at = seg * MQ
        ht[at : at + 64, :] = stage[lo : lo + OQ, column : column + 9 * LEV].astype(BF)
        spare = column + 9 * LEV
        ht[at + 64 : at + MQ, :640] = stage[lo : lo + 32, spare : spare + 640].astype(BF)
        ht[at + 64 : at + MQ, 640:] = stage[lo + 32 : lo + OQ, spare : spare + 512].astype(BF)
        gt[lo : lo + OQ, :] = stage[lo : lo + OQ, spare + 640 : spare + 896]
    for a in range(3):
        for tap in range(3 * a, 3 * a + 3):
            wide_m[:, tap * MESO : (tap + 1) * MESO] = dot_nt(
                ht[:, tap * LEV : (tap + 1) * LEV], lw[...]
            )
        part = slice(3 * a * MESO, 3 * (a + 1) * MESO)
        writes.append(pltpu.make_async_copy(wide_m.at[:, part], meso.at[:, part], sems.at[4 + a]))
        writes[-1].start()
    pw16 = sixteen(pw[...], 0).astype(BF)
    g = gt[...]
    for tap in range(9):
        wide_t[:, tap * TERR : (tap + 1) * TERR] = dot(
            g[:, tap * SLAB : (tap + 1) * SLAB].astype(BF), pw16
        )
    writes.append(pltpu.make_async_copy(wide_t, terrain, sems.at[7]))
    writes[-1].start()
    turned = g.T
    head[...] = turned[9 * SLAB + 8 : 9 * SLAB + 11, :]
    reads[1].wait()
    patch[...] = sum(
        dot(
            turned[tap * SLAB : (tap + 1) * SLAB, :].astype(BF),
            tw[:, tap * TERR : (tap + 1) * TERR],
        )
        for tap in range(9)
    )[:8]
    turned = ht[...].astype(F32).T.astype(BF)
    reads[0].wait()
    lift[...] = sum(
        dot(turned[tap * LEV : (tap + 1) * LEV, :], mw[:, tap * MESO : (tap + 1) * MESO])
        for tap in range(9)
    ).T
    for copy in writes:
        copy.wait()


def finish(place, blocks, lift_weight, patch_turned, meso_weight, terrain_weight):
    smem = pl.BlockSpec(memory_space=pltpu.SMEM)
    vmem = pl.BlockSpec(memory_space=pltpu.VMEM)
    hbm = pl.BlockSpec(memory_space=pl.ANY)
    patch, lift, head, terrain, meso, merging, decoder = pl.pallas_call(
        finish_kernel,
        out_shape=(
            jax.ShapeDtypeStruct((8, TERR), F32),
            jax.ShapeDtypeStruct((MESO, LEV), F32),
            jax.ShapeDtypeStruct((3, MIX), F32),
            jax.ShapeDtypeStruct((TERR, 9 * TERR), F32),
            jax.ShapeDtypeStruct((MESO, 9 * MESO), F32),
            jax.ShapeDtypeStruct((MIX, 9 * JOINT), F32),
            jax.ShapeDtypeStruct((MIX, 9 * MIX), F32),
        ),
        in_specs=[smem] + [vmem] * 10 + [hbm] * 2,
        out_specs=(vmem,) * 3 + (hbm,) * 4,
        scratch_shapes=[
            pltpu.VMEM((MESO, 9 * MESO), BF),
            pltpu.VMEM((TERR, 9 * TERR), BF),
            pltpu.VMEM((MIX, 8 * WIDE), F32),
            pltpu.VMEM((MESO, 9 * MESO), F32),
            pltpu.VMEM((TERR, 9 * TERR), F32),
            pltpu.VMEM((MESO, 9 * LEV), BF),
            pltpu.VMEM((MIX, 256), F32),
            pltpu.SemaphoreType.DMA((8,)),
        ],
        compiler_params=params(40),
        name="finish",
    )(place, *blocks, lift_weight, patch_turned, meso_weight, terrain_weight)
    return patch.T, terrain, lift, meso, merging, decoder, head


def packed(terrain_in, meso_in, wind_cot):
    samples, rows = meso_in.shape[0], meso_in.shape[3]
    source = lax.broadcasted_iota(jnp.int32, (2 * COLS, 2 * COLS), 0)
    target = lax.broadcasted_iota(jnp.int32, (2 * COLS, 2 * COLS), 1)
    pick = (source == 2 * (target % COLS) + target // COLS).astype(BF)
    split = dot(terrain_in.reshape(samples * 4 * rows, 2 * COLS), pick).astype(BF)
    patches = (
        split.reshape(samples, 2, rows, 2, 2, COLS)
        .transpose(0, 2, 1, 3, 4, 5)
        .reshape(samples, rows, 8, COLS)
    )
    levels = meso_in.reshape(samples, LEV, rows, COLS).transpose(0, 2, 1, 3)
    cot = wind_cot.transpose(0, 2, 1, 3)
    rest = jnp.zeros((samples, rows, PACK - LEV - 11, COLS), BF)
    return jnp.concatenate([levels, patches, cot, rest], axis=2)


def to_chip(v, by):
    return moved(v, lambda z, x, y, c: (z, x, y + by, c) if 0 <= y + by < 4 else None)


def local(
    terrain_in,
    meso_in,
    wind_cot,
    patch_weight,
    terrain_weight,
    lift_weight,
    meso_weight,
    merging_weight,
    decoder_weight,
    head_weight,
):
    own = packed(terrain_in, meso_in, wind_cot)
    place = jnp.stack([lax.axis_index(a) for a in ("segment", "space", "dp")]).astype(jnp.int32)
    eight, first, last = chip_rows(place, own, to_partner(own))
    above, below = to_chip(last, 1), to_chip(first, -1)
    patch_turned = patch_weight.T
    wm, wt, gt, dt = prep(
        meso_weight, lift_weight, terrain_weight, patch_turned, merging_weight, decoder_weight
    )
    keep, send = main(
        place, above, eight, below, head_weight, wm, wt, merging_weight, decoder_weight, dt, gt
    )
    blocks = summed_everywhere(keep, send)
    return finish(place, blocks, lift_weight, patch_turned, meso_weight, terrain_weight)


def solution(mesh):
    placed = (
        P("dp", None, "space", None),
        P("dp", None, None, "space", None),
        P("dp", None, "space", None),
        P(),
        P(),
        P(),
        P(),
        P(),
        P(),
        P(),
    )
    return jax.shard_map(
        local,
        mesh=mesh,
        in_specs=placed,
        out_specs=(P(), P(), P(), P(), P(), P(), P()),
        check_vma=False,
    )
```

```python
import functools
import math

import jax
import jax.numpy as jnp
from jax import lax
from jax.experimental import pallas as pl
from jax.experimental.pallas import tpu as pltpu
from jax.sharding import PartitionSpec as P

BF = jnp.bfloat16
F32 = jnp.float32
TERR, MESO, MIX = 256, 384, 256
JOINT = TERR + MESO
LEV = 128
SLAB = 16
PACK = LEV + SLAB
ROWS, COLS = 8, 128
HALO = 5
OQ, MQ = MIX // 4, MESO // 4
WIDE = 1280
NT = (((1,), (1,)), ((), ()))


def dot(a, b):
    return jnp.dot(a, b, preferred_element_type=F32)


def dot_nt(a, b):
    return lax.dot_general(a, b, NT, preferred_element_type=F32)


def params(mib):
    return pltpu.CompilerParams(vmem_limit_bytes=mib * 1024 * 1024)


def sixteen(v, above):
    rows, width = v.shape
    parts = [v.astype(F32)]
    if above:
        parts.insert(0, jnp.zeros((above, width), F32))
    if above + rows < SLAB:
        parts.append(jnp.zeros((SLAB - above - rows, width), F32))
    return jnp.concatenate(parts, axis=0)


def small_kernel(lw, pw, hw, lw_out, pw_out, head_turned):
    lw_out[...] = lw[...]
    pw_out[...] = sixteen(pw[...], 0).astype(BF)
    head_turned[...] = sixteen(hw[...], 8).T.astype(BF)


def small_weights(lift_weight, patch_turned, head_weight):
    return pl.pallas_call(
        small_kernel,
        out_shape=(
            jax.ShapeDtypeStruct((MESO, LEV), BF),
            jax.ShapeDtypeStruct((SLAB, TERR), BF),
            jax.ShapeDtypeStruct((MIX, SLAB), BF),
        ),
        compiler_params=params(16),
        cost_estimate=pl.CostEstimate(flops=0, bytes_accessed=4_000_000, transcendentals=0),
        name="small_weights",
    )(lift_weight, patch_turned, head_weight)


def rows_kernel(place, own, partner, eight, first, last):
    core = place[1] % 2
    for c in range(2):

        @pl.when(core == c)
        def _(c=c):
            halves = (own, partner) if c == 0 else (partner, own)
            for r in range(ROWS):
                v = halves[r // 4][c, r % 4]
                eight[r] = v
                if r < HALO:
                    first[r] = v
                if r >= ROWS - HALO:
                    last[r - (ROWS - HALO)] = v


def chip_rows(place, own, partner):
    smem = pl.BlockSpec(memory_space=pltpu.SMEM)
    vmem = pl.BlockSpec(memory_space=pltpu.VMEM)
    return pl.pallas_call(
        rows_kernel,
        out_shape=tuple(
            jax.ShapeDtypeStruct((n, PACK, COLS), BF) for n in (ROWS, HALO, HALO)
        ),
        in_specs=[smem, vmem, vmem],
        out_specs=(vmem,) * 3,
        compiler_params=params(16),
        name="rows",
    )(place, own, partner)


def neighbours(v):
    width = v.shape[1]
    lane = lax.broadcasted_iota(jnp.int32, (1, width), 1) % COLS
    left, right = [], []
    for r in range(width // COLS):
        piece = v[:, r * COLS : (r + 1) * COLS]
        left.append(pltpu.roll(piece, 1, 1))
        right.append(pltpu.roll(piece, COLS - 1, 1))
    left = jnp.where(lane == 0, 0.0, jnp.concatenate(left, axis=1))
    right = jnp.where(lane == COLS - 1, 0.0, jnp.concatenate(right, axis=1))
    return left, right


def logistic(v):
    return 0.5 * (1.0 + jnp.tanh(0.5 * v))


def main_kernel(place, above, eight, below, lw, pw16, head_turned, *refs):
    n_w = 4
    weights_hbm, keep, send, out = refs[:n_w], *refs[n_w : n_w + 3]
    mw, tw, gw, dw = weights = refs[n_w + 3 : 2 * n_w + 3]
    sems, wm, wt, dt, gt = refs[2 * n_w + 3 : 2 * n_w + 8]
    x3, p9, j3, jslope, jdelta, m3, mslope, dout, d3, e3 = refs[2 * n_w + 8 :]
    copies = [
        pltpu.make_async_copy(u, v, sems.at[i]) for i, (u, v) in enumerate(zip(weights_hbm, weights))
    ]
    for copy in copies:
        copy.start()
    segment, depth = place[0], place[2]
    chip, core = place[1] // 2, place[1] % 2
    first_row = chip * ROWS

    def cut(row, rows):
        return slice(row * COLS, (row + rows) * COLS)

    def inside(row, rows):
        at = lax.broadcasted_iota(jnp.int32, (1, rows * COLS), 1) // COLS + row + first_row
        return jnp.logical_and(at >= 0, at < 4 * ROWS)

    def slab(r):
        for ref, rows in ((above, HALO), (eight, ROWS), (below, HALO)):
            if r < rows:
                return ref[r]
            r -= rows

    n_in, n_join = ROWS + 2 * HALO, ROWS + 8

    for r in range(n_in):
        v = slab(r).astype(F32)
        left, right = neighbours(v)
        for b, u in enumerate((left, v, right)):
            u = u.astype(BF)
            x3[b * LEV : (b + 1) * LEV, cut(r, 1)] = u[:LEV]
            for a in range(3):
                if a <= r < n_join + a:
                    tap = 3 * a + b
                    p9[tap * SLAB : (tap + 1) * SLAB, cut(r - a, 1)] = u[LEV:]

    copies[0].wait()
    for tap in range(9):
        wm[:, tap * LEV : (tap + 1) * LEV] = dot(
            mw[:, tap * MESO : (tap + 1) * MESO], lw[...]
        ).astype(BF)
    copies[1].wait()
    wt[...] = jnp.concatenate(
        [dot_nt(tw[:, tap * TERR : (tap + 1) * TERR], pw16[...]).astype(BF) for tap in range(9)], axis=1
    )

    for row in (0, 4, 8, 12):
        pre_t = dot(wt[...], p9[:, cut(row, 4)])
        pre_m = sum(
            dot(wm[:, a * 3 * LEV : (a + 1) * 3 * LEV], x3[:, cut(row + a, 4)]) for a in range(3)
        )
        for at, pre in ((0, pre_t), (TERR, pre_m)):
            size = pre.shape[0]
            sigma = logistic(pre)
            v = jnp.where(inside(row - 4, 4), pre * sigma, 0.0)
            left, right = neighbours(v)
            for b, u in enumerate((left, v, right)):
                j3[b * JOINT + at : b * JOINT + at + size, cut(row, 4)] = u.astype(BF)
            if row in (4, 8):
                jslope[at : at + size, cut(row - 4, 4)] = sigma * (1.0 + pre * (1.0 - sigma))

    copies[2].wait()
    copies[3].wait()
    for tap in range(9):
        gt[:, tap * MIX : (tap + 1) * MIX] = gw[:, tap * JOINT : (tap + 1) * JOINT].T
        dt[:, tap * MIX : (tap + 1) * MIX] = dw[:, tap * MIX : (tap + 1) * MIX].T

    for row, rows in ((0, 4), (4, 5), (9, 5)):
        pre = sum(
            dot(gw[:, a * 3 * JOINT : (a + 1) * 3 * JOINT], j3[:, cut(row + a, rows)])
            for a in range(3)
        )
        sigma = logistic(pre)
        v = jnp.where(inside(row - 3, rows), pre * sigma, 0.0)
        left, right = neighbours(v)
        for b, u in enumerate((left, v, right)):
            m3[b * MIX : (b + 1) * MIX, cut(row, rows)] = u.astype(BF)
        mslope[:, cut(row, rows)] = sigma * (1.0 + pre * (1.0 - sigma))

    scale = 1.0 / math.sqrt(8 * 32 * 128)

    for row in (0, 4, 8):
        pre = sum(
            dot(dw[:, a * 3 * MIX : (a + 1) * 3 * MIX], m3[:, cut(row + a, 4)]) for a in range(3)
        )
        sigma = logistic(pre)
        cot = jnp.concatenate([slab(row + 3 + r)[LEV:] for r in range(4)], axis=1)
        back = scale * dot(head_turned[...], cot)
        v = sigma * (1.0 + pre * (1.0 - sigma)) * back
        left, right = neighbours(v)
        for b, u in enumerate((right, v, left)):
            d3[b * MIX : (b + 1) * MIX, cut(row, 4)] = u.astype(BF)
        lo, hi = max(row, 2), min(row + 4, 10)
        dout[:, cut(lo - 2, hi - lo)] = (pre * sigma)[:, cut(lo - row, hi - lo)].astype(BF)

    for row in (0, 5):
        back = sum(
            dot(dt[:, a * 3 * MIX : (a + 1) * 3 * MIX], d3[:, cut(row + 2 - a, 5)])
            for a in range(3)
        )
        v = jnp.where(inside(row - 1, 5), mslope[:, cut(row + 2, 5)] * back, 0.0)
        left, right = neighbours(v)
        for b, u in enumerate((right, v, left)):
            e3[b * MIX : (b + 1) * MIX, cut(row, 5)] = u.astype(BF)

    for row in (0, 4):
        back = sum(
            dot(gt[:, a * 3 * MIX : (a + 1) * 3 * MIX], e3[:, cut(row + 2 - a, 4)])
            for a in range(3)
        )
        jdelta[:, cut(row, 4)] = (jslope[:, cut(row, 4)] * back).astype(BF)

    def put(rows, column, value):
        value = value.astype(BF)
        width = value.shape[1]
        done = 0
        while done < width:
            group, offset = divmod(column + done, WIDE)
            take = min(width - done, WIDE - offset)
            along = chip if group < 4 else depth
            slot = 4 * lax.rem(core + group // 4, 2) + lax.rem(group % 4 + 4 - along, 4)
            out[slot, rows : rows + value.shape[0], offset : offset + take] = value[
                :, done : done + take
            ]
            done += take

    def stacked(delta):
        def zero(rows):
            return jnp.zeros((delta.shape[0], rows * COLS), BF)

        return jnp.concatenate(
            [
                jnp.concatenate([delta, zero(2)], axis=1),
                jnp.concatenate([zero(1), delta, zero(1)], axis=1),
                jnp.concatenate([zero(2), delta], axis=1),
            ],
            axis=0,
        )

    q = pl.ds(pl.multiple_of(segment * OQ, OQ), OQ)
    qd = pl.ds(pl.multiple_of(MIX + segment * OQ, OQ), OQ)
    qm = pl.ds(pl.multiple_of(TERR + segment * MQ, 32), MQ)
    d_own = stacked(d3[qd, cut(2, ROWS)])
    e_own = stacked(e3[qd, cut(1, ROWS)])
    h_own = stacked(jdelta[qm, :])
    for b in range(3):
        part = dot_nt(e_own, j3[b * JOINT : (b + 1) * JOINT, cut(3, ROWS + 2)])
        for a in range(3):
            put(0, (3 * a + b) * JOINT, part[a * OQ : (a + 1) * OQ])
    column = 9 * JOINT
    part = dot_nt(d_own, m3[:, cut(2, ROWS + 2)])
    for a in range(3):
        put(0, column + a * 3 * MIX, part[a * OQ : (a + 1) * OQ])
    column += 9 * MIX
    part = dot_nt(h_own, x3[:, cut(4, ROWS + 2)])
    for a in range(3):
        h = part[a * MQ : (a + 1) * MQ]
        put(0, column + a * 3 * LEV, h[:64])
        spare = column + 9 * LEV
        for c in range(3):
            at = a * 3 * LEV + c * LEV
            piece = h[64:, c * LEV : (c + 1) * LEV]
            if at < 640:
                put(0, spare + at, piece)
            else:
                put(32, spare + at - 640, piece)
    put(32, column + 9 * LEV + 512, jnp.zeros((32, 128), F32))
    column += 9 * LEV + 640
    g = dot_nt(jdelta[q, :], p9[:, cut(4, ROWS)])
    head = scale * dot_nt(
        dout[q, :], jnp.concatenate([eight[r, LEV:] for r in range(ROWS)], axis=1)
    )
    tail = 8 * WIDE - column
    put(0, column, jnp.concatenate([g, head, jnp.zeros((OQ, tail - 10 * SLAB), F32)], axis=1))
    keep[...] = out[:4]
    send[...] = out[4:]


def main(place, above, eight, below, small_ones, *weights):
    smem = pl.BlockSpec(memory_space=pltpu.SMEM)
    vmem = pl.BlockSpec(memory_space=pltpu.VMEM)
    hbm = pl.BlockSpec(memory_space=pltpu.HBM)
    return pl.pallas_call(
        main_kernel,
        out_shape=(jax.ShapeDtypeStruct((4, OQ, WIDE), BF),) * 2,
        in_specs=[smem] + [vmem] * 6 + [hbm] * len(weights),
        out_specs=(vmem, vmem),
        scratch_shapes=[
            pltpu.VMEM((8, OQ, WIDE), BF),
            *[pltpu.VMEM(w.shape, BF) for w in weights],
            pltpu.SemaphoreType.DMA((len(weights),)),
            pltpu.VMEM((MESO, 9 * LEV), BF),
            pltpu.VMEM((TERR, 9 * SLAB), BF),
            pltpu.VMEM((MIX, 9 * MIX), BF),
            pltpu.VMEM((JOINT, 9 * MIX), BF),
            pltpu.VMEM((3 * LEV, (ROWS + 2 * HALO) * COLS), BF),
            pltpu.VMEM((9 * SLAB, (ROWS + 8) * COLS), BF),
            pltpu.VMEM((3 * JOINT, (ROWS + 8) * COLS), BF),
            pltpu.VMEM((JOINT, ROWS * COLS), F32),
            pltpu.VMEM((JOINT, ROWS * COLS), BF),
            pltpu.VMEM((3 * MIX, (ROWS + 6) * COLS), BF),
            pltpu.VMEM((MIX, (ROWS + 6) * COLS), F32),
            pltpu.VMEM((MIX, ROWS * COLS), BF),
            pltpu.VMEM((3 * MIX, (ROWS + 4) * COLS), BF),
            pltpu.VMEM((3 * MIX, (ROWS + 2) * COLS), BF),
        ],
        compiler_params=params(51),
        cost_estimate=pl.CostEstimate(
            flops=15_000_000_000, bytes_accessed=12_000_000, transcendentals=3_000_000
        ),
        name="sections",
    )(place, above, eight, below, *small_ones, *weights)


def split_kernel(keep, came, own, next1, next2, next3):
    own[...] = keep[0].astype(F32) + came[0].astype(F32)
    for j, to in enumerate((next1, next2, next3), 1):
        to[...] = (keep[j].astype(F32) + came[j].astype(F32)).astype(BF)


def total_kernel(own, one, two, three, out):
    parts = [v[...].astype(F32) for v in (own, one, two, three)]
    out[...] = sum(parts[1:], parts[0]).astype(BF)


def pair_kernel(own, other, out):
    out[...] = (own[...].astype(F32) + other[...].astype(F32)).astype(BF)


def stack_kernel(own, one, two, three, out):
    for j, v in enumerate((own, one, two, three)):
        out[j] = v[...]


def small(kernel, out_shape, *operands):
    return pl.pallas_call(
        kernel, out_shape=out_shape, compiler_params=params(16), name=kernel.__name__[:-7]
    )(*operands)


def moved(v, where):
    pairs = []
    for source in range(128):
        at = (source // 32, source // 8 % 4, source // 2 % 4, source % 2)
        to = where(*at)
        if to is not None:
            pairs.append((source, to[0] * 32 + to[1] * 8 + to[2] * 2 + to[3]))
    return lax.ppermute(v, ("dp", "segment", "space"), pairs)


DP, SEGMENT, CHIP = 0, 1, 2


def along(v, axes, by):
    def where(*at):
        to = list(at)
        to[axes[at[3]]] = (to[axes[at[3]]] + by) % 4
        return to

    return moved(v, where)


def across(v, axes, bits):
    def where(*at):
        to = list(at)
        to[axes[at[3]]] ^= bits
        return to

    return moved(v, where)


def to_partner(v):
    return moved(v, lambda z, x, y, c: (z, x, y, 1 - c))


STEPS = (0, -1, 1, -2)


def summed_everywhere(keep, send):
    piece = jax.ShapeDtypeStruct((OQ, WIDE), BF)
    wide = jax.ShapeDtypeStruct((OQ, WIDE), F32)
    turns = (1, 2, 3)
    own, *parts = small(split_kernel, (wide, piece, piece, piece), keep, to_partner(send))
    own = small(total_kernel, piece, own, *[along(p, (CHIP, DP), j) for p, j in zip(parts, turns)])
    for bits in (1, 3):
        own = small(pair_kernel, piece, own, across(own, (DP, CHIP), bits))
    four = jax.ShapeDtypeStruct((4, OQ, WIDE), BF)
    block = small(stack_kernel, four, own, *[along(own, (CHIP, SEGMENT), j) for j in turns])
    mine = (block,) + tuple(along(block, (SEGMENT, DP), -step) for step in STEPS[1:])
    return mine + tuple(to_partner(v) for v in mine)


def origin(place, i, j, theirs):
    segment, core, depth = place[0], place[1] % 2, place[2]
    chip = place[1] // 2
    kind = 1 - core if theirs else core
    group = jnp.where(
        kind == 0, lax.rem(chip - j + 4, 4), 4 + lax.rem(depth + STEPS[i] + 4, 4)
    )
    row = lax.rem(segment + jnp.where(kind == 0, STEPS[i], -j) + 4, 4)
    return group, row


def write_out(place, blocks, steps, merging, decoder, stage, sems):
    def pieces(k, j):
        group, row = origin(place, steps[k // 2], j, k % 2)
        slot = stage.at[4 * k + j]
        sem = sems.at[4 * k + j]
        rows = pl.ds(pl.multiple_of(row * OQ, OQ), OQ)
        left = 9 * JOINT - 4 * WIDE
        yield group < 4, [
            (slot, merging.at[rows, pl.ds(pl.multiple_of(group * WIDE, WIDE), WIDE)], sem)
        ]
        yield group == 4, [
            (slot.at[:, :left], merging.at[rows, 4 * WIDE :], sem),
            (slot.at[:, left:], decoder.at[rows, : WIDE - left], sems.at[4 * len(blocks)]),
        ]
        yield group == 5, [(slot, decoder.at[rows, WIDE - left : 2 * WIDE - left], sem)]
        last = 9 * MIX - (2 * WIDE - left)
        yield group == 6, [(slot.at[:, :last], decoder.at[rows, 2 * WIDE - left :], sem)]

    def each(do):
        for k in range(len(blocks)):
            for j in range(4):
                for when, copies in pieces(k, j):

                    @pl.when(when)
                    def _(copies=copies):
                        for copy in copies:
                            do(pltpu.make_async_copy(*copy))

    for k, block in enumerate(blocks):
        stage[4 * k : 4 * k + 4] = block[...].astype(F32)
    each(lambda copy: copy.start())
    return lambda: each(lambda copy: copy.wait())


def early_kernel(step, n_old, place, *refs):
    blocks, (merging, decoder, stage, sems) = refs[n_old : n_old + 2], refs[n_old + 2 :]
    write_out(place, blocks, (step,), merging, decoder, stage, sems)()


def write_early(place, step, mine, theirs, old):
    smem = pl.BlockSpec(memory_space=pltpu.SMEM)
    vmem = pl.BlockSpec(memory_space=pltpu.VMEM)
    hbm = pl.BlockSpec(memory_space=pltpu.HBM)
    return pl.pallas_call(
        functools.partial(early_kernel, step, len(old)),
        out_shape=(
            jax.ShapeDtypeStruct((MIX, 9 * JOINT), F32),
            jax.ShapeDtypeStruct((MIX, 9 * MIX), F32),
        ),
        in_specs=[smem] + [hbm] * len(old) + [vmem] * 2,
        out_specs=(hbm, hbm),
        scratch_shapes=[pltpu.VMEM((8, OQ, WIDE), F32), pltpu.SemaphoreType.DMA((9,))],
        input_output_aliases={1 + i: i for i in range(len(old))},
        compiler_params=params(12),
        cost_estimate=pl.CostEstimate(flops=0, bytes_accessed=4_000_000, transcendentals=0),
        name="early",
    )(place, *old, mine, theirs)


def finish_kernel(place, *refs):
    blocks, (lw, pw16, mw_hbm, tw_hbm) = refs[2:10], refs[10:14]
    patch, lift, head, terrain, meso, merging, decoder = refs[14:21]
    mw, tw, stage, rest, wide_m, wide_t, ht, gt, sems, late_sems = refs[21:]
    reads = [
        pltpu.make_async_copy(mw_hbm, mw, sems.at[0]),
        pltpu.make_async_copy(tw_hbm, tw, sems.at[1]),
    ]
    for copy in reads:
        copy.start()
    late = [blocks[4 * theirs + i] for i in (1, 2) for theirs in (0, 1)]
    written = write_out(place, late, (1, 2), merging, decoder, stage, late_sems)
    for i in range(4):
        for theirs in range(2):
            for j in range(4):
                group, row = origin(place, i, j, theirs)

                @pl.when(group >= 6)
                def _(i=i, theirs=theirs, j=j, group=group, row=row):
                    rest[
                        pl.ds(pl.multiple_of(row * OQ, OQ), OQ),
                        pl.ds(pl.multiple_of((group - 6) * WIDE, WIDE), WIDE),
                    ] = blocks[4 * theirs + i][j]

    column = 9 * JOINT + 9 * MIX - 6 * WIDE
    writes = []
    for seg in range(4):
        lo = seg * OQ
        at = seg * MQ
        ht[at : at + 64, :] = rest[lo : lo + OQ, column : column + 9 * LEV]
        spare = column + 9 * LEV
        ht[at + 64 : at + MQ, :640] = rest[lo : lo + 32, spare : spare + 640]
        ht[at + 64 : at + MQ, 640:] = rest[lo + 32 : lo + OQ, spare : spare + 512]
        gt[lo : lo + OQ, :] = rest[lo : lo + OQ, spare + 640 : spare + 896].astype(F32)
    for a in range(3):
        for tap in range(3 * a, 3 * a + 3):
            wide_m[:, tap * MESO : (tap + 1) * MESO] = dot_nt(
                ht[:, tap * LEV : (tap + 1) * LEV], lw[...]
            )
        part = slice(3 * a * MESO, 3 * (a + 1) * MESO)
        writes.append(pltpu.make_async_copy(wide_m.at[:, part], meso.at[:, part], sems.at[4 + a]))
        writes[-1].start()
    g = gt[...]
    for tap in range(9):
        wide_t[:, tap * TERR : (tap + 1) * TERR] = dot(
            g[:, tap * SLAB : (tap + 1) * SLAB].astype(BF), pw16[...]
        )
    writes.append(pltpu.make_async_copy(wide_t, terrain, sems.at[7]))
    writes[-1].start()
    turned = g.T
    head[...] = turned[9 * SLAB + 8 : 9 * SLAB + 11, :]
    reads[1].wait()
    patch[...] = sum(
        dot(
            turned[tap * SLAB : (tap + 1) * SLAB, :].astype(BF),
            tw[:, tap * TERR : (tap + 1) * TERR],
        )
        for tap in range(9)
    )[:8]
    turned = ht[...].astype(F32).T.astype(BF)
    reads[0].wait()
    lift[...] = sum(
        dot(turned[tap * LEV : (tap + 1) * LEV, :], mw[:, tap * MESO : (tap + 1) * MESO])
        for tap in range(9)
    ).T
    for copy in writes:
        copy.wait()
    written()


def finish(place, old, blocks, lift_copy, patch_turned, meso_weight, terrain_weight):
    smem = pl.BlockSpec(memory_space=pltpu.SMEM)
    vmem = pl.BlockSpec(memory_space=pltpu.VMEM)
    hbm = pl.BlockSpec(memory_space=pltpu.HBM)
    patch, lift, head, terrain, meso, merging, decoder = pl.pallas_call(
        finish_kernel,
        out_shape=(
            jax.ShapeDtypeStruct((8, TERR), F32),
            jax.ShapeDtypeStruct((MESO, LEV), F32),
            jax.ShapeDtypeStruct((3, MIX), F32),
            jax.ShapeDtypeStruct((TERR, 9 * TERR), F32),
            jax.ShapeDtypeStruct((MESO, 9 * MESO), F32),
            jax.ShapeDtypeStruct((MIX, 9 * JOINT), F32),
            jax.ShapeDtypeStruct((MIX, 9 * MIX), F32),
        ),
        in_specs=[smem] + [hbm] * 2 + [vmem] * 10 + [hbm] * 2,
        out_specs=(vmem,) * 3 + (hbm,) * 4,
        scratch_shapes=[
            pltpu.VMEM((MESO, 9 * MESO), BF),
            pltpu.VMEM((TERR, 9 * TERR), BF),
            pltpu.VMEM((16, OQ, WIDE), F32),
            pltpu.VMEM((MIX, 2 * WIDE), BF),
            pltpu.VMEM((MESO, 9 * MESO), F32),
            pltpu.VMEM((TERR, 9 * TERR), F32),
            pltpu.VMEM((MESO, 9 * LEV), BF),
            pltpu.VMEM((MIX, 256), F32),
            pltpu.SemaphoreType.DMA((8,)),
            pltpu.SemaphoreType.DMA((17,)),
        ],
        input_output_aliases={1: 5, 2: 6},
        compiler_params=params(36),
        name="finish",
    )(place, *old, *blocks, lift_copy, patch_turned, meso_weight, terrain_weight)
    return patch.T, terrain, lift, meso, merging, decoder, head


def packed(terrain_in, meso_in, wind_cot):
    samples, rows = meso_in.shape[0], meso_in.shape[3]
    source = lax.broadcasted_iota(jnp.int32, (2 * COLS, 2 * COLS), 0)
    target = lax.broadcasted_iota(jnp.int32, (2 * COLS, 2 * COLS), 1)
    pick = (source == 2 * (target % COLS) + target // COLS).astype(BF)
    split = dot(terrain_in.reshape(samples * 4 * rows, 2 * COLS), pick).astype(BF)
    patches = (
        split.reshape(samples, 2, rows, 2, 2, COLS)
        .transpose(0, 2, 1, 3, 4, 5)
        .reshape(samples, rows, 8, COLS)
    )
    levels = meso_in.reshape(samples, LEV, rows, COLS).transpose(0, 2, 1, 3)
    cot = wind_cot.transpose(0, 2, 1, 3)
    rest = jnp.zeros((samples, rows, PACK - LEV - 11, COLS), BF)
    return jnp.concatenate([levels, patches, cot, rest], axis=2)


def to_chip(v, by):
    return moved(v, lambda z, x, y, c: (z, x, y + by, c) if 0 <= y + by < 4 else None)


def local(
    terrain_in,
    meso_in,
    wind_cot,
    patch_weight,
    terrain_weight,
    lift_weight,
    meso_weight,
    merging_weight,
    decoder_weight,
    head_weight,
):
    own = packed(terrain_in, meso_in, wind_cot)
    place = jnp.stack([lax.axis_index(a) for a in ("segment", "space", "dp")]).astype(jnp.int32)
    eight, first, last = chip_rows(place, own, to_partner(own))
    above, below = to_chip(last, 1), to_chip(first, -1)
    small_ones = small_weights(lift_weight, patch_weight.T, head_weight)
    keep, send = main(
        place,
        above,
        eight,
        below,
        small_ones,
        meso_weight,
        terrain_weight,
        merging_weight,
        decoder_weight,
    )
    blocks = summed_everywhere(keep, send)
    old = write_early(place, 0, blocks[0], blocks[4], ())
    old = write_early(place, 3, blocks[3], blocks[7], old)
    return finish(place, old, blocks, *small_ones[:2], meso_weight, terrain_weight)


def solution(mesh):
    placed = (
        P("dp", None, "space", None),
        P("dp", None, None, "space", None),
        P("dp", None, "space", None),
        P(),
        P(),
        P(),
        P(),
        P(),
        P(),
        P(),
    )
    return jax.shard_map(
        local,
        mesh=mesh,
        in_specs=placed,
        out_specs=(P(), P(), P(), P(), P(), P(), P()),
        check_vma=False,
    )
```

```python
import functools
import math

import jax
import jax.numpy as jnp
from jax import lax
from jax.experimental import pallas as pl
from jax.experimental.pallas import tpu as pltpu
from jax.sharding import PartitionSpec as P

BF = jnp.bfloat16
F32 = jnp.float32
TERR, MESO, MIX = 256, 384, 256
JOINT = TERR + MESO
LEV = 128
SLAB = 16
PACK = LEV + SLAB
ROWS, COLS = 8, 128
HALO = 5
OQ, MQ = MIX // 4, MESO // 4
WIDE = 1280
NT = (((1,), (1,)), ((), ()))


def dot(a, b):
    return jnp.dot(a, b, preferred_element_type=F32)


def dot_nt(a, b):
    return lax.dot_general(a, b, NT, preferred_element_type=F32)


def params(mib):
    return pltpu.CompilerParams(vmem_limit_bytes=mib * 1024 * 1024)


def sixteen(v, above):
    rows, width = v.shape
    parts = [v.astype(F32)]
    if above:
        parts.insert(0, jnp.zeros((above, width), F32))
    if above + rows < SLAB:
        parts.append(jnp.zeros((SLAB - above - rows, width), F32))
    return jnp.concatenate(parts, axis=0)


def small_kernel(lw, pw, hw, lw_out, pw_out, head_turned):
    lw_out[...] = lw[...]
    pw_out[...] = sixteen(pw[...], 0).astype(BF)
    head_turned[...] = sixteen(hw[...], 8).T.astype(BF)


def small_weights(lift_weight, patch_turned, head_weight):
    return pl.pallas_call(
        small_kernel,
        out_shape=(
            jax.ShapeDtypeStruct((MESO, LEV), BF),
            jax.ShapeDtypeStruct((SLAB, TERR), BF),
            jax.ShapeDtypeStruct((MIX, SLAB), BF),
        ),
        compiler_params=params(16),
        cost_estimate=pl.CostEstimate(flops=0, bytes_accessed=4_000_000, transcendentals=0),
        name="small_weights",
    )(lift_weight, patch_turned, head_weight)


def rows_kernel(place, own, partner, eight, first, last):
    core = place[1] % 2
    for c in range(2):

        @pl.when(core == c)
        def _(c=c):
            halves = (own, partner) if c == 0 else (partner, own)
            for r in range(ROWS):
                v = halves[r // 4][c, r % 4]
                eight[r] = v
                if r < HALO:
                    first[r] = v
                if r >= ROWS - HALO:
                    last[r - (ROWS - HALO)] = v


def chip_rows(place, own, partner):
    smem = pl.BlockSpec(memory_space=pltpu.SMEM)
    vmem = pl.BlockSpec(memory_space=pltpu.VMEM)
    return pl.pallas_call(
        rows_kernel,
        out_shape=tuple(
            jax.ShapeDtypeStruct((n, PACK, COLS), BF) for n in (ROWS, HALO, HALO)
        ),
        in_specs=[smem, vmem, vmem],
        out_specs=(vmem,) * 3,
        compiler_params=params(16),
        name="rows",
    )(place, own, partner)


def neighbours(v):
    width = v.shape[1]
    lane = lax.broadcasted_iota(jnp.int32, (1, width), 1) % COLS
    left, right = [], []
    for r in range(width // COLS):
        piece = v[:, r * COLS : (r + 1) * COLS]
        left.append(pltpu.roll(piece, 1, 1))
        right.append(pltpu.roll(piece, COLS - 1, 1))
    left = jnp.where(lane == 0, 0.0, jnp.concatenate(left, axis=1))
    right = jnp.where(lane == COLS - 1, 0.0, jnp.concatenate(right, axis=1))
    return left, right


def logistic(v):
    return 0.5 * (1.0 + jnp.tanh(0.5 * v))


def main_kernel(place, above, eight, below, lw, pw16, head_turned, *refs):
    n_w = 4
    weights_hbm, keep, send, out = refs[:n_w], *refs[n_w : n_w + 3]
    mw, tw, gw, dw = weights = refs[n_w + 3 : 2 * n_w + 3]
    sems, wm, wt, dt, gt = refs[2 * n_w + 3 : 2 * n_w + 8]
    x3, p9, j3, jslope, jdelta, m3, mslope, dout, d3, e3 = refs[2 * n_w + 8 :]
    copies = [
        pltpu.make_async_copy(u, v, sems.at[i]) for i, (u, v) in enumerate(zip(weights_hbm, weights))
    ]
    for copy in copies:
        copy.start()
    segment, depth = place[0], place[2]
    chip, core = place[1] // 2, place[1] % 2
    first_row = chip * ROWS

    def cut(row, rows):
        return slice(row * COLS, (row + rows) * COLS)

    def inside(row, rows):
        at = lax.broadcasted_iota(jnp.int32, (1, rows * COLS), 1) // COLS + row + first_row
        return jnp.logical_and(at >= 0, at < 4 * ROWS)

    def slab(r):
        for ref, rows in ((above, HALO), (eight, ROWS), (below, HALO)):
            if r < rows:
                return ref[r]
            r -= rows

    n_in, n_join = ROWS + 2 * HALO, ROWS + 8

    for r in range(n_in):
        v = slab(r).astype(F32)
        left, right = neighbours(v)
        for b, u in enumerate((left, v, right)):
            u = u.astype(BF)
            x3[b * LEV : (b + 1) * LEV, cut(r, 1)] = u[:LEV]
            for a in range(3):
                if a <= r < n_join + a:
                    tap = 3 * a + b
                    p9[tap * SLAB : (tap + 1) * SLAB, cut(r - a, 1)] = u[LEV:]

    copies[0].wait()
    for tap in range(9):
        wm[:, tap * LEV : (tap + 1) * LEV] = dot(
            mw[:, tap * MESO : (tap + 1) * MESO], lw[...]
        ).astype(BF)
    copies[1].wait()
    wt[...] = jnp.concatenate(
        [dot_nt(tw[:, tap * TERR : (tap + 1) * TERR], pw16[...]).astype(BF) for tap in range(9)], axis=1
    )

    for row in (0, 4, 8, 12):
        pre_t = dot(wt[...], p9[:, cut(row, 4)])
        pre_m = sum(
            dot(wm[:, a * 3 * LEV : (a + 1) * 3 * LEV], x3[:, cut(row + a, 4)]) for a in range(3)
        )
        for at, pre in ((0, pre_t), (TERR, pre_m)):
            size = pre.shape[0]
            sigma = logistic(pre)
            v = jnp.where(inside(row - 4, 4), pre * sigma, 0.0)
            left, right = neighbours(v)
            for b, u in enumerate((left, v, right)):
                j3[b * JOINT + at : b * JOINT + at + size, cut(row, 4)] = u.astype(BF)
            if row in (4, 8):
                jslope[at : at + size, cut(row - 4, 4)] = sigma * (1.0 + pre * (1.0 - sigma))

    copies[2].wait()
    copies[3].wait()
    for tap in range(9):
        gt[:, tap * MIX : (tap + 1) * MIX] = gw[:, tap * JOINT : (tap + 1) * JOINT].T
        dt[:, tap * MIX : (tap + 1) * MIX] = dw[:, tap * MIX : (tap + 1) * MIX].T

    for row, rows in ((0, 4), (4, 5), (9, 5)):
        pre = sum(
            dot(gw[:, a * 3 * JOINT : (a + 1) * 3 * JOINT], j3[:, cut(row + a, rows)])
            for a in range(3)
        )
        sigma = logistic(pre)
        v = jnp.where(inside(row - 3, rows), pre * sigma, 0.0)
        left, right = neighbours(v)
        for b, u in enumerate((left, v, right)):
            m3[b * MIX : (b + 1) * MIX, cut(row, rows)] = u.astype(BF)
        mslope[:, cut(row, rows)] = sigma * (1.0 + pre * (1.0 - sigma))

    scale = 1.0 / math.sqrt(8 * 32 * 128)

    for row in (0, 4, 8):
        pre = sum(
            dot(dw[:, a * 3 * MIX : (a + 1) * 3 * MIX], m3[:, cut(row + a, 4)]) for a in range(3)
        )
        sigma = logistic(pre)
        cot = jnp.concatenate([slab(row + 3 + r)[LEV:] for r in range(4)], axis=1)
        back = scale * dot(head_turned[...], cot)
        v = sigma * (1.0 + pre * (1.0 - sigma)) * back
        left, right = neighbours(v)
        for b, u in enumerate((right, v, left)):
            d3[b * MIX : (b + 1) * MIX, cut(row, 4)] = u.astype(BF)
        lo, hi = max(row, 2), min(row + 4, 10)
        dout[:, cut(lo - 2, hi - lo)] = (pre * sigma)[:, cut(lo - row, hi - lo)].astype(BF)

    for row in (0, 5):
        back = sum(
            dot(dt[:, a * 3 * MIX : (a + 1) * 3 * MIX], d3[:, cut(row + 2 - a, 5)])
            for a in range(3)
        )
        v = jnp.where(inside(row - 1, 5), mslope[:, cut(row + 2, 5)] * back, 0.0)
        left, right = neighbours(v)
        for b, u in enumerate((right, v, left)):
            e3[b * MIX : (b + 1) * MIX, cut(row, 5)] = u.astype(BF)

    for row in (0, 4):
        back = sum(
            dot(gt[:, a * 3 * MIX : (a + 1) * 3 * MIX], e3[:, cut(row + 2 - a, 4)])
            for a in range(3)
        )
        jdelta[:, cut(row, 4)] = (jslope[:, cut(row, 4)] * back).astype(BF)

    def put(rows, column, value):
        value = value.astype(BF)
        width = value.shape[1]
        done = 0
        while done < width:
            group, offset = divmod(column + done, WIDE)
            take = min(width - done, WIDE - offset)
            along = chip if group < 4 else depth
            slot = 4 * lax.rem(core + group // 4, 2) + lax.rem(group % 4 + 4 - along, 4)
            out[slot, rows : rows + value.shape[0], offset : offset + take] = value[
                :, done : done + take
            ]
            done += take

    def stacked(delta):
        def zero(rows):
            return jnp.zeros((delta.shape[0], rows * COLS), BF)

        return jnp.concatenate(
            [
                jnp.concatenate([delta, zero(2)], axis=1),
                jnp.concatenate([zero(1), delta, zero(1)], axis=1),
                jnp.concatenate([zero(2), delta], axis=1),
            ],
            axis=0,
        )

    q = pl.ds(pl.multiple_of(segment * OQ, OQ), OQ)
    qd = pl.ds(pl.multiple_of(MIX + segment * OQ, OQ), OQ)
    qm = pl.ds(pl.multiple_of(TERR + segment * MQ, 32), MQ)
    d_own = stacked(d3[qd, cut(2, ROWS)])
    e_own = stacked(e3[qd, cut(1, ROWS)])
    h_own = stacked(jdelta[qm, :])
    for b in range(3):
        part = dot_nt(e_own, j3[b * JOINT : (b + 1) * JOINT, cut(3, ROWS + 2)])
        for a in range(3):
            put(0, (3 * a + b) * JOINT, part[a * OQ : (a + 1) * OQ])
    column = 9 * JOINT
    part = dot_nt(d_own, m3[:, cut(2, ROWS + 2)])
    for a in range(3):
        put(0, column + a * 3 * MIX, part[a * OQ : (a + 1) * OQ])
    column += 9 * MIX
    part = dot_nt(h_own, x3[:, cut(4, ROWS + 2)])
    for a in range(3):
        h = part[a * MQ : (a + 1) * MQ]
        put(0, column + a * 3 * LEV, h[:64])
        spare = column + 9 * LEV
        for c in range(3):
            at = a * 3 * LEV + c * LEV
            piece = h[64:, c * LEV : (c + 1) * LEV]
            if at < 640:
                put(0, spare + at, piece)
            else:
                put(32, spare + at - 640, piece)
    put(32, column + 9 * LEV + 512, jnp.zeros((32, 128), F32))
    column += 9 * LEV + 640
    g = dot_nt(jdelta[q, :], p9[:, cut(4, ROWS)])
    head = scale * dot_nt(
        dout[q, :], jnp.concatenate([eight[r, LEV:] for r in range(ROWS)], axis=1)
    )
    tail = 8 * WIDE - column
    put(0, column, jnp.concatenate([g, head, jnp.zeros((OQ, tail - 10 * SLAB), F32)], axis=1))
    keep[...] = out[:4]
    send[...] = out[4:]


def main(place, above, eight, below, small_ones, *weights):
    smem = pl.BlockSpec(memory_space=pltpu.SMEM)
    vmem = pl.BlockSpec(memory_space=pltpu.VMEM)
    hbm = pl.BlockSpec(memory_space=pltpu.HBM)
    return pl.pallas_call(
        main_kernel,
        out_shape=(jax.ShapeDtypeStruct((4, OQ, WIDE), BF),) * 2,
        in_specs=[smem] + [vmem] * 6 + [hbm] * len(weights),
        out_specs=(vmem, vmem),
        scratch_shapes=[
            pltpu.VMEM((8, OQ, WIDE), BF),
            *[pltpu.VMEM(w.shape, BF) for w in weights],
            pltpu.SemaphoreType.DMA((len(weights),)),
            pltpu.VMEM((MESO, 9 * LEV), BF),
            pltpu.VMEM((TERR, 9 * SLAB), BF),
            pltpu.VMEM((MIX, 9 * MIX), BF),
            pltpu.VMEM((JOINT, 9 * MIX), BF),
            pltpu.VMEM((3 * LEV, (ROWS + 2 * HALO) * COLS), BF),
            pltpu.VMEM((9 * SLAB, (ROWS + 8) * COLS), BF),
            pltpu.VMEM((3 * JOINT, (ROWS + 8) * COLS), BF),
            pltpu.VMEM((JOINT, ROWS * COLS), F32),
            pltpu.VMEM((JOINT, ROWS * COLS), BF),
            pltpu.VMEM((3 * MIX, (ROWS + 6) * COLS), BF),
            pltpu.VMEM((MIX, (ROWS + 6) * COLS), F32),
            pltpu.VMEM((MIX, ROWS * COLS), BF),
            pltpu.VMEM((3 * MIX, (ROWS + 4) * COLS), BF),
            pltpu.VMEM((3 * MIX, (ROWS + 2) * COLS), BF),
        ],
        compiler_params=params(51),
        cost_estimate=pl.CostEstimate(
            flops=15_000_000_000, bytes_accessed=12_000_000, transcendentals=3_000_000
        ),
        name="sections",
    )(place, above, eight, below, *small_ones, *weights)


def split_kernel(keep, came, own, next1, next2, next3):
    own[...] = keep[0].astype(F32) + came[0].astype(F32)
    for j, to in enumerate((next1, next2, next3), 1):
        to[...] = (keep[j].astype(F32) + came[j].astype(F32)).astype(BF)


def total_kernel(own, one, two, three, out):
    parts = [v[...].astype(F32) for v in (own, one, two, three)]
    out[...] = sum(parts[1:], parts[0]).astype(BF)


def pair_kernel(own, other, out):
    out[...] = (own[...].astype(F32) + other[...].astype(F32)).astype(BF)


def stack_kernel(own, one, two, three, out, half0, half1):
    for j, v in enumerate((own, one, two, three)):
        out[j] = v[...]
        (half0, half1)[j // 2][j % 2] = v[...]


def small(kernel, out_shape, *operands):
    return pl.pallas_call(
        kernel, out_shape=out_shape, compiler_params=params(16), name=kernel.__name__[:-7]
    )(*operands)


def moved(v, where):
    pairs = []
    for source in range(128):
        at = (source // 32, source // 8 % 4, source // 2 % 4, source % 2)
        to = where(*at)
        if to is not None:
            pairs.append((source, to[0] * 32 + to[1] * 8 + to[2] * 2 + to[3]))
    return lax.ppermute(v, ("dp", "segment", "space"), pairs)


DP, SEGMENT, CHIP = 0, 1, 2


def along(v, axes, by):
    def where(*at):
        to = list(at)
        to[axes[at[3]]] = (to[axes[at[3]]] + by) % 4
        return to

    return moved(v, where)


def across(v, axes, bits):
    def where(*at):
        to = list(at)
        to[axes[at[3]]] ^= bits
        return to

    return moved(v, where)


def to_partner(v):
    return moved(v, lambda z, x, y, c: (z, x, y, 1 - c))


PARTS = ((0, 0, 4), (-1, 0, 2), (-1, 2, 2), (1, 0, 2), (1, 2, 2), (-2, 0, 2), (-2, 2, 2))


def summed_everywhere(place, keep, send):
    piece = jax.ShapeDtypeStruct((OQ, WIDE), BF)
    wide = jax.ShapeDtypeStruct((OQ, WIDE), F32)
    turns = (1, 2, 3)
    own, *parts = small(split_kernel, (wide, piece, piece, piece), keep, to_partner(send))
    own = small(total_kernel, piece, own, *[along(p, (CHIP, DP), j) for p, j in zip(parts, turns)])
    for bits in (1, 3):
        own = small(pair_kernel, piece, own, across(own, (DP, CHIP), bits))
    four = jax.ShapeDtypeStruct((4, OQ, WIDE), BF)
    two = jax.ShapeDtypeStruct((2, OQ, WIDE), BF)
    block, half0, half1 = small(
        stack_kernel, (four, two, two), own, *[along(own, (CHIP, SEGMENT), j) for j in turns]
    )
    rings = (SEGMENT, DP)
    behind0, ahead1 = along(half0, rings, 1), along(half1, rings, -1)
    behind1, ahead0 = along(half1, rings, 1), along(half0, rings, -1)
    far0, far1 = along(behind0, rings, 1), along(ahead1, rings, -1)
    mine = (block, behind0, behind1, ahead0, ahead1, far0, far1)
    theirs = [to_partner(v) for v in mine[:5]]
    written, token = write_early(place, ((0, 0), (0, 1)), (block, theirs[0]))
    far0, token = lax.optimization_barrier((far0, token))
    theirs.append(to_partner(far0))
    written, token = write_early(place, ((1, 0), (2, 0), (3, 0), (4, 0)), mine[1:5], written, token)
    far1, token = lax.optimization_barrier((far1, token))
    theirs.append(to_partner(far1))
    return mine[:5] + (far0, far1), theirs, (*written, token)


def origin(place, part, j, theirs):
    segment, chip, core, depth = place[0], place[1] // 2, place[1] % 2, place[2]
    step, first, _ = PARTS[part]
    kind = 1 - core if theirs else core
    group = jnp.where(
        kind == 0, lax.rem(chip - (first + j) + 4, 4), 4 + lax.rem(depth + step + 4, 4)
    )
    row = lax.rem(segment + jnp.where(kind == 0, step, -(first + j)) + 4, 4)
    return group, row


def write_out(place, which, refs, merging, decoder, stage, sems):
    chunks = []
    for (part, theirs), ref in zip(which, refs):
        for j in range(PARTS[part][2]):
            stage[len(chunks)] = ref[j].astype(F32)
            chunks.append((len(chunks), *origin(place, part, j, theirs)))

    def pieces(i, group, row):
        slot = stage.at[i]
        rows = pl.ds(pl.multiple_of(row * OQ, OQ), OQ)
        left = 9 * JOINT - 4 * WIDE
        last = 9 * MIX - (2 * WIDE - left)
        yield group < 4, [
            (slot, merging.at[rows, pl.ds(pl.multiple_of(group * WIDE, WIDE), WIDE)])
        ]
        yield group == 4, [
            (slot.at[:, :left], merging.at[rows, 4 * WIDE :]),
            (slot.at[:, left:], decoder.at[rows, : WIDE - left]),
        ]
        yield group == 5, [(slot, decoder.at[rows, WIDE - left : 2 * WIDE - left])]
        yield group == 6, [(slot.at[:, :last], decoder.at[rows, 2 * WIDE - left :])]

    def each(do):
        for i, group, row in chunks:
            for when, copies in pieces(i, group, row):

                @pl.when(when)
                def _(i=i, copies=copies):
                    for n, (source, target) in enumerate(copies):
                        do(pltpu.make_async_copy(source, target, sems.at[2 * i + n]))

    each(lambda copy: copy.start())
    return lambda: each(lambda copy: copy.wait())


def early_kernel(which, n_old, place, *refs):
    n = len(which)
    n_old += min(n_old, 1)
    parts, (merging, decoder, token, stage, sems) = refs[n_old : n_old + n], refs[n_old + n :]
    write_out(place, which, parts, merging, decoder, stage, sems)()
    token[...] = jnp.zeros(token.shape, F32)


def write_early(place, which, parts, old=(), *after):
    smem = pl.BlockSpec(memory_space=pltpu.SMEM)
    vmem = pl.BlockSpec(memory_space=pltpu.VMEM)
    hbm = pl.BlockSpec(memory_space=pltpu.HBM)
    chunks = sum(PARTS[part][2] for part, _ in which)
    *written, token = pl.pallas_call(
        functools.partial(early_kernel, which, len(old)),
        out_shape=(
            jax.ShapeDtypeStruct((MIX, 9 * JOINT), F32),
            jax.ShapeDtypeStruct((MIX, 9 * MIX), F32),
            jax.ShapeDtypeStruct((8, 128), F32),
        ),
        in_specs=[smem] + [hbm] * len(old) + [vmem] * (len(after) + len(parts)),
        out_specs=(hbm, hbm, vmem),
        scratch_shapes=[
            pltpu.VMEM((chunks, OQ, WIDE), F32),
            pltpu.SemaphoreType.DMA((2 * chunks,)),
        ],
        input_output_aliases={1 + i: i for i in range(len(old))},
        compiler_params=params(12),
        cost_estimate=pl.CostEstimate(flops=0, bytes_accessed=4_000_000, transcendentals=0),
        name="early",
    )(place, *old, *after, *parts)
    return written, token


LATE = ((1, 1), (2, 1), (3, 1), (4, 1), (5, 0), (6, 0), (5, 1), (6, 1))


def finish_kernel(place, *refs):
    n = len(PARTS)
    sides, refs = (refs[3 : 3 + n], refs[3 + n : 3 + 2 * n]), refs[3 + 2 * n :]
    lw, pw16, mw_hbm, tw_hbm = refs[:4]
    patch, lift, head, terrain, meso, merging, decoder = refs[4:11]
    mw, tw, stage, rest, wide_m, wide_t, ht, gt, sems, late_sems = refs[11:]
    reads = [
        pltpu.make_async_copy(mw_hbm, mw, sems.at[0]),
        pltpu.make_async_copy(tw_hbm, tw, sems.at[1]),
    ]
    for copy in reads:
        copy.start()
    late = [sides[theirs][part] for part, theirs in LATE]
    written = write_out(place, LATE, late, merging, decoder, stage, late_sems)
    for part in range(n):
        for theirs in range(2):
            for j in range(PARTS[part][2]):
                group, row = origin(place, part, j, theirs)

                @pl.when(group >= 6)
                def _(part=part, theirs=theirs, j=j, group=group, row=row):
                    rest[
                        pl.ds(pl.multiple_of(row * OQ, OQ), OQ),
                        pl.ds(pl.multiple_of((group - 6) * WIDE, WIDE), WIDE),
                    ] = sides[theirs][part][j]

    column = 9 * JOINT + 9 * MIX - 6 * WIDE
    writes = []
    for seg in range(4):
        lo = seg * OQ
        at = seg * MQ
        ht[at : at + 64, :] = rest[lo : lo + OQ, column : column + 9 * LEV]
        spare = column + 9 * LEV
        ht[at + 64 : at + MQ, :640] = rest[lo : lo + 32, spare : spare + 640]
        ht[at + 64 : at + MQ, 640:] = rest[lo + 32 : lo + OQ, spare : spare + 512]
        gt[lo : lo + OQ, :] = rest[lo : lo + OQ, spare + 640 : spare + 896].astype(F32)
    for a in range(3):
        for tap in range(3 * a, 3 * a + 3):
            wide_m[:, tap * MESO : (tap + 1) * MESO] = dot_nt(
                ht[:, tap * LEV : (tap + 1) * LEV], lw[...]
            )
        part = slice(3 * a * MESO, 3 * (a + 1) * MESO)
        writes.append(pltpu.make_async_copy(wide_m.at[:, part], meso.at[:, part], sems.at[4 + a]))
        writes[-1].start()
    g = gt[...]
    for tap in range(9):
        wide_t[:, tap * TERR : (tap + 1) * TERR] = dot(
            g[:, tap * SLAB : (tap + 1) * SLAB].astype(BF), pw16[...]
        )
    writes.append(pltpu.make_async_copy(wide_t, terrain, sems.at[7]))
    writes[-1].start()
    turned = g.T
    head[...] = turned[9 * SLAB + 8 : 9 * SLAB + 11, :]
    reads[1].wait()
    patch[...] = sum(
        dot(
            turned[tap * SLAB : (tap + 1) * SLAB, :].astype(BF),
            tw[:, tap * TERR : (tap + 1) * TERR],
        )
        for tap in range(9)
    )[:8]
    turned = ht[...].astype(F32).T.astype(BF)
    reads[0].wait()
    lift[...] = sum(
        dot(turned[tap * LEV : (tap + 1) * LEV, :], mw[:, tap * MESO : (tap + 1) * MESO])
        for tap in range(9)
    ).T
    for copy in writes:
        copy.wait()
    written()


def finish(place, old, parts, lift_copy, patch_turned, meso_weight, terrain_weight):
    smem = pl.BlockSpec(memory_space=pltpu.SMEM)
    vmem = pl.BlockSpec(memory_space=pltpu.VMEM)
    hbm = pl.BlockSpec(memory_space=pltpu.HBM)
    patch, lift, head, terrain, meso, merging, decoder = pl.pallas_call(
        finish_kernel,
        out_shape=(
            jax.ShapeDtypeStruct((8, TERR), F32),
            jax.ShapeDtypeStruct((MESO, LEV), F32),
            jax.ShapeDtypeStruct((3, MIX), F32),
            jax.ShapeDtypeStruct((TERR, 9 * TERR), F32),
            jax.ShapeDtypeStruct((MESO, 9 * MESO), F32),
            jax.ShapeDtypeStruct((MIX, 9 * JOINT), F32),
            jax.ShapeDtypeStruct((MIX, 9 * MIX), F32),
        ),
        in_specs=[smem] + [hbm] * 2 + [vmem] * (3 + len(parts)) + [hbm] * 2,
        out_specs=(vmem,) * 3 + (hbm,) * 4,
        scratch_shapes=[
            pltpu.VMEM((MESO, 9 * MESO), BF),
            pltpu.VMEM((TERR, 9 * TERR), BF),
            pltpu.VMEM((16, OQ, WIDE), F32),
            pltpu.VMEM((MIX, 2 * WIDE), BF),
            pltpu.VMEM((MESO, 9 * MESO), F32),
            pltpu.VMEM((TERR, 9 * TERR), F32),
            pltpu.VMEM((MESO, 9 * LEV), BF),
            pltpu.VMEM((MIX, 256), F32),
            pltpu.SemaphoreType.DMA((8,)),
            pltpu.SemaphoreType.DMA((32,)),
        ],
        input_output_aliases={1: 5, 2: 6},
        compiler_params=params(36),
        name="finish",
    )(place, *old, *parts, lift_copy, patch_turned, meso_weight, terrain_weight)
    return patch.T, terrain, lift, meso, merging, decoder, head


def packed(terrain_in, meso_in, wind_cot):
    samples, rows = meso_in.shape[0], meso_in.shape[3]
    source = lax.broadcasted_iota(jnp.int32, (2 * COLS, 2 * COLS), 0)
    target = lax.broadcasted_iota(jnp.int32, (2 * COLS, 2 * COLS), 1)
    pick = (source == 2 * (target % COLS) + target // COLS).astype(BF)
    split = dot(terrain_in.reshape(samples * 4 * rows, 2 * COLS), pick).astype(BF)
    patches = (
        split.reshape(samples, 2, rows, 2, 2, COLS)
        .transpose(0, 2, 1, 3, 4, 5)
        .reshape(samples, rows, 8, COLS)
    )
    levels = meso_in.reshape(samples, LEV, rows, COLS).transpose(0, 2, 1, 3)
    cot = wind_cot.transpose(0, 2, 1, 3)
    rest = jnp.zeros((samples, rows, PACK - LEV - 11, COLS), BF)
    return jnp.concatenate([levels, patches, cot, rest], axis=2)


def to_chip(v, by):
    return moved(v, lambda z, x, y, c: (z, x, y + by, c) if 0 <= y + by < 4 else None)


def local(
    terrain_in,
    meso_in,
    wind_cot,
    patch_weight,
    terrain_weight,
    lift_weight,
    meso_weight,
    merging_weight,
    decoder_weight,
    head_weight,
):
    own = packed(terrain_in, meso_in, wind_cot)
    place = jnp.stack([lax.axis_index(a) for a in ("segment", "space", "dp")]).astype(jnp.int32)
    eight, first, last = chip_rows(place, own, to_partner(own))
    above, below = to_chip(last, 1), to_chip(first, -1)
    small_ones = small_weights(lift_weight, patch_weight.T, head_weight)
    keep, send = main(
        place,
        above,
        eight,
        below,
        small_ones,
        meso_weight,
        terrain_weight,
        merging_weight,
        decoder_weight,
    )
    mine, theirs, written = summed_everywhere(place, keep, send)
    return finish(
        place, written, (*mine, *theirs), *small_ones[:2], meso_weight, terrain_weight
    )


def solution(mesh):
    placed = (
        P("dp", None, "space", None),
        P("dp", None, None, "space", None),
        P("dp", None, "space", None),
        P(),
        P(),
        P(),
        P(),
        P(),
        P(),
        P(),
    )
    return jax.shard_map(
        local,
        mesh=mesh,
        in_specs=placed,
        out_specs=(P(), P(), P(), P(), P(), P(), P()),
        check_vma=False,
    )
```

```python
import functools
import math

import jax
import jax.numpy as jnp
from jax import lax
from jax.experimental import pallas as pl
from jax.experimental.pallas import tpu as pltpu
from jax.sharding import PartitionSpec as P

BF = jnp.bfloat16
F32 = jnp.float32
TERR, MESO, MIX = 256, 384, 256
JOINT = TERR + MESO
LEV = 128
SLAB = 16
PACK = LEV + SLAB
ROWS, COLS = 8, 128
HALO = 5
OQ, MQ = MIX // 4, MESO // 4
WIDE = 1280
NT = (((1,), (1,)), ((), ()))


def dot(a, b):
    return jnp.dot(a, b, preferred_element_type=F32)


def dot_nt(a, b):
    return lax.dot_general(a, b, NT, preferred_element_type=F32)


def params(mib):
    return pltpu.CompilerParams(vmem_limit_bytes=mib * 1024 * 1024)


def sixteen(v, above):
    rows, width = v.shape
    parts = [v.astype(F32)]
    if above:
        parts.insert(0, jnp.zeros((above, width), F32))
    if above + rows < SLAB:
        parts.append(jnp.zeros((SLAB - above - rows, width), F32))
    return jnp.concatenate(parts, axis=0)


def small_kernel(lw, pw, hw, lw_out, pw_out, head_turned):
    lw_out[...] = lw[...]
    pw_out[...] = sixteen(pw[...], 0).astype(BF)
    head_turned[...] = sixteen(hw[...], 8).T.astype(BF)


def small_weights(lift_weight, patch_turned, head_weight):
    return pl.pallas_call(
        small_kernel,
        out_shape=(
            jax.ShapeDtypeStruct((MESO, LEV), BF),
            jax.ShapeDtypeStruct((SLAB, TERR), BF),
            jax.ShapeDtypeStruct((MIX, SLAB), BF),
        ),
        compiler_params=params(16),
        cost_estimate=pl.CostEstimate(flops=0, bytes_accessed=4_000_000, transcendentals=0),
        name="small_weights",
    )(lift_weight, patch_turned, head_weight)


def rows_kernel(place, own, partner, eight, first, last):
    core = place[1] % 2
    for c in range(2):

        @pl.when(core == c)
        def _(c=c):
            halves = (own, partner) if c == 0 else (partner, own)
            for r in range(ROWS):
                v = halves[r // 4][c, r % 4]
                eight[r] = v
                if r < HALO:
                    first[r] = v
                if r >= ROWS - HALO:
                    last[r - (ROWS - HALO)] = v


def chip_rows(place, own, partner):
    smem = pl.BlockSpec(memory_space=pltpu.SMEM)
    vmem = pl.BlockSpec(memory_space=pltpu.VMEM)
    return pl.pallas_call(
        rows_kernel,
        out_shape=tuple(
            jax.ShapeDtypeStruct((n, PACK, COLS), BF) for n in (ROWS, HALO, HALO)
        ),
        in_specs=[smem, vmem, vmem],
        out_specs=(vmem,) * 3,
        compiler_params=params(16),
        name="rows",
    )(place, own, partner)


def neighbours(v):
    width = v.shape[1]
    lane = lax.broadcasted_iota(jnp.int32, (1, width), 1) % COLS
    left, right = [], []
    for r in range(width // COLS):
        piece = v[:, r * COLS : (r + 1) * COLS]
        left.append(pltpu.roll(piece, 1, 1))
        right.append(pltpu.roll(piece, COLS - 1, 1))
    left = jnp.where(lane == 0, 0.0, jnp.concatenate(left, axis=1))
    right = jnp.where(lane == COLS - 1, 0.0, jnp.concatenate(right, axis=1))
    return left, right


def logistic(v):
    return 0.5 * (1.0 + jnp.tanh(0.5 * v))


def main_kernel(place, above, eight, below, lw, pw16, head_turned, *refs):
    n_w = 4
    weights_hbm, keep, send, out = refs[:n_w], *refs[n_w : n_w + 3]
    mw, tw, gw, dw = weights = refs[n_w + 3 : 2 * n_w + 3]
    sems, wm, wt, dt, gt = refs[2 * n_w + 3 : 2 * n_w + 8]
    x3, p9, j3, jslope, jdelta, m3, mslope, dout, d3, e3 = refs[2 * n_w + 8 :]
    copies = [
        pltpu.make_async_copy(u, v, sems.at[i]) for i, (u, v) in enumerate(zip(weights_hbm, weights))
    ]
    for copy in copies[:2]:
        copy.start()
    segment, depth = place[0], place[2]
    chip, core = place[1] // 2, place[1] % 2
    first_row = chip * ROWS

    def cut(row, rows):
        return slice(row * COLS, (row + rows) * COLS)

    def inside(row, rows):
        at = lax.broadcasted_iota(jnp.int32, (1, rows * COLS), 1) // COLS + row + first_row
        return jnp.logical_and(at >= 0, at < 4 * ROWS)

    def slab(r):
        for ref, rows in ((above, HALO), (eight, ROWS), (below, HALO)):
            if r < rows:
                return ref[r]
            r -= rows

    n_in, n_join = ROWS + 2 * HALO, ROWS + 8

    for r in range(n_in):
        v = slab(r).astype(F32)
        left, right = neighbours(v)
        for b, u in enumerate((left, v, right)):
            u = u.astype(BF)
            x3[b * LEV : (b + 1) * LEV, cut(r, 1)] = u[:LEV]
            for a in range(3):
                if a <= r < n_join + a:
                    tap = 3 * a + b
                    p9[tap * SLAB : (tap + 1) * SLAB, cut(r - a, 1)] = u[LEV:]

    copies[0].wait()
    for tap in range(9):
        wm[:, tap * LEV : (tap + 1) * LEV] = dot(
            mw[:, tap * MESO : (tap + 1) * MESO], lw[...]
        ).astype(BF)
    copies[1].wait()
    for copy in copies[2:]:
        copy.start()
    wt[...] = jnp.concatenate(
        [dot_nt(tw[:, tap * TERR : (tap + 1) * TERR], pw16[...]).astype(BF) for tap in range(9)], axis=1
    )

    for row in (0, 4, 8, 12):
        pre_t = dot(wt[...], p9[:, cut(row, 4)])
        pre_m = sum(
            dot(wm[:, a * 3 * LEV : (a + 1) * 3 * LEV], x3[:, cut(row + a, 4)]) for a in range(3)
        )
        for at, pre in ((0, pre_t), (TERR, pre_m)):
            size = pre.shape[0]
            sigma = logistic(pre)
            v = jnp.where(inside(row - 4, 4), pre * sigma, 0.0)
            left, right = neighbours(v)
            for b, u in enumerate((left, v, right)):
                j3[b * JOINT + at : b * JOINT + at + size, cut(row, 4)] = u.astype(BF)
            if row in (4, 8):
                jslope[at : at + size, cut(row - 4, 4)] = sigma * (1.0 + pre * (1.0 - sigma))

    copies[2].wait()
    copies[3].wait()
    for tap in range(9):
        gt[:, tap * MIX : (tap + 1) * MIX] = gw[:, tap * JOINT : (tap + 1) * JOINT].T
        dt[:, tap * MIX : (tap + 1) * MIX] = dw[:, tap * MIX : (tap + 1) * MIX].T

    for row, rows in ((0, 4), (4, 5), (9, 5)):
        pre = sum(
            dot(gw[:, a * 3 * JOINT : (a + 1) * 3 * JOINT], j3[:, cut(row + a, rows)])
            for a in range(3)
        )
        sigma = logistic(pre)
        v = jnp.where(inside(row - 3, rows), pre * sigma, 0.0)
        left, right = neighbours(v)
        for b, u in enumerate((left, v, right)):
            m3[b * MIX : (b + 1) * MIX, cut(row, rows)] = u.astype(BF)
        mslope[:, cut(row, rows)] = sigma * (1.0 + pre * (1.0 - sigma))

    scale = 1.0 / math.sqrt(8 * 32 * 128)

    for row in (0, 4, 8):
        pre = sum(
            dot(dw[:, a * 3 * MIX : (a + 1) * 3 * MIX], m3[:, cut(row + a, 4)]) for a in range(3)
        )
        sigma = logistic(pre)
        cot = jnp.concatenate([slab(row + 3 + r)[LEV:] for r in range(4)], axis=1)
        back = scale * dot(head_turned[...], cot)
        v = sigma * (1.0 + pre * (1.0 - sigma)) * back
        left, right = neighbours(v)
        for b, u in enumerate((right, v, left)):
            d3[b * MIX : (b + 1) * MIX, cut(row, 4)] = u.astype(BF)
        lo, hi = max(row, 2), min(row + 4, 10)
        dout[:, cut(lo - 2, hi - lo)] = (pre * sigma)[:, cut(lo - row, hi - lo)].astype(BF)

    for row in (0, 5):
        back = sum(
            dot(dt[:, a * 3 * MIX : (a + 1) * 3 * MIX], d3[:, cut(row + 2 - a, 5)])
            for a in range(3)
        )
        v = jnp.where(inside(row - 1, 5), mslope[:, cut(row + 2, 5)] * back, 0.0)
        left, right = neighbours(v)
        for b, u in enumerate((right, v, left)):
            e3[b * MIX : (b + 1) * MIX, cut(row, 5)] = u.astype(BF)

    for row in (0, 4):
        back = sum(
            dot(gt[:, a * 3 * MIX : (a + 1) * 3 * MIX], e3[:, cut(row + 2 - a, 4)])
            for a in range(3)
        )
        jdelta[:, cut(row, 4)] = (jslope[:, cut(row, 4)] * back).astype(BF)

    def put(rows, column, value):
        value = value.astype(BF)
        width = value.shape[1]
        done = 0
        while done < width:
            group, offset = divmod(column + done, WIDE)
            take = min(width - done, WIDE - offset)
            along = chip if group < 4 else depth
            slot = 4 * lax.rem(core + group // 4, 2) + lax.rem(group % 4 + 4 - along, 4)
            out[slot, rows : rows + value.shape[0], offset : offset + take] = value[
                :, done : done + take
            ]
            done += take

    def stacked(delta):
        def zero(rows):
            return jnp.zeros((delta.shape[0], rows * COLS), BF)

        return jnp.concatenate(
            [
                jnp.concatenate([delta, zero(2)], axis=1),
                jnp.concatenate([zero(1), delta, zero(1)], axis=1),
                jnp.concatenate([zero(2), delta], axis=1),
            ],
            axis=0,
        )

    q = pl.ds(pl.multiple_of(segment * OQ, OQ), OQ)
    qd = pl.ds(pl.multiple_of(MIX + segment * OQ, OQ), OQ)
    qm = pl.ds(pl.multiple_of(TERR + segment * MQ, 32), MQ)
    d_own = stacked(d3[qd, cut(2, ROWS)])
    e_own = stacked(e3[qd, cut(1, ROWS)])
    h_own = stacked(jdelta[qm, :])
    for b in range(3):
        part = dot_nt(e_own, j3[b * JOINT : (b + 1) * JOINT, cut(3, ROWS + 2)])
        for a in range(3):
            put(0, (3 * a + b) * JOINT, part[a * OQ : (a + 1) * OQ])
    column = 9 * JOINT
    part = dot_nt(d_own, m3[:, cut(2, ROWS + 2)])
    for a in range(3):
        put(0, column + a * 3 * MIX, part[a * OQ : (a + 1) * OQ])
    column += 9 * MIX
    part = dot_nt(h_own, x3[:, cut(4, ROWS + 2)])
    for a in range(3):
        h = part[a * MQ : (a + 1) * MQ]
        put(0, column + a * 3 * LEV, h[:64])
        spare = column + 9 * LEV
        for c in range(3):
            at = a * 3 * LEV + c * LEV
            piece = h[64:, c * LEV : (c + 1) * LEV]
            if at < 640:
                put(0, spare + at, piece)
            else:
                put(32, spare + at - 640, piece)
    put(32, column + 9 * LEV + 512, jnp.zeros((32, 128), F32))
    column += 9 * LEV + 640
    g = dot_nt(jdelta[q, :], p9[:, cut(4, ROWS)])
    head = scale * dot_nt(
        dout[q, :], jnp.concatenate([eight[r, LEV:] for r in range(ROWS)], axis=1)
    )
    tail = 8 * WIDE - column
    put(0, column, jnp.concatenate([g, head, jnp.zeros((OQ, tail - 10 * SLAB), F32)], axis=1))
    keep[...] = out[:4]
    send[...] = out[4:]


def main(place, above, eight, below, small_ones, *weights):
    smem = pl.BlockSpec(memory_space=pltpu.SMEM)
    vmem = pl.BlockSpec(memory_space=pltpu.VMEM)
    hbm = pl.BlockSpec(memory_space=pltpu.HBM)
    return pl.pallas_call(
        main_kernel,
        out_shape=(jax.ShapeDtypeStruct((4, OQ, WIDE), BF),) * 2,
        in_specs=[smem] + [vmem] * 6 + [hbm] * len(weights),
        out_specs=(vmem, vmem),
        scratch_shapes=[
            pltpu.VMEM((8, OQ, WIDE), BF),
            *[pltpu.VMEM(w.shape, BF) for w in weights],
            pltpu.SemaphoreType.DMA((len(weights),)),
            pltpu.VMEM((MESO, 9 * LEV), BF),
            pltpu.VMEM((TERR, 9 * SLAB), BF),
            pltpu.VMEM((MIX, 9 * MIX), BF),
            pltpu.VMEM((JOINT, 9 * MIX), BF),
            pltpu.VMEM((3 * LEV, (ROWS + 2 * HALO) * COLS), BF),
            pltpu.VMEM((9 * SLAB, (ROWS + 8) * COLS), BF),
            pltpu.VMEM((3 * JOINT, (ROWS + 8) * COLS), BF),
            pltpu.VMEM((JOINT, ROWS * COLS), F32),
            pltpu.VMEM((JOINT, ROWS * COLS), BF),
            pltpu.VMEM((3 * MIX, (ROWS + 6) * COLS), BF),
            pltpu.VMEM((MIX, (ROWS + 6) * COLS), F32),
            pltpu.VMEM((MIX, ROWS * COLS), BF),
            pltpu.VMEM((3 * MIX, (ROWS + 4) * COLS), BF),
            pltpu.VMEM((3 * MIX, (ROWS + 2) * COLS), BF),
        ],
        compiler_params=params(51),
        cost_estimate=pl.CostEstimate(
            flops=15_000_000_000, bytes_accessed=12_000_000, transcendentals=3_000_000
        ),
        name="sections",
    )(place, above, eight, below, *small_ones, *weights)


def split_kernel(keep, came, own, next1, next2, next3):
    own[...] = keep[0].astype(F32) + came[0].astype(F32)
    for j, to in enumerate((next1, next2, next3), 1):
        to[...] = (keep[j].astype(F32) + came[j].astype(F32)).astype(BF)


def total_kernel(own, one, two, three, out):
    parts = [v[...].astype(F32) for v in (own, one, two, three)]
    out[...] = sum(parts[1:], parts[0]).astype(BF)


def pair_kernel(own, other, out):
    out[...] = (own[...].astype(F32) + other[...].astype(F32)).astype(BF)


def stack_kernel(own, one, two, three, out, half0, half1):
    for j, v in enumerate((own, one, two, three)):
        out[j] = v[...]
        (half0, half1)[j // 2][j % 2] = v[...]


def small(kernel, out_shape, *operands):
    return pl.pallas_call(
        kernel, out_shape=out_shape, compiler_params=params(16), name=kernel.__name__[:-7]
    )(*operands)


def moved(v, where):
    pairs = []
    for source in range(128):
        at = (source // 32, source // 8 % 4, source // 2 % 4, source % 2)
        to = where(*at)
        if to is not None:
            pairs.append((source, to[0] * 32 + to[1] * 8 + to[2] * 2 + to[3]))
    return lax.ppermute(v, ("dp", "segment", "space"), pairs)


DP, SEGMENT, CHIP = 0, 1, 2


def along(v, axes, by):
    def where(*at):
        to = list(at)
        to[axes[at[3]]] = (to[axes[at[3]]] + by) % 4
        return to

    return moved(v, where)


def across(v, axes, bits):
    def where(*at):
        to = list(at)
        to[axes[at[3]]] ^= bits
        return to

    return moved(v, where)


def to_partner(v):
    return moved(v, lambda z, x, y, c: (z, x, y, 1 - c))


PARTS = ((0, 0, 4), (-1, 0, 2), (-1, 2, 2), (1, 0, 2), (1, 2, 2), (-2, 0, 2), (-2, 2, 2))


def summed_everywhere(place, keep, send):
    piece = jax.ShapeDtypeStruct((OQ, WIDE), BF)
    wide = jax.ShapeDtypeStruct((OQ, WIDE), F32)
    turns = (1, 2, 3)
    own, *parts = small(split_kernel, (wide, piece, piece, piece), keep, to_partner(send))
    own = small(total_kernel, piece, own, *[along(p, (CHIP, DP), j) for p, j in zip(parts, turns)])
    for bits in (1, 3):
        own = small(pair_kernel, piece, own, across(own, (DP, CHIP), bits))
    four = jax.ShapeDtypeStruct((4, OQ, WIDE), BF)
    two = jax.ShapeDtypeStruct((2, OQ, WIDE), BF)
    block, half0, half1 = small(
        stack_kernel, (four, two, two), own, *[along(own, (CHIP, SEGMENT), j) for j in turns]
    )
    rings = (SEGMENT, DP)
    behind0, ahead1 = along(half0, rings, 1), along(half1, rings, -1)
    behind1, ahead0 = along(half1, rings, 1), along(half0, rings, -1)
    mine = [block, behind0, behind1, ahead0, ahead1]
    theirs = [to_partner(v) for v in mine]
    written, token = write_early(place, ((0, 0), (0, 1)), (block, theirs[0]))
    behind0, token = lax.optimization_barrier((behind0, token))
    far0, far1 = along(behind0, rings, 1), along(ahead1, rings, -1)
    written, token = write_early(
        place, ((1, 0), (2, 0), (3, 0), (4, 0)), mine[1:], written, token
    )
    far0, token = lax.optimization_barrier((far0, token))
    written, token = write_early(
        place, ((1, 1), (2, 1), (3, 1), (4, 1)), theirs[1:], written, token
    )
    mine += [far0, far1]
    theirs += [to_partner(far0), to_partner(far1)]
    return mine, theirs, (*written, token)


def origin(place, part, j, theirs):
    segment, chip, core, depth = place[0], place[1] // 2, place[1] % 2, place[2]
    step, first, _ = PARTS[part]
    kind = 1 - core if theirs else core
    group = jnp.where(
        kind == 0, lax.rem(chip - (first + j) + 4, 4), 4 + lax.rem(depth + step + 4, 4)
    )
    row = lax.rem(segment + jnp.where(kind == 0, step, -(first + j)) + 4, 4)
    return group, row


def write_out(place, which, refs, merging, decoder, stage, sems):
    chunks = []
    for (part, theirs), ref in zip(which, refs):
        for j in range(PARTS[part][2]):
            stage[len(chunks)] = ref[j].astype(F32)
            chunks.append((len(chunks), *origin(place, part, j, theirs)))

    def pieces(i, group, row):
        slot = stage.at[i]
        rows = pl.ds(pl.multiple_of(row * OQ, OQ), OQ)
        left = 9 * JOINT - 4 * WIDE
        last = 9 * MIX - (2 * WIDE - left)
        yield group < 4, [
            (slot, merging.at[rows, pl.ds(pl.multiple_of(group * WIDE, WIDE), WIDE)])
        ]
        yield group == 4, [
            (slot.at[:, :left], merging.at[rows, 4 * WIDE :]),
            (slot.at[:, left:], decoder.at[rows, : WIDE - left]),
        ]
        yield group == 5, [(slot, decoder.at[rows, WIDE - left : 2 * WIDE - left])]
        yield group == 6, [(slot.at[:, :last], decoder.at[rows, 2 * WIDE - left :])]

    def each(do):
        for i, group, row in chunks:
            for when, copies in pieces(i, group, row):

                @pl.when(when)
                def _(i=i, copies=copies):
                    for n, (source, target) in enumerate(copies):
                        do(pltpu.make_async_copy(source, target, sems.at[2 * i + n]))

    each(lambda copy: copy.start())
    return lambda: each(lambda copy: copy.wait())


def early_kernel(which, n_old, place, *refs):
    n = len(which)
    n_old += min(n_old, 1)
    parts, (merging, decoder, token, stage, sems) = refs[n_old : n_old + n], refs[n_old + n :]
    write_out(place, which, parts, merging, decoder, stage, sems)()
    token[...] = jnp.zeros(token.shape, F32)


def write_early(place, which, parts, old=(), *after):
    smem = pl.BlockSpec(memory_space=pltpu.SMEM)
    vmem = pl.BlockSpec(memory_space=pltpu.VMEM)
    hbm = pl.BlockSpec(memory_space=pltpu.HBM)
    chunks = sum(PARTS[part][2] for part, _ in which)
    *written, token = pl.pallas_call(
        functools.partial(early_kernel, which, len(old)),
        out_shape=(
            jax.ShapeDtypeStruct((MIX, 9 * JOINT), F32),
            jax.ShapeDtypeStruct((MIX, 9 * MIX), F32),
            jax.ShapeDtypeStruct((8, 128), F32),
        ),
        in_specs=[smem] + [hbm] * len(old) + [vmem] * (len(after) + len(parts)),
        out_specs=(hbm, hbm, vmem),
        scratch_shapes=[
            pltpu.VMEM((chunks, OQ, WIDE), F32),
            pltpu.SemaphoreType.DMA((2 * chunks,)),
        ],
        input_output_aliases={1 + i: i for i in range(len(old))},
        compiler_params=params(12),
        cost_estimate=pl.CostEstimate(flops=0, bytes_accessed=4_000_000, transcendentals=0),
        name="early",
    )(place, *old, *after, *parts)
    return written, token


LATE = ((5, 0), (6, 0), (5, 1), (6, 1))


def finish_kernel(place, *refs):
    n = len(PARTS)
    sides, refs = (refs[3 : 3 + n], refs[3 + n : 3 + 2 * n]), refs[3 + 2 * n :]
    lw, pw16, mw_hbm, tw_hbm = refs[:4]
    patch, lift, head, terrain, meso, merging, decoder = refs[4:11]
    mw, tw, stage, rest, wide_m, wide_t, ht, gt, sems, late_sems = refs[11:]
    reads = [
        pltpu.make_async_copy(mw_hbm, mw, sems.at[0]),
        pltpu.make_async_copy(tw_hbm, tw, sems.at[1]),
    ]
    for copy in reads:
        copy.start()
    late = [sides[theirs][part] for part, theirs in LATE]
    written = write_out(place, LATE, late, merging, decoder, stage, late_sems)
    for part in range(n):
        for theirs in range(2):
            for j in range(PARTS[part][2]):
                group, row = origin(place, part, j, theirs)

                @pl.when(group >= 6)
                def _(part=part, theirs=theirs, j=j, group=group, row=row):
                    rest[
                        pl.ds(pl.multiple_of(row * OQ, OQ), OQ),
                        pl.ds(pl.multiple_of((group - 6) * WIDE, WIDE), WIDE),
                    ] = sides[theirs][part][j]

    column = 9 * JOINT + 9 * MIX - 6 * WIDE
    writes = []
    for seg in range(4):
        lo = seg * OQ
        at = seg * MQ
        ht[at : at + 64, :] = rest[lo : lo + OQ, column : column + 9 * LEV]
        spare = column + 9 * LEV
        ht[at + 64 : at + MQ, :640] = rest[lo : lo + 32, spare : spare + 640]
        ht[at + 64 : at + MQ, 640:] = rest[lo + 32 : lo + OQ, spare : spare + 512]
        gt[lo : lo + OQ, :] = rest[lo : lo + OQ, spare + 640 : spare + 896].astype(F32)
    for a in range(3):
        for tap in range(3 * a, 3 * a + 3):
            wide_m[:, tap * MESO : (tap + 1) * MESO] = dot_nt(
                ht[:, tap * LEV : (tap + 1) * LEV], lw[...]
            )
        part = slice(3 * a * MESO, 3 * (a + 1) * MESO)
        writes.append(pltpu.make_async_copy(wide_m.at[:, part], meso.at[:, part], sems.at[4 + a]))
        writes[-1].start()
    g = gt[...]
    for tap in range(9):
        wide_t[:, tap * TERR : (tap + 1) * TERR] = dot(
            g[:, tap * SLAB : (tap + 1) * SLAB].astype(BF), pw16[...]
        )
    writes.append(pltpu.make_async_copy(wide_t, terrain, sems.at[7]))
    writes[-1].start()
    turned = g.T
    head[...] = turned[9 * SLAB + 8 : 9 * SLAB + 11, :]
    reads[1].wait()
    patch[...] = sum(
        dot(
            turned[tap * SLAB : (tap + 1) * SLAB, :].astype(BF),
            tw[:, tap * TERR : (tap + 1) * TERR],
        )
        for tap in range(9)
    )[:8]
    turned = ht[...].astype(F32).T.astype(BF)
    reads[0].wait()
    lift[...] = sum(
        dot(turned[tap * LEV : (tap + 1) * LEV, :], mw[:, tap * MESO : (tap + 1) * MESO])
        for tap in range(9)
    ).T
    for copy in writes:
        copy.wait()
    written()


def finish(place, old, parts, lift_copy, patch_turned, meso_weight, terrain_weight):
    smem = pl.BlockSpec(memory_space=pltpu.SMEM)
    vmem = pl.BlockSpec(memory_space=pltpu.VMEM)
    hbm = pl.BlockSpec(memory_space=pltpu.HBM)
    patch, lift, head, terrain, meso, merging, decoder = pl.pallas_call(
        finish_kernel,
        out_shape=(
            jax.ShapeDtypeStruct((8, TERR), F32),
            jax.ShapeDtypeStruct((MESO, LEV), F32),
            jax.ShapeDtypeStruct((3, MIX), F32),
            jax.ShapeDtypeStruct((TERR, 9 * TERR), F32),
            jax.ShapeDtypeStruct((MESO, 9 * MESO), F32),
            jax.ShapeDtypeStruct((MIX, 9 * JOINT), F32),
            jax.ShapeDtypeStruct((MIX, 9 * MIX), F32),
        ),
        in_specs=[smem] + [hbm] * 2 + [vmem] * (3 + len(parts)) + [hbm] * 2,
        out_specs=(vmem,) * 3 + (hbm,) * 4,
        scratch_shapes=[
            pltpu.VMEM((MESO, 9 * MESO), BF),
            pltpu.VMEM((TERR, 9 * TERR), BF),
            pltpu.VMEM((8, OQ, WIDE), F32),
            pltpu.VMEM((MIX, 2 * WIDE), BF),
            pltpu.VMEM((MESO, 9 * MESO), F32),
            pltpu.VMEM((TERR, 9 * TERR), F32),
            pltpu.VMEM((MESO, 9 * LEV), BF),
            pltpu.VMEM((MIX, 256), F32),
            pltpu.SemaphoreType.DMA((8,)),
            pltpu.SemaphoreType.DMA((16,)),
        ],
        input_output_aliases={1: 5, 2: 6},
        compiler_params=params(36),
        name="finish",
    )(place, *old, *parts, lift_copy, patch_turned, meso_weight, terrain_weight)
    return patch.T, terrain, lift, meso, merging, decoder, head


def packed(terrain_in, meso_in, wind_cot):
    samples, rows = meso_in.shape[0], meso_in.shape[3]
    source = lax.broadcasted_iota(jnp.int32, (2 * COLS, 2 * COLS), 0)
    target = lax.broadcasted_iota(jnp.int32, (2 * COLS, 2 * COLS), 1)
    pick = (source == 2 * (target % COLS) + target // COLS).astype(BF)
    split = dot(terrain_in.reshape(samples * 4 * rows, 2 * COLS), pick).astype(BF)
    patches = (
        split.reshape(samples, 2, rows, 2, 2, COLS)
        .transpose(0, 2, 1, 3, 4, 5)
        .reshape(samples, rows, 8, COLS)
    )
    levels = meso_in.reshape(samples, LEV, rows, COLS).transpose(0, 2, 1, 3)
    cot = wind_cot.transpose(0, 2, 1, 3)
    rest = jnp.zeros((samples, rows, PACK - LEV - 11, COLS), BF)
    return jnp.concatenate([levels, patches, cot, rest], axis=2)


def to_chip(v, by):
    return moved(v, lambda z, x, y, c: (z, x, y + by, c) if 0 <= y + by < 4 else None)


def local(
    terrain_in,
    meso_in,
    wind_cot,
    patch_weight,
    terrain_weight,
    lift_weight,
    meso_weight,
    merging_weight,
    decoder_weight,
    head_weight,
):
    own = packed(terrain_in, meso_in, wind_cot)
    place = jnp.stack([lax.axis_index(a) for a in ("segment", "space", "dp")]).astype(jnp.int32)
    eight, first, last = chip_rows(place, own, to_partner(own))
    above, below = to_chip(last, 1), to_chip(first, -1)
    small_ones = small_weights(lift_weight, patch_weight.T, head_weight)
    keep, send = main(
        place,
        above,
        eight,
        below,
        small_ones,
        meso_weight,
        terrain_weight,
        merging_weight,
        decoder_weight,
    )
    mine, theirs, written = summed_everywhere(place, keep, send)
    return finish(
        place, written, (*mine, *theirs), *small_ones[:2], meso_weight, terrain_weight
    )


def solution(mesh):
    placed = (
        P("dp", None, "space", None),
        P("dp", None, None, "space", None),
        P("dp", None, "space", None),
        P(),
        P(),
        P(),
        P(),
        P(),
        P(),
        P(),
    )
    return jax.shard_map(
        local,
        mesh=mesh,
        in_specs=placed,
        out_specs=(P(), P(), P(), P(), P(), P(), P()),
        check_vma=False,
    )
```

```python
import functools
import math

import jax
import jax.numpy as jnp
from jax import lax
from jax.experimental import pallas as pl
from jax.experimental.pallas import tpu as pltpu
from jax.sharding import PartitionSpec as P

BF = jnp.bfloat16
F32 = jnp.float32
TERR, MESO, MIX = 256, 384, 256
JOINT = TERR + MESO
LEV = 128
SLAB = 16
PACK = LEV + SLAB
ROWS, COLS = 8, 128
HALO = 5
OQ, MQ = MIX // 4, MESO // 4
WIDE = 1280
NT = (((1,), (1,)), ((), ()))


def dot(a, b):
    return jnp.dot(a, b, preferred_element_type=F32)


def dot_nt(a, b):
    return lax.dot_general(a, b, NT, preferred_element_type=F32)


def params(mib):
    return pltpu.CompilerParams(vmem_limit_bytes=mib * 1024 * 1024)


def sixteen(v, above):
    rows, width = v.shape
    parts = [v.astype(F32)]
    if above:
        parts.insert(0, jnp.zeros((above, width), F32))
    if above + rows < SLAB:
        parts.append(jnp.zeros((SLAB - above - rows, width), F32))
    return jnp.concatenate(parts, axis=0)


def small_kernel(lw, pw, hw, lw_out, pw_out, head_turned):
    lw_out[...] = lw[...]
    pw_out[...] = sixteen(pw[...], 0).astype(BF)
    head_turned[...] = sixteen(hw[...], 8).T.astype(BF)


def small_weights(lift_weight, patch_turned, head_weight):
    return pl.pallas_call(
        small_kernel,
        out_shape=(
            jax.ShapeDtypeStruct((MESO, LEV), BF),
            jax.ShapeDtypeStruct((SLAB, TERR), BF),
            jax.ShapeDtypeStruct((MIX, SLAB), BF),
        ),
        compiler_params=params(16),
        cost_estimate=pl.CostEstimate(flops=0, bytes_accessed=4_000_000, transcendentals=0),
        name="small_weights",
    )(lift_weight, patch_turned, head_weight)


def rows_kernel(place, own, partner, eight, first, last):
    core = place[1] % 2
    for c in range(2):

        @pl.when(core == c)
        def _(c=c):
            halves = (own, partner) if c == 0 else (partner, own)
            for r in range(ROWS):
                v = halves[r // 4][c, r % 4]
                eight[r] = v
                if r < HALO:
                    first[r] = v
                if r >= ROWS - HALO:
                    last[r - (ROWS - HALO)] = v


def chip_rows(place, own, partner):
    smem = pl.BlockSpec(memory_space=pltpu.SMEM)
    vmem = pl.BlockSpec(memory_space=pltpu.VMEM)
    return pl.pallas_call(
        rows_kernel,
        out_shape=tuple(
            jax.ShapeDtypeStruct((n, PACK, COLS), BF) for n in (ROWS, HALO, HALO)
        ),
        in_specs=[smem, vmem, vmem],
        out_specs=(vmem,) * 3,
        compiler_params=params(16),
        name="rows",
    )(place, own, partner)


def neighbours(v):
    width = v.shape[1]
    lane = lax.broadcasted_iota(jnp.int32, (1, width), 1) % COLS
    left, right = [], []
    for r in range(width // COLS):
        piece = v[:, r * COLS : (r + 1) * COLS]
        left.append(pltpu.roll(piece, 1, 1))
        right.append(pltpu.roll(piece, COLS - 1, 1))
    left = jnp.where(lane == 0, 0.0, jnp.concatenate(left, axis=1))
    right = jnp.where(lane == COLS - 1, 0.0, jnp.concatenate(right, axis=1))
    return left, right


def logistic(v):
    return 0.5 * (1.0 + jnp.tanh(0.5 * v))


def main_kernel(place, above, eight, below, lw, pw16, head_turned, *refs):
    n_w = 4
    weights_hbm, keep, send, out = refs[:n_w], *refs[n_w : n_w + 3]
    mw, tw, gw, dw = weights = refs[n_w + 3 : 2 * n_w + 3]
    sems, wm, wt, dt, gt = refs[2 * n_w + 3 : 2 * n_w + 8]
    x3, p9, j3, jslope, jdelta, m3, mslope, dout, d3, e3 = refs[2 * n_w + 8 :]
    copies = [
        pltpu.make_async_copy(u, v, sems.at[i]) for i, (u, v) in enumerate(zip(weights_hbm, weights))
    ]
    for copy in copies:
        copy.start()
    segment, depth = place[0], place[2]
    chip, core = place[1] // 2, place[1] % 2
    first_row = chip * ROWS

    def cut(row, rows):
        return slice(row * COLS, (row + rows) * COLS)

    def inside(row, rows):
        at = lax.broadcasted_iota(jnp.int32, (1, rows * COLS), 1) // COLS + row + first_row
        return jnp.logical_and(at >= 0, at < 4 * ROWS)

    def slab(r):
        for ref, rows in ((above, HALO), (eight, ROWS), (below, HALO)):
            if r < rows:
                return ref[r]
            r -= rows

    n_in, n_join = ROWS + 2 * HALO, ROWS + 8

    there = {0: (chip > 0).astype(F32), 1: (chip < 3).astype(F32)}
    for r in range(n_in):
        v = slab(r).astype(F32)
        if not HALO <= r < HALO + ROWS:
            v = v * there[r // (HALO + ROWS)]
        left, right = neighbours(v)
        for b, u in enumerate((left, v, right)):
            u = u.astype(BF)
            x3[b * LEV : (b + 1) * LEV, cut(r, 1)] = u[:LEV]
            for a in range(3):
                if a <= r < n_join + a:
                    tap = 3 * a + b
                    p9[tap * SLAB : (tap + 1) * SLAB, cut(r - a, 1)] = u[LEV:]

    copies[0].wait()
    for tap in range(9):
        wm[:, tap * LEV : (tap + 1) * LEV] = dot(
            mw[:, tap * MESO : (tap + 1) * MESO], lw[...]
        ).astype(BF)
    copies[1].wait()
    wt[...] = jnp.concatenate(
        [dot_nt(tw[:, tap * TERR : (tap + 1) * TERR], pw16[...]).astype(BF) for tap in range(9)], axis=1
    )

    for row in (0, 4, 8, 12):
        pre_t = dot(wt[...], p9[:, cut(row, 4)])
        pre_m = sum(
            dot(wm[:, a * 3 * LEV : (a + 1) * 3 * LEV], x3[:, cut(row + a, 4)]) for a in range(3)
        )
        for at, pre in ((0, pre_t), (TERR, pre_m)):
            size = pre.shape[0]
            sigma = logistic(pre)
            v = jnp.where(inside(row - 4, 4), pre * sigma, 0.0)
            left, right = neighbours(v)
            for b, u in enumerate((left, v, right)):
                j3[b * JOINT + at : b * JOINT + at + size, cut(row, 4)] = u.astype(BF)
            if row in (4, 8):
                jslope[at : at + size, cut(row - 4, 4)] = sigma * (1.0 + pre * (1.0 - sigma))

    copies[2].wait()
    copies[3].wait()
    for tap in range(9):
        gt[:, tap * MIX : (tap + 1) * MIX] = gw[:, tap * JOINT : (tap + 1) * JOINT].T
        dt[:, tap * MIX : (tap + 1) * MIX] = dw[:, tap * MIX : (tap + 1) * MIX].T

    for row, rows in ((0, 4), (4, 5), (9, 5)):
        pre = sum(
            dot(gw[:, a * 3 * JOINT : (a + 1) * 3 * JOINT], j3[:, cut(row + a, rows)])
            for a in range(3)
        )
        sigma = logistic(pre)
        v = jnp.where(inside(row - 3, rows), pre * sigma, 0.0)
        left, right = neighbours(v)
        for b, u in enumerate((left, v, right)):
            m3[b * MIX : (b + 1) * MIX, cut(row, rows)] = u.astype(BF)
        mslope[:, cut(row, rows)] = sigma * (1.0 + pre * (1.0 - sigma))

    scale = 1.0 / math.sqrt(8 * 32 * 128)

    for row in (0, 4, 8):
        pre = sum(
            dot(dw[:, a * 3 * MIX : (a + 1) * 3 * MIX], m3[:, cut(row + a, 4)]) for a in range(3)
        )
        sigma = logistic(pre)
        cot = jnp.concatenate([slab(row + 3 + r)[LEV:] for r in range(4)], axis=1)
        back = scale * dot(head_turned[...], cot)
        v = jnp.where(inside(row - 2, 4), sigma * (1.0 + pre * (1.0 - sigma)) * back, 0.0)
        left, right = neighbours(v)
        for b, u in enumerate((right, v, left)):
            d3[b * MIX : (b + 1) * MIX, cut(row, 4)] = u.astype(BF)
        lo, hi = max(row, 2), min(row + 4, 10)
        dout[:, cut(lo - 2, hi - lo)] = (pre * sigma)[:, cut(lo - row, hi - lo)].astype(BF)

    for row in (0, 5):
        back = sum(
            dot(dt[:, a * 3 * MIX : (a + 1) * 3 * MIX], d3[:, cut(row + 2 - a, 5)])
            for a in range(3)
        )
        v = jnp.where(inside(row - 1, 5), mslope[:, cut(row + 2, 5)] * back, 0.0)
        left, right = neighbours(v)
        for b, u in enumerate((right, v, left)):
            e3[b * MIX : (b + 1) * MIX, cut(row, 5)] = u.astype(BF)

    for row in (0, 4):
        back = sum(
            dot(gt[:, a * 3 * MIX : (a + 1) * 3 * MIX], e3[:, cut(row + 2 - a, 4)])
            for a in range(3)
        )
        jdelta[:, cut(row, 4)] = (jslope[:, cut(row, 4)] * back).astype(BF)

    def put(rows, column, value):
        value = value.astype(BF)
        width = value.shape[1]
        done = 0
        while done < width:
            group, offset = divmod(column + done, WIDE)
            take = min(width - done, WIDE - offset)
            along = chip if group < 4 else depth
            slot = 4 * lax.rem(core + group // 4, 2) + lax.rem(group % 4 + 4 - along, 4)
            out[slot, rows : rows + value.shape[0], offset : offset + take] = value[
                :, done : done + take
            ]
            done += take

    def stacked(delta):
        def zero(rows):
            return jnp.zeros((delta.shape[0], rows * COLS), BF)

        return jnp.concatenate(
            [
                jnp.concatenate([delta, zero(2)], axis=1),
                jnp.concatenate([zero(1), delta, zero(1)], axis=1),
                jnp.concatenate([zero(2), delta], axis=1),
            ],
            axis=0,
        )

    q = pl.ds(pl.multiple_of(segment * OQ, OQ), OQ)
    qd = pl.ds(pl.multiple_of(MIX + segment * OQ, OQ), OQ)
    qm = pl.ds(pl.multiple_of(TERR + segment * MQ, 32), MQ)
    d_own = stacked(d3[qd, cut(2, ROWS)])
    e_own = stacked(e3[qd, cut(1, ROWS)])
    h_own = stacked(jdelta[qm, :])
    for b in range(3):
        part = dot_nt(e_own, j3[b * JOINT : (b + 1) * JOINT, cut(3, ROWS + 2)])
        for a in range(3):
            put(0, (3 * a + b) * JOINT, part[a * OQ : (a + 1) * OQ])
    column = 9 * JOINT
    part = dot_nt(d_own, m3[:, cut(2, ROWS + 2)])
    for a in range(3):
        put(0, column + a * 3 * MIX, part[a * OQ : (a + 1) * OQ])
    column += 9 * MIX
    part = dot_nt(h_own, x3[:, cut(4, ROWS + 2)])
    for a in range(3):
        h = part[a * MQ : (a + 1) * MQ]
        put(0, column + a * 3 * LEV, h[:64])
        spare = column + 9 * LEV
        for c in range(3):
            at = a * 3 * LEV + c * LEV
            piece = h[64:, c * LEV : (c + 1) * LEV]
            if at < 640:
                put(0, spare + at, piece)
            else:
                put(32, spare + at - 640, piece)
    put(32, column + 9 * LEV + 512, jnp.zeros((32, 128), F32))
    column += 9 * LEV + 640
    g = dot_nt(jdelta[q, :], p9[:, cut(4, ROWS)])
    head = scale * dot_nt(
        dout[q, :], jnp.concatenate([eight[r, LEV:] for r in range(ROWS)], axis=1)
    )
    tail = 8 * WIDE - column
    put(0, column, jnp.concatenate([g, head, jnp.zeros((OQ, tail - 10 * SLAB), F32)], axis=1))
    keep[...] = out[:4]
    send[...] = out[4:]


def main(place, above, eight, below, small_ones, *weights):
    smem = pl.BlockSpec(memory_space=pltpu.SMEM)
    vmem = pl.BlockSpec(memory_space=pltpu.VMEM)
    hbm = pl.BlockSpec(memory_space=pltpu.HBM)
    return pl.pallas_call(
        main_kernel,
        out_shape=(jax.ShapeDtypeStruct((4, OQ, WIDE), BF),) * 2,
        in_specs=[smem] + [vmem] * 6 + [hbm] * len(weights),
        out_specs=(vmem, vmem),
        scratch_shapes=[
            pltpu.VMEM((8, OQ, WIDE), BF),
            *[pltpu.VMEM(w.shape, BF) for w in weights],
            pltpu.SemaphoreType.DMA((len(weights),)),
            pltpu.VMEM((MESO, 9 * LEV), BF),
            pltpu.VMEM((TERR, 9 * SLAB), BF),
            pltpu.VMEM((MIX, 9 * MIX), BF),
            pltpu.VMEM((JOINT, 9 * MIX), BF),
            pltpu.VMEM((3 * LEV, (ROWS + 2 * HALO) * COLS), BF),
            pltpu.VMEM((9 * SLAB, (ROWS + 8) * COLS), BF),
            pltpu.VMEM((3 * JOINT, (ROWS + 8) * COLS), BF),
            pltpu.VMEM((JOINT, ROWS * COLS), F32),
            pltpu.VMEM((JOINT, ROWS * COLS), BF),
            pltpu.VMEM((3 * MIX, (ROWS + 6) * COLS), BF),
            pltpu.VMEM((MIX, (ROWS + 6) * COLS), F32),
            pltpu.VMEM((MIX, ROWS * COLS), BF),
            pltpu.VMEM((3 * MIX, (ROWS + 4) * COLS), BF),
            pltpu.VMEM((3 * MIX, (ROWS + 2) * COLS), BF),
        ],
        compiler_params=params(51),
        cost_estimate=pl.CostEstimate(
            flops=15_000_000_000, bytes_accessed=12_000_000, transcendentals=3_000_000
        ),
        name="sections",
    )(place, above, eight, below, *small_ones, *weights)


def split_kernel(keep, came, own, next1, next2, next3):
    own[...] = keep[0].astype(F32) + came[0].astype(F32)
    for j, to in enumerate((next1, next2, next3), 1):
        to[...] = (keep[j].astype(F32) + came[j].astype(F32)).astype(BF)


def total_kernel(own, one, two, three, out):
    parts = [v[...].astype(F32) for v in (own, one, two, three)]
    out[...] = sum(parts[1:], parts[0]).astype(BF)


def pair_kernel(own, other, out):
    out[...] = (own[...].astype(F32) + other[...].astype(F32)).astype(BF)


def stack_kernel(own, one, two, three, out, half0, half1):
    for j, v in enumerate((own, one, two, three)):
        out[j] = v[...]
        (half0, half1)[j // 2][j % 2] = v[...]


def small(kernel, out_shape, *operands):
    return pl.pallas_call(
        kernel, out_shape=out_shape, compiler_params=params(16), name=kernel.__name__[:-7]
    )(*operands)


def moved(v, where):
    pairs = []
    for source in range(128):
        at = (source // 32, source // 8 % 4, source // 2 % 4, source % 2)
        to = where(*at)
        pairs.append((source, to[0] * 32 + to[1] * 8 + to[2] * 2 + to[3]))
    return lax.ppermute(v, ("dp", "segment", "space"), pairs)


DP, SEGMENT, CHIP = 0, 1, 2


def along(v, axes, by):
    def where(*at):
        to = list(at)
        to[axes[at[3]]] = (to[axes[at[3]]] + by) % 4
        return to

    return moved(v, where)


def across(v, axes, bits):
    def where(*at):
        to = list(at)
        to[axes[at[3]]] ^= bits
        return to

    return moved(v, where)


def to_partner(v):
    return moved(v, lambda z, x, y, c: (z, x, y, 1 - c))


PARTS = ((0, 0, 4), (-1, 0, 2), (-1, 2, 2), (1, 0, 2), (1, 2, 2), (-2, 0, 2), (-2, 2, 2))


def summed_everywhere(place, keep, send):
    piece = jax.ShapeDtypeStruct((OQ, WIDE), BF)
    wide = jax.ShapeDtypeStruct((OQ, WIDE), F32)
    turns = (1, 2, 3)
    own, *parts = small(split_kernel, (wide, piece, piece, piece), keep, to_partner(send))
    own = small(total_kernel, piece, own, *[along(p, (CHIP, DP), j) for p, j in zip(parts, turns)])
    for bits in (1, 3):
        own = small(pair_kernel, piece, own, across(own, (DP, CHIP), bits))
    four = jax.ShapeDtypeStruct((4, OQ, WIDE), BF)
    two = jax.ShapeDtypeStruct((2, OQ, WIDE), BF)
    block, half0, half1 = small(
        stack_kernel, (four, two, two), own, *[along(own, (CHIP, SEGMENT), j) for j in turns]
    )
    rings = (SEGMENT, DP)
    behind0, ahead1 = along(half0, rings, 1), along(half1, rings, -1)
    behind1, ahead0 = along(half1, rings, 1), along(half0, rings, -1)
    far0, far1 = along(behind0, rings, 1), along(ahead1, rings, -1)
    mine = (block, behind0, behind1, ahead0, ahead1, far0, far1)
    theirs = [to_partner(v) for v in mine[:5]]
    written, token = write_early(place, ((0, 0), (0, 1)), (block, theirs[0]))
    far0, token = lax.optimization_barrier((far0, token))
    theirs.append(to_partner(far0))
    theirs.append(to_partner(far1))
    written, token = write_early(
        place, ((1, 0), (2, 0), (3, 0), (4, 0)), mine[1:5], written, token
    )
    return mine[:5] + (far0, far1), theirs, (*written, token)


def origin(place, part, j, theirs):
    segment, chip, core, depth = place[0], place[1] // 2, place[1] % 2, place[2]
    step, first, _ = PARTS[part]
    kind = 1 - core if theirs else core
    group = jnp.where(
        kind == 0, lax.rem(chip - (first + j) + 4, 4), 4 + lax.rem(depth + step + 4, 4)
    )
    row = lax.rem(segment + jnp.where(kind == 0, step, -(first + j)) + 4, 4)
    return group, row


def write_out(place, which, refs, merging, decoder, stage, sems):
    chunks = []
    for (part, theirs), ref in zip(which, refs):
        for j in range(PARTS[part][2]):
            stage[len(chunks)] = ref[j].astype(F32)
            chunks.append((len(chunks), *origin(place, part, j, theirs)))

    def pieces(i, group, row):
        slot = stage.at[i]
        rows = pl.ds(pl.multiple_of(row * OQ, OQ), OQ)
        left = 9 * JOINT - 4 * WIDE
        last = 9 * MIX - (2 * WIDE - left)
        yield group < 4, [
            (slot, merging.at[rows, pl.ds(pl.multiple_of(group * WIDE, WIDE), WIDE)])
        ]
        yield group == 4, [
            (slot.at[:, :left], merging.at[rows, 4 * WIDE :]),
            (slot.at[:, left:], decoder.at[rows, : WIDE - left]),
        ]
        yield group == 5, [(slot, decoder.at[rows, WIDE - left : 2 * WIDE - left])]
        yield group == 6, [(slot.at[:, :last], decoder.at[rows, 2 * WIDE - left :])]

    def each(do):
        for i, group, row in chunks:
            for when, copies in pieces(i, group, row):

                @pl.when(when)
                def _(i=i, copies=copies):
                    for n, (source, target) in enumerate(copies):
                        do(pltpu.make_async_copy(source, target, sems.at[2 * i + n]))

    each(lambda copy: copy.start())
    return lambda: each(lambda copy: copy.wait())


def early_kernel(which, n_old, place, *refs):
    n = len(which)
    n_old += min(n_old, 1)
    parts, (merging, decoder, token, stage, sems) = refs[n_old : n_old + n], refs[n_old + n :]
    write_out(place, which, parts, merging, decoder, stage, sems)()
    token[...] = jnp.zeros(token.shape, F32)


def write_early(place, which, parts, old=(), *after):
    smem = pl.BlockSpec(memory_space=pltpu.SMEM)
    vmem = pl.BlockSpec(memory_space=pltpu.VMEM)
    hbm = pl.BlockSpec(memory_space=pltpu.HBM)
    chunks = sum(PARTS[part][2] for part, _ in which)
    *written, token = pl.pallas_call(
        functools.partial(early_kernel, which, len(old)),
        out_shape=(
            jax.ShapeDtypeStruct((MIX, 9 * JOINT), F32),
            jax.ShapeDtypeStruct((MIX, 9 * MIX), F32),
            jax.ShapeDtypeStruct((8, 128), F32),
        ),
        in_specs=[smem] + [hbm] * len(old) + [vmem] * (len(after) + len(parts)),
        out_specs=(hbm, hbm, vmem),
        scratch_shapes=[
            pltpu.VMEM((chunks, OQ, WIDE), F32),
            pltpu.SemaphoreType.DMA((2 * chunks,)),
        ],
        input_output_aliases={1 + i: i for i in range(len(old))},
        compiler_params=params(12),
        cost_estimate=pl.CostEstimate(flops=0, bytes_accessed=4_000_000, transcendentals=0),
        name="early",
    )(place, *old, *after, *parts)
    return written, token


LATE = ((1, 1), (2, 1), (3, 1), (4, 1), (5, 0), (6, 0), (5, 1), (6, 1))


def finish_kernel(place, *refs):
    n = len(PARTS)
    sides, refs = (refs[3 : 3 + n], refs[3 + n : 3 + 2 * n]), refs[3 + 2 * n :]
    lw, pw16, mw, tw = refs[:4]
    patch, lift, head, terrain, meso, merging, decoder = refs[4:11]
    stage, rest, wide_m, wide_t, ht, gt, sems, late_sems = refs[11:]
    late = [sides[theirs][part] for part, theirs in LATE]
    written = write_out(place, LATE, late, merging, decoder, stage, late_sems)
    for part in range(n):
        for theirs in range(2):
            for j in range(PARTS[part][2]):
                group, row = origin(place, part, j, theirs)

                @pl.when(group >= 6)
                def _(part=part, theirs=theirs, j=j, group=group, row=row):
                    rest[
                        pl.ds(pl.multiple_of(row * OQ, OQ), OQ),
                        pl.ds(pl.multiple_of((group - 6) * WIDE, WIDE), WIDE),
                    ] = sides[theirs][part][j]

    column = 9 * JOINT + 9 * MIX - 6 * WIDE
    writes = []
    for seg in range(4):
        lo = seg * OQ
        at = seg * MQ
        ht[at : at + 64, :] = rest[lo : lo + OQ, column : column + 9 * LEV]
        spare = column + 9 * LEV
        ht[at + 64 : at + MQ, :640] = rest[lo : lo + 32, spare : spare + 640]
        ht[at + 64 : at + MQ, 640:] = rest[lo + 32 : lo + OQ, spare : spare + 512]
        gt[lo : lo + OQ, :] = rest[lo : lo + OQ, spare + 640 : spare + 896].astype(F32)
    g = gt[...]
    for tap in range(9):
        part = slice(tap * MESO, (tap + 1) * MESO)
        wide_m[:, part] = dot_nt(ht[:, tap * LEV : (tap + 1) * LEV], lw[...])
        writes.append(pltpu.make_async_copy(wide_m.at[:, part], meso.at[:, part], sems.at[tap]))
        writes[-1].start()
    for tap in range(9):
        part = slice(tap * TERR, (tap + 1) * TERR)
        wide_t[:, part] = dot(g[:, tap * SLAB : (tap + 1) * SLAB].astype(BF), pw16[...])
        writes.append(pltpu.make_async_copy(wide_t.at[:, part], terrain.at[:, part], sems.at[9 + tap]))
        writes[-1].start()
    turned = g.T
    head[...] = turned[9 * SLAB + 8 : 9 * SLAB + 11, :]
    patch[...] = sum(
        dot(
            turned[tap * SLAB : (tap + 1) * SLAB, :].astype(BF),
            tw[:, tap * TERR : (tap + 1) * TERR],
        )
        for tap in range(9)
    )[:8]
    turned = ht[...].astype(F32).T.astype(BF)
    lift[...] = sum(
        dot(turned[tap * LEV : (tap + 1) * LEV, :], mw[:, tap * MESO : (tap + 1) * MESO])
        for tap in range(9)
    ).T
    for copy in writes:
        copy.wait()
    written()


def finish(place, old, parts, lift_copy, patch_turned, meso_weight, terrain_weight):
    smem = pl.BlockSpec(memory_space=pltpu.SMEM)
    vmem = pl.BlockSpec(memory_space=pltpu.VMEM)
    hbm = pl.BlockSpec(memory_space=pltpu.HBM)
    patch, lift, head, terrain, meso, merging, decoder = pl.pallas_call(
        finish_kernel,
        out_shape=(
            jax.ShapeDtypeStruct((8, TERR), F32),
            jax.ShapeDtypeStruct((MESO, LEV), F32),
            jax.ShapeDtypeStruct((3, MIX), F32),
            jax.ShapeDtypeStruct((TERR, 9 * TERR), F32),
            jax.ShapeDtypeStruct((MESO, 9 * MESO), F32),
            jax.ShapeDtypeStruct((MIX, 9 * JOINT), F32),
            jax.ShapeDtypeStruct((MIX, 9 * MIX), F32),
        ),
        in_specs=[smem] + [hbm] * 2 + [vmem] * (5 + len(parts)),
        out_specs=(vmem,) * 3 + (hbm,) * 4,
        scratch_shapes=[
            pltpu.VMEM((16, OQ, WIDE), F32),
            pltpu.VMEM((MIX, 2 * WIDE), BF),
            pltpu.VMEM((MESO, 9 * MESO), F32),
            pltpu.VMEM((TERR, 9 * TERR), F32),
            pltpu.VMEM((MESO, 9 * LEV), BF),
            pltpu.VMEM((MIX, 256), F32),
            pltpu.SemaphoreType.DMA((18,)),
            pltpu.SemaphoreType.DMA((32,)),
        ],
        input_output_aliases={1: 5, 2: 6},
        compiler_params=params(36),
        name="finish",
    )(place, *old, *parts, lift_copy, patch_turned, meso_weight, terrain_weight)
    return patch.T, terrain, lift, meso, merging, decoder, head


def packed(terrain_in, meso_in, wind_cot):
    samples, rows = meso_in.shape[0], meso_in.shape[3]
    source = lax.broadcasted_iota(jnp.int32, (2 * COLS, 2 * COLS), 0)
    target = lax.broadcasted_iota(jnp.int32, (2 * COLS, 2 * COLS), 1)
    pick = (source == 2 * (target % COLS) + target // COLS).astype(BF)
    split = dot(terrain_in.reshape(samples * 4 * rows, 2 * COLS), pick).astype(BF)
    patches = (
        split.reshape(samples, 2, rows, 2, 2, COLS)
        .transpose(0, 2, 1, 3, 4, 5)
        .reshape(samples, rows, 8, COLS)
    )
    levels = meso_in.reshape(samples, LEV, rows, COLS).transpose(0, 2, 1, 3)
    cot = wind_cot.transpose(0, 2, 1, 3)
    rest = jnp.zeros((samples, rows, PACK - LEV - 11, COLS), BF)
    return jnp.concatenate([levels, patches, cot, rest], axis=2)


def to_chip(v, by):
    return along(v, (CHIP, CHIP), by)


def local(
    terrain_in,
    meso_in,
    wind_cot,
    patch_weight,
    terrain_weight,
    lift_weight,
    meso_weight,
    merging_weight,
    decoder_weight,
    head_weight,
):
    own = packed(terrain_in, meso_in, wind_cot)
    place = jnp.stack([lax.axis_index(a) for a in ("segment", "space", "dp")]).astype(jnp.int32)
    eight, first, last = chip_rows(place, own, to_partner(own))
    above, below = to_chip(last, 1), to_chip(first, -1)
    small_ones = small_weights(lift_weight, patch_weight.T, head_weight)
    keep, send = main(
        place,
        above,
        eight,
        below,
        small_ones,
        meso_weight,
        terrain_weight,
        merging_weight,
        decoder_weight,
    )
    mine, theirs, written = summed_everywhere(place, keep, send)
    return finish(
        place, written, (*mine, *theirs), *small_ones[:2], meso_weight, terrain_weight
    )


def solution(mesh):
    placed = (
        P("dp", None, "space", None),
        P("dp", None, None, "space", None),
        P("dp", None, "space", None),
        P(),
        P(),
        P(),
        P(),
        P(),
        P(),
        P(),
    )
    return jax.shard_map(
        local,
        mesh=mesh,
        in_specs=placed,
        out_specs=(P(), P(), P(), P(), P(), P(), P()),
        check_vma=False,
    )
```

```python
import functools
import math

import jax
import jax.numpy as jnp
from jax import lax
from jax.experimental import pallas as pl
from jax.experimental.pallas import tpu as pltpu
from jax.sharding import PartitionSpec as P

BF = jnp.bfloat16
F32 = jnp.float32
TERR, MESO, MIX = 256, 384, 256
JOINT = TERR + MESO
LEV = 128
SLAB = 16
PACK = LEV + SLAB
ROWS, COLS = 8, 128
HALO = 5
OQ, MQ = MIX // 4, MESO // 4
WIDE = 1280
NT = (((1,), (1,)), ((), ()))


def dot(a, b):
    return jnp.dot(a, b, preferred_element_type=F32)


def dot_nt(a, b):
    return lax.dot_general(a, b, NT, preferred_element_type=F32)


def params(mib):
    return pltpu.CompilerParams(vmem_limit_bytes=mib * 1024 * 1024)


def sixteen(v, above):
    rows, width = v.shape
    parts = [v.astype(F32)]
    if above:
        parts.insert(0, jnp.zeros((above, width), F32))
    if above + rows < SLAB:
        parts.append(jnp.zeros((SLAB - above - rows, width), F32))
    return jnp.concatenate(parts, axis=0)


def small_kernel(lw, pw, hw, lw_out, pw_out, head_turned):
    lw_out[...] = lw[...]
    pw_out[...] = sixteen(pw[...], 0).astype(BF)
    head_turned[...] = sixteen(hw[...], 8).T.astype(BF)


def small_weights(lift_weight, patch_turned, head_weight):
    return pl.pallas_call(
        small_kernel,
        out_shape=(
            jax.ShapeDtypeStruct((MESO, LEV), BF),
            jax.ShapeDtypeStruct((SLAB, TERR), BF),
            jax.ShapeDtypeStruct((MIX, SLAB), BF),
        ),
        compiler_params=params(16),
        cost_estimate=pl.CostEstimate(flops=0, bytes_accessed=4_000_000, transcendentals=0),
        name="small_weights",
    )(lift_weight, patch_turned, head_weight)


def rows_kernel(place, own, partner, eight, first, last):
    core = place[1] % 2
    for c in range(2):

        @pl.when(core == c)
        def _(c=c):
            halves = (own, partner) if c == 0 else (partner, own)
            for r in range(ROWS):
                v = halves[r // 4][c, r % 4]
                eight[r] = v
                if r < HALO:
                    first[r] = v
                if r >= ROWS - HALO:
                    last[r - (ROWS - HALO)] = v


def chip_rows(place, own, partner):
    smem = pl.BlockSpec(memory_space=pltpu.SMEM)
    vmem = pl.BlockSpec(memory_space=pltpu.VMEM)
    return pl.pallas_call(
        rows_kernel,
        out_shape=tuple(
            jax.ShapeDtypeStruct((n, PACK, COLS), BF) for n in (ROWS, HALO, HALO)
        ),
        in_specs=[smem, vmem, vmem],
        out_specs=(vmem,) * 3,
        compiler_params=params(16),
        name="rows",
    )(place, own, partner)


def neighbours(v):
    width = v.shape[1]
    lane = lax.broadcasted_iota(jnp.int32, (1, width), 1) % COLS
    left, right = [], []
    for r in range(width // COLS):
        piece = v[:, r * COLS : (r + 1) * COLS]
        left.append(pltpu.roll(piece, 1, 1))
        right.append(pltpu.roll(piece, COLS - 1, 1))
    left = jnp.where(lane == 0, 0.0, jnp.concatenate(left, axis=1))
    right = jnp.where(lane == COLS - 1, 0.0, jnp.concatenate(right, axis=1))
    return left, right


def logistic(v):
    return 0.5 * (1.0 + jnp.tanh(0.5 * v))


def main_kernel(place, above, eight, below, lw, pw16, head_turned, *refs):
    n_w = 4
    weights_hbm, keep, send, out = refs[:n_w], *refs[n_w : n_w + 3]
    mw, tw, gw, dw = weights = refs[n_w + 3 : 2 * n_w + 3]
    sems, wm, wt, dt, gt = refs[2 * n_w + 3 : 2 * n_w + 8]
    x3, p9, j3, jslope, jdelta, m3, mslope, dout, d3, e3 = refs[2 * n_w + 8 :]
    copies = [
        pltpu.make_async_copy(u, v, sems.at[i]) for i, (u, v) in enumerate(zip(weights_hbm, weights))
    ]
    for copy in copies:
        copy.start()
    segment, depth = place[0], place[2]
    chip, core = place[1] // 2, place[1] % 2
    first_row = chip * ROWS

    def cut(row, rows):
        return slice(row * COLS, (row + rows) * COLS)

    def inside(row, rows):
        at = lax.broadcasted_iota(jnp.int32, (1, rows * COLS), 1) // COLS + row + first_row
        return jnp.logical_and(at >= 0, at < 4 * ROWS)

    def slab(r):
        for ref, rows in ((above, HALO), (eight, ROWS), (below, HALO)):
            if r < rows:
                return ref[r]
            r -= rows

    n_in, n_join = ROWS + 2 * HALO, ROWS + 8

    there = {0: (chip > 0).astype(F32), 1: (chip < 3).astype(F32)}
    for r in range(n_in):
        v = slab(r).astype(F32)
        if not HALO <= r < HALO + ROWS:
            v = v * there[r // (HALO + ROWS)]
        left, right = neighbours(v)
        for b, u in enumerate((left, v, right)):
            u = u.astype(BF)
            x3[b * LEV : (b + 1) * LEV, cut(r, 1)] = u[:LEV]
            for a in range(3):
                if a <= r < n_join + a:
                    tap = 3 * a + b
                    p9[tap * SLAB : (tap + 1) * SLAB, cut(r - a, 1)] = u[LEV:]

    copies[0].wait()
    for tap in range(9):
        wm[:, tap * LEV : (tap + 1) * LEV] = dot(
            mw[:, tap * MESO : (tap + 1) * MESO], lw[...]
        ).astype(BF)
    copies[1].wait()
    wt[...] = jnp.concatenate(
        [dot_nt(tw[:, tap * TERR : (tap + 1) * TERR], pw16[...]).astype(BF) for tap in range(9)], axis=1
    )

    for row in (0, 4, 8, 12):
        pre_t = dot(wt[...], p9[:, cut(row, 4)])
        pre_m = sum(
            dot(wm[:, a * 3 * LEV : (a + 1) * 3 * LEV], x3[:, cut(row + a, 4)]) for a in range(3)
        )
        for at, pre in ((0, pre_t), (TERR, pre_m)):
            size = pre.shape[0]
            sigma = logistic(pre)
            v = jnp.where(inside(row - 4, 4), pre * sigma, 0.0)
            left, right = neighbours(v)
            for b, u in enumerate((left, v, right)):
                j3[b * JOINT + at : b * JOINT + at + size, cut(row, 4)] = u.astype(BF)
            if row in (4, 8):
                jslope[at : at + size, cut(row - 4, 4)] = sigma * (1.0 + pre * (1.0 - sigma))

    copies[2].wait()
    copies[3].wait()
    for tap in range(9):
        gt[:, tap * MIX : (tap + 1) * MIX] = gw[:, tap * JOINT : (tap + 1) * JOINT].T
        dt[:, tap * MIX : (tap + 1) * MIX] = dw[:, tap * MIX : (tap + 1) * MIX].T

    for row, rows in ((0, 4), (4, 5), (9, 5)):
        pre = sum(
            dot(gw[:, a * 3 * JOINT : (a + 1) * 3 * JOINT], j3[:, cut(row + a, rows)])
            for a in range(3)
        )
        sigma = logistic(pre)
        v = jnp.where(inside(row - 3, rows), pre * sigma, 0.0)
        left, right = neighbours(v)
        for b, u in enumerate((left, v, right)):
            m3[b * MIX : (b + 1) * MIX, cut(row, rows)] = u.astype(BF)
        mslope[:, cut(row, rows)] = sigma * (1.0 + pre * (1.0 - sigma))

    scale = 1.0 / math.sqrt(8 * 32 * 128)

    for row in (0, 4, 8):
        pre = sum(
            dot(dw[:, a * 3 * MIX : (a + 1) * 3 * MIX], m3[:, cut(row + a, 4)]) for a in range(3)
        )
        sigma = logistic(pre)
        cot = jnp.concatenate([slab(row + 3 + r)[LEV:] for r in range(4)], axis=1)
        back = scale * dot(head_turned[...], cot)
        v = jnp.where(inside(row - 2, 4), sigma * (1.0 + pre * (1.0 - sigma)) * back, 0.0)
        left, right = neighbours(v)
        for b, u in enumerate((right, v, left)):
            d3[b * MIX : (b + 1) * MIX, cut(row, 4)] = u.astype(BF)
        lo, hi = max(row, 2), min(row + 4, 10)
        dout[:, cut(lo - 2, hi - lo)] = (pre * sigma)[:, cut(lo - row, hi - lo)].astype(BF)

    for row in (0, 5):
        back = sum(
            dot(dt[:, a * 3 * MIX : (a + 1) * 3 * MIX], d3[:, cut(row + 2 - a, 5)])
            for a in range(3)
        )
        v = jnp.where(inside(row - 1, 5), mslope[:, cut(row + 2, 5)] * back, 0.0)
        left, right = neighbours(v)
        for b, u in enumerate((right, v, left)):
            e3[b * MIX : (b + 1) * MIX, cut(row, 5)] = u.astype(BF)

    for row in (0, 4):
        back = sum(
            dot(gt[:, a * 3 * MIX : (a + 1) * 3 * MIX], e3[:, cut(row + 2 - a, 4)])
            for a in range(3)
        )
        jdelta[:, cut(row, 4)] = (jslope[:, cut(row, 4)] * back).astype(BF)

    def put(rows, column, value):
        value = value.astype(BF)
        width = value.shape[1]
        done = 0
        while done < width:
            group, offset = divmod(column + done, WIDE)
            take = min(width - done, WIDE - offset)
            along = chip if group < 4 else depth
            slot = 4 * lax.rem(core + group // 4, 2) + lax.rem(group % 4 + 4 - along, 4)
            out[slot, rows : rows + value.shape[0], offset : offset + take] = value[
                :, done : done + take
            ]
            done += take

    def stacked(delta):
        def zero(rows):
            return jnp.zeros((delta.shape[0], rows * COLS), BF)

        return jnp.concatenate(
            [
                jnp.concatenate([delta, zero(2)], axis=1),
                jnp.concatenate([zero(1), delta, zero(1)], axis=1),
                jnp.concatenate([zero(2), delta], axis=1),
            ],
            axis=0,
        )

    q = pl.ds(pl.multiple_of(segment * OQ, OQ), OQ)
    qd = pl.ds(pl.multiple_of(MIX + segment * OQ, OQ), OQ)
    qm = pl.ds(pl.multiple_of(TERR + segment * MQ, 32), MQ)
    d_own = stacked(d3[qd, cut(2, ROWS)])
    e_own = stacked(e3[qd, cut(1, ROWS)])
    h_own = stacked(jdelta[qm, :])
    for b in range(3):
        part = dot_nt(e_own, j3[b * JOINT : (b + 1) * JOINT, cut(3, ROWS + 2)])
        for a in range(3):
            put(0, (3 * a + b) * JOINT, part[a * OQ : (a + 1) * OQ])
    column = 9 * JOINT
    part = dot_nt(d_own, m3[:, cut(2, ROWS + 2)])
    for a in range(3):
        put(0, column + a * 3 * MIX, part[a * OQ : (a + 1) * OQ])
    column += 9 * MIX
    part = dot_nt(h_own, x3[:, cut(4, ROWS + 2)])
    for a in range(3):
        h = part[a * MQ : (a + 1) * MQ]
        put(0, column + a * 3 * LEV, h[:64])
        spare = column + 9 * LEV
        for c in range(3):
            at = a * 3 * LEV + c * LEV
            piece = h[64:, c * LEV : (c + 1) * LEV]
            if at < 640:
                put(0, spare + at, piece)
            else:
                put(32, spare + at - 640, piece)
    put(32, column + 9 * LEV + 512, jnp.zeros((32, 128), F32))
    column += 9 * LEV + 640
    g = dot_nt(jdelta[q, :], p9[:, cut(4, ROWS)])
    head = scale * dot_nt(
        dout[q, :], jnp.concatenate([eight[r, LEV:] for r in range(ROWS)], axis=1)
    )
    tail = 8 * WIDE - column
    put(0, column, jnp.concatenate([g, head, jnp.zeros((OQ, tail - 10 * SLAB), F32)], axis=1))
    keep[...] = out[:4]
    send[...] = out[4:]


def main(place, above, eight, below, small_ones, *weights):
    smem = pl.BlockSpec(memory_space=pltpu.SMEM)
    vmem = pl.BlockSpec(memory_space=pltpu.VMEM)
    hbm = pl.BlockSpec(memory_space=pltpu.HBM)
    return pl.pallas_call(
        main_kernel,
        out_shape=(jax.ShapeDtypeStruct((4, OQ, WIDE), BF),) * 2,
        in_specs=[smem] + [vmem] * 6 + [hbm] * len(weights),
        out_specs=(vmem, vmem),
        scratch_shapes=[
            pltpu.VMEM((8, OQ, WIDE), BF),
            *[pltpu.VMEM(w.shape, BF) for w in weights],
            pltpu.SemaphoreType.DMA((len(weights),)),
            pltpu.VMEM((MESO, 9 * LEV), BF),
            pltpu.VMEM((TERR, 9 * SLAB), BF),
            pltpu.VMEM((MIX, 9 * MIX), BF),
            pltpu.VMEM((JOINT, 9 * MIX), BF),
            pltpu.VMEM((3 * LEV, (ROWS + 2 * HALO) * COLS), BF),
            pltpu.VMEM((9 * SLAB, (ROWS + 8) * COLS), BF),
            pltpu.VMEM((3 * JOINT, (ROWS + 8) * COLS), BF),
            pltpu.VMEM((JOINT, ROWS * COLS), F32),
            pltpu.VMEM((JOINT, ROWS * COLS), BF),
            pltpu.VMEM((3 * MIX, (ROWS + 6) * COLS), BF),
            pltpu.VMEM((MIX, (ROWS + 6) * COLS), F32),
            pltpu.VMEM((MIX, ROWS * COLS), BF),
            pltpu.VMEM((3 * MIX, (ROWS + 4) * COLS), BF),
            pltpu.VMEM((3 * MIX, (ROWS + 2) * COLS), BF),
        ],
        compiler_params=params(51),
        cost_estimate=pl.CostEstimate(
            flops=15_000_000_000, bytes_accessed=12_000_000, transcendentals=3_000_000
        ),
        name="sections",
    )(place, above, eight, below, *small_ones, *weights)


def split_kernel(keep, came, own, next1, next2, next3):
    own[...] = keep[0].astype(F32) + came[0].astype(F32)
    for j, to in enumerate((next1, next2, next3), 1):
        to[...] = (keep[j].astype(F32) + came[j].astype(F32)).astype(BF)


def total_kernel(own, one, two, three, out):
    out[...] = (
        (own[...].astype(F32) + two[...].astype(F32))
        + (one[...].astype(F32) + three[...].astype(F32))
    ).astype(BF)


def stack_kernel(own, one, two, three, out, half0, half1):
    for j, v in enumerate((own, one, two, three)):
        out[j] = v[...]
        (half0, half1)[j // 2][j % 2] = v[...]


def small(kernel, out_shape, *operands):
    return pl.pallas_call(
        kernel, out_shape=out_shape, compiler_params=params(16), name=kernel.__name__[:-7]
    )(*operands)


def moved(v, where):
    pairs = []
    for source in range(128):
        at = (source // 32, source // 8 % 4, source // 2 % 4, source % 2)
        to = where(*at)
        pairs.append((source, to[0] * 32 + to[1] * 8 + to[2] * 2 + to[3]))
    return lax.ppermute(v, ("dp", "segment", "space"), pairs)


DP, SEGMENT, CHIP = 0, 1, 2


def along(v, axes, by):
    def where(*at):
        to = list(at)
        to[axes[at[3]]] = (to[axes[at[3]]] + by) % 4
        return to

    return moved(v, where)


def to_partner(v):
    return moved(v, lambda z, x, y, c: (z, x, y, 1 - c))


PARTS = ((0, 0, 4), (-1, 0, 2), (-1, 2, 2), (1, 0, 2), (1, 2, 2), (-2, 0, 2), (-2, 2, 2))


def summed_everywhere(place, keep, send):
    piece = jax.ShapeDtypeStruct((OQ, WIDE), BF)
    wide = jax.ShapeDtypeStruct((OQ, WIDE), F32)
    turns = (1, 2, 3)
    own, *parts = small(split_kernel, (wide, piece, piece, piece), keep, to_partner(send))
    own = small(total_kernel, piece, own, *[along(p, (CHIP, DP), j) for p, j in zip(parts, turns)])
    own = small(total_kernel, piece, own, *[along(own, (DP, CHIP), j) for j in turns])
    four = jax.ShapeDtypeStruct((4, OQ, WIDE), BF)
    two = jax.ShapeDtypeStruct((2, OQ, WIDE), BF)
    block, half0, half1 = small(
        stack_kernel, (four, two, two), own, *[along(own, (CHIP, SEGMENT), j) for j in turns]
    )
    rings = (SEGMENT, DP)
    behind0, ahead1 = along(half0, rings, 1), along(half1, rings, -1)
    behind1, ahead0 = along(half1, rings, 1), along(half0, rings, -1)
    far0, far1 = along(behind0, rings, 1), along(ahead1, rings, -1)
    mine = (block, behind0, behind1, ahead0, ahead1, far0, far1)
    theirs = [to_partner(v) for v in mine[:5]]
    written, token = write_early(
        place, ((0, 0), (0, 1), (1, 0), (4, 0)), (block, theirs[0], behind0, ahead1)
    )
    far0, token = lax.optimization_barrier((far0, token))
    theirs.append(to_partner(far0))
    theirs.append(to_partner(far1))
    written, token = write_early(
        place,
        ((2, 0), (3, 0), (1, 1), (4, 1)),
        (behind1, ahead0, theirs[1], theirs[4]),
        written,
        token,
    )
    return mine[:5] + (far0, far1), theirs, (*written, token)


def origin(place, part, j, theirs):
    segment, chip, core, depth = place[0], place[1] // 2, place[1] % 2, place[2]
    step, first, _ = PARTS[part]
    kind = 1 - core if theirs else core
    group = jnp.where(
        kind == 0, lax.rem(chip - (first + j) + 4, 4), 4 + lax.rem(depth + step + 4, 4)
    )
    row = lax.rem(segment + jnp.where(kind == 0, step, -(first + j)) + 4, 4)
    return group, row


def write_out(place, which, refs, merging, decoder, stage, sems):
    chunks = []
    for (part, theirs), ref in zip(which, refs):
        for j in range(PARTS[part][2]):
            stage[len(chunks)] = ref[j].astype(F32)
            chunks.append((len(chunks), *origin(place, part, j, theirs)))

    def pieces(i, group, row):
        slot = stage.at[i]
        rows = pl.ds(pl.multiple_of(row * OQ, OQ), OQ)
        left = 9 * JOINT - 4 * WIDE
        last = 9 * MIX - (2 * WIDE - left)
        yield group < 4, [
            (slot, merging.at[rows, pl.ds(pl.multiple_of(group * WIDE, WIDE), WIDE)])
        ]
        yield group == 4, [
            (slot.at[:, :left], merging.at[rows, 4 * WIDE :]),
            (slot.at[:, left:], decoder.at[rows, : WIDE - left]),
        ]
        yield group == 5, [(slot, decoder.at[rows, WIDE - left : 2 * WIDE - left])]
        yield group == 6, [(slot.at[:, :last], decoder.at[rows, 2 * WIDE - left :])]

    def each(do):
        for i, group, row in chunks:
            for when, copies in pieces(i, group, row):

                @pl.when(when)
                def _(i=i, copies=copies):
                    for n, (source, target) in enumerate(copies):
                        do(pltpu.make_async_copy(source, target, sems.at[2 * i + n]))

    each(lambda copy: copy.start())
    return lambda: each(lambda copy: copy.wait())


def early_kernel(which, n_old, place, *refs):
    n = len(which)
    n_old += min(n_old, 1)
    parts, (merging, decoder, token, stage, sems) = refs[n_old : n_old + n], refs[n_old + n :]
    write_out(place, which, parts, merging, decoder, stage, sems)()
    token[...] = jnp.zeros(token.shape, F32)


def write_early(place, which, parts, old=(), *after):
    smem = pl.BlockSpec(memory_space=pltpu.SMEM)
    vmem = pl.BlockSpec(memory_space=pltpu.VMEM)
    hbm = pl.BlockSpec(memory_space=pltpu.HBM)
    chunks = sum(PARTS[part][2] for part, _ in which)
    *written, token = pl.pallas_call(
        functools.partial(early_kernel, which, len(old)),
        out_shape=(
            jax.ShapeDtypeStruct((MIX, 9 * JOINT), F32),
            jax.ShapeDtypeStruct((MIX, 9 * MIX), F32),
            jax.ShapeDtypeStruct((8, 128), F32),
        ),
        in_specs=[smem] + [hbm] * len(old) + [vmem] * (len(after) + len(parts)),
        out_specs=(hbm, hbm, vmem),
        scratch_shapes=[
            pltpu.VMEM((chunks, OQ, WIDE), F32),
            pltpu.SemaphoreType.DMA((2 * chunks,)),
        ],
        input_output_aliases={1 + i: i for i in range(len(old))},
        compiler_params=params(12),
        cost_estimate=pl.CostEstimate(flops=0, bytes_accessed=4_000_000, transcendentals=0),
        name="early",
    )(place, *old, *after, *parts)
    return written, token


LATE = ((2, 1), (3, 1), (5, 0), (6, 0), (5, 1), (6, 1))


def finish_kernel(place, *refs):
    n = len(PARTS)
    sides, refs = (refs[3 : 3 + n], refs[3 + n : 3 + 2 * n]), refs[3 + 2 * n :]
    lw, pw16, mw, tw = refs[:4]
    patch, lift, head, terrain, meso, merging, decoder = refs[4:11]
    stage, rest, wide_m, wide_t, ht, gt, sems, late_sems = refs[11:]
    late = [sides[theirs][part] for part, theirs in LATE]
    written = write_out(place, LATE, late, merging, decoder, stage, late_sems)
    for part in range(n):
        for theirs in range(2):
            for j in range(PARTS[part][2]):
                group, row = origin(place, part, j, theirs)

                @pl.when(group >= 6)
                def _(part=part, theirs=theirs, j=j, group=group, row=row):
                    rest[
                        pl.ds(pl.multiple_of(row * OQ, OQ), OQ),
                        pl.ds(pl.multiple_of((group - 6) * WIDE, WIDE), WIDE),
                    ] = sides[theirs][part][j]

    column = 9 * JOINT + 9 * MIX - 6 * WIDE
    writes = []
    for seg in range(4):
        lo = seg * OQ
        at = seg * MQ
        ht[at : at + 64, :] = rest[lo : lo + OQ, column : column + 9 * LEV]
        spare = column + 9 * LEV
        ht[at + 64 : at + MQ, :640] = rest[lo : lo + 32, spare : spare + 640]
        ht[at + 64 : at + MQ, 640:] = rest[lo + 32 : lo + OQ, spare : spare + 512]
        gt[lo : lo + OQ, :] = rest[lo : lo + OQ, spare + 640 : spare + 896].astype(F32)
    g = gt[...]
    for tap in range(9):
        part = slice(tap * MESO, (tap + 1) * MESO)
        wide_m[:, part] = dot_nt(ht[:, tap * LEV : (tap + 1) * LEV], lw[...])
        writes.append(pltpu.make_async_copy(wide_m.at[:, part], meso.at[:, part], sems.at[tap]))
        writes[-1].start()
    for tap in range(9):
        part = slice(tap * TERR, (tap + 1) * TERR)
        wide_t[:, part] = dot(g[:, tap * SLAB : (tap + 1) * SLAB].astype(BF), pw16[...])
        writes.append(pltpu.make_async_copy(wide_t.at[:, part], terrain.at[:, part], sems.at[9 + tap]))
        writes[-1].start()
    turned = g.T
    head[...] = turned[9 * SLAB + 8 : 9 * SLAB + 11, :]
    patch[...] = sum(
        dot(
            turned[tap * SLAB : (tap + 1) * SLAB, :].astype(BF),
            tw[:, tap * TERR : (tap + 1) * TERR],
        )
        for tap in range(9)
    )[:8]
    turned = ht[...].astype(F32).T.astype(BF)
    lift[...] = sum(
        dot(turned[tap * LEV : (tap + 1) * LEV, :], mw[:, tap * MESO : (tap + 1) * MESO])
        for tap in range(9)
    ).T
    for copy in writes:
        copy.wait()
    written()


def finish(place, old, parts, lift_copy, patch_turned, meso_weight, terrain_weight):
    smem = pl.BlockSpec(memory_space=pltpu.SMEM)
    vmem = pl.BlockSpec(memory_space=pltpu.VMEM)
    hbm = pl.BlockSpec(memory_space=pltpu.HBM)
    patch, lift, head, terrain, meso, merging, decoder = pl.pallas_call(
        finish_kernel,
        out_shape=(
            jax.ShapeDtypeStruct((8, TERR), F32),
            jax.ShapeDtypeStruct((MESO, LEV), F32),
            jax.ShapeDtypeStruct((3, MIX), F32),
            jax.ShapeDtypeStruct((TERR, 9 * TERR), F32),
            jax.ShapeDtypeStruct((MESO, 9 * MESO), F32),
            jax.ShapeDtypeStruct((MIX, 9 * JOINT), F32),
            jax.ShapeDtypeStruct((MIX, 9 * MIX), F32),
        ),
        in_specs=[smem] + [hbm] * 2 + [vmem] * (5 + len(parts)),
        out_specs=(vmem,) * 3 + (hbm,) * 4,
        scratch_shapes=[
            pltpu.VMEM((12, OQ, WIDE), F32),
            pltpu.VMEM((MIX, 2 * WIDE), BF),
            pltpu.VMEM((MESO, 9 * MESO), F32),
            pltpu.VMEM((TERR, 9 * TERR), F32),
            pltpu.VMEM((MESO, 9 * LEV), BF),
            pltpu.VMEM((MIX, 256), F32),
            pltpu.SemaphoreType.DMA((18,)),
            pltpu.SemaphoreType.DMA((24,)),
        ],
        input_output_aliases={1: 5, 2: 6},
        compiler_params=params(36),
        name="finish",
    )(place, *old, *parts, lift_copy, patch_turned, meso_weight, terrain_weight)
    return patch.T, terrain, lift, meso, merging, decoder, head


def packed(terrain_in, meso_in, wind_cot):
    samples, rows = meso_in.shape[0], meso_in.shape[3]
    source = lax.broadcasted_iota(jnp.int32, (2 * COLS, 2 * COLS), 0)
    target = lax.broadcasted_iota(jnp.int32, (2 * COLS, 2 * COLS), 1)
    pick = (source == 2 * (target % COLS) + target // COLS).astype(BF)
    split = dot(terrain_in.reshape(samples * 4 * rows, 2 * COLS), pick).astype(BF)
    patches = (
        split.reshape(samples, 2, rows, 2, 2, COLS)
        .transpose(0, 2, 1, 3, 4, 5)
        .reshape(samples, rows, 8, COLS)
    )
    levels = meso_in.reshape(samples, LEV, rows, COLS).transpose(0, 2, 1, 3)
    cot = wind_cot.transpose(0, 2, 1, 3)
    rest = jnp.zeros((samples, rows, PACK - LEV - 11, COLS), BF)
    return jnp.concatenate([levels, patches, cot, rest], axis=2)


def to_chip(v, by):
    return along(v, (CHIP, CHIP), by)


def local(
    terrain_in,
    meso_in,
    wind_cot,
    patch_weight,
    terrain_weight,
    lift_weight,
    meso_weight,
    merging_weight,
    decoder_weight,
    head_weight,
):
    own = packed(terrain_in, meso_in, wind_cot)
    place = jnp.stack([lax.axis_index(a) for a in ("segment", "space", "dp")]).astype(jnp.int32)
    eight, first, last = chip_rows(place, own, to_partner(own))
    above, below = to_chip(last, 1), to_chip(first, -1)
    small_ones = small_weights(lift_weight, patch_weight.T, head_weight)
    keep, send = main(
        place,
        above,
        eight,
        below,
        small_ones,
        meso_weight,
        terrain_weight,
        merging_weight,
        decoder_weight,
    )
    mine, theirs, written = summed_everywhere(place, keep, send)
    return finish(
        place, written, (*mine, *theirs), *small_ones[:2], meso_weight, terrain_weight
    )


def solution(mesh):
    placed = (
        P("dp", None, "space", None),
        P("dp", None, None, "space", None),
        P("dp", None, "space", None),
        P(),
        P(),
        P(),
        P(),
        P(),
        P(),
        P(),
    )
    return jax.shard_map(
        local,
        mesh=mesh,
        in_specs=placed,
        out_specs=(P(), P(), P(), P(), P(), P(), P()),
        check_vma=False,
    )
```
